512 devices in a mesh: row: 64 (over z, y_hi, core), col: 8 (over x, y_lo).
Axes of the slice: x: 4, y: 4 (y_hi: 2, y_lo: 2; y = y_hi * 2 + y_lo), z: 16, core: 2. Of those that a mesh axis runs over, the one named last changes fastest.
Arguments:
- positions: float32 [3, 131072], P(None, ('row', 'col')), as said below
- velocities: float32 [3, 131072], P(None, ('row', 'col')), may hold values from -6 to 6
- old_forces: float32 [3, 131072], P(None, ('row', 'col')), may hold values from -6 to 6
- charges: float32 [131072], P(('row', 'col')), may hold values from -3 to 3
- atom_types: int32 [131072], P(('row', 'col')), may hold values from 0 to 7
- type_table: float32 [7, 8], replicated, may hold values from 0.003 to 2, as said below
- tile_pairs: int32 [64, 8, 2, 32], P('row', 'col'), may hold values from -1 to 127, as said below
Outputs:
- new_positions: float32 [3, 131072], P(None, ('row', 'col'))
- new_velocities: float32 [3, 131072], P(None, ('row', 'col'))
- new_forces: float32 [3, 131072], P(None, ('row', 'col'))
The draws below stay inside these ranges and needn't reach their ends.
Inputs may be any that keep to these rules, and one draw needn't show every extreme that they name: `positions`: the atoms of one block lie together in a cube of its own; the blocks' cubes fill a cubic lattice in the order of the block numbers, at about 0.1 atoms per cubic angstrom. `tile_pairs`: on each device the first n slots hold distinct pairs (a, g) with a below 16 and g below 128, each a tile whose blocks' cubes lie within 12 angstrom of each other; the other slots hold -1 in both entries. n is at most 32, differs from device to device, and equals 32 on the device with the most such tiles when it has 32 or more; the list is a sampled part of each device's near tiles, not all of them. `type_table`: Rows: intrinsic radii 1 to 2, screening scales 0.15 to 0.6, neck weights 0.003 to 0.012, alpha 0.6 to 1, beta 0.3 to 0.9, gamma 0.2 to 0.6, masses 0.5 to 2.
All inputs are finite; a program needn't handle non-finite values.
Results may differ from the reference program's by a relative error of at most 0.0003.
Values sent between devices are 32-bit elements; how exact they have to be, the bound alone decides.
No kernel may reach another device: no remote copies, remote signals or barrier semaphores. Data moves between devices by JAX's collectives and lax.ppermute only.
A program may use at most 64 MiB of HBM per device.

```python
import math
import jax
import jax.numpy as jnp
from jax import lax

TILE = 128
BLK_DEV = 2
TILE_CAP = 32
TYPES = 8
ATOMS = 131072
I_BLOCKS = 16
N_ROW = 64
N_COL = 8


def block_frame():
    block_total = ATOMS // TILE
    lattice_side = int(math.ceil(block_total ** (1.0 / 3.0) - 1e-09))
    if lattice_side ** 3 < block_total:
        lattice_side = lattice_side + 1
    cube_edge = (TILE * 10.0) ** (1.0 / 3.0)
    block_ids = jnp.arange(block_total, dtype=jnp.int32)
    lattice = jnp.stack([block_ids // (lattice_side * lattice_side), block_ids // lattice_side % lattice_side, block_ids % lattice_side], axis=0)
    return (lattice.astype(jnp.float32) * cube_edge, cube_edge)


def draw_positions(key, part):
    corners, cube_edge = block_frame()
    unit = jax.random.uniform(jax.random.fold_in(key, 21), (3, ATOMS), jnp.float32)
    return (jnp.repeat(corners, TILE, axis=1) + cube_edge * unit).astype(jnp.float32)


def draw_type_table(key, part):
    lowest = jnp.array([1.0, 0.15, 0.003, 0.6, 0.3, 0.2, 0.5], jnp.float32)[:, None]
    highest = jnp.array([2.0, 0.6, 0.012, 1.0, 0.9, 0.6, 2.0], jnp.float32)[:, None]
    in_logs = jnp.array([1.0, 1.0, 1.0, 0.0, 0.0, 0.0, 1.0], jnp.float32)[:, None]
    unit = jax.random.uniform(jax.random.fold_in(key, 5), (7, TYPES), jnp.float32)
    linear = lowest + (highest - lowest) * unit
    logged = jnp.exp(jnp.log(lowest) + (jnp.log(highest) - jnp.log(lowest)) * unit)
    return (in_logs * logged + (1.0 - in_logs) * linear).astype(jnp.float32)


def draw_tile_pairs(key, part):
    devices_all = N_ROW * N_COL
    i_count = BLK_DEV * N_COL
    j_count = BLK_DEV * N_ROW
    combos = i_count * j_count
    corners, cube_edge = block_frame()
    row_ids = jnp.arange(N_ROW, dtype=jnp.int32)[:, None, None]
    col_ids = jnp.arange(N_COL, dtype=jnp.int32)[None, :, None]
    local_i = jnp.arange(i_count, dtype=jnp.int32)[None, None, :]
    local_j = jnp.arange(j_count, dtype=jnp.int32)[None, None, :]
    global_i = row_ids * i_count + local_i + 0 * col_ids
    global_j = (local_j // BLK_DEV * N_COL + col_ids) * BLK_DEV + local_j % BLK_DEV + 0 * row_ids
    corner_i = jnp.take(corners, global_i.reshape(-1), axis=1).reshape(3, N_ROW, N_COL, i_count)
    corner_j = jnp.take(corners, global_j.reshape(-1), axis=1).reshape(3, N_ROW, N_COL, j_count)
    apart = jnp.abs(corner_i[:, :, :, :, None] - corner_j[:, :, :, None, :])
    gap = jnp.maximum(apart - cube_edge - 0.001, 0.0)
    near = (jnp.sum(gap * gap, axis=0) < 144.0).reshape(devices_all, combos)
    key_list = jax.random.split(jax.random.fold_in(key, 11), devices_all)
    ranks = jax.vmap(lambda subkey: jax.random.permutation(subkey, combos))(key_list).astype(jnp.int32)
    score = jnp.where(near, ranks + 1, 0)
    chosen_score, chosen = lax_top(score)
    near_count = jnp.sum(near.astype(jnp.int32), axis=1)
    fewest = (TILE_CAP + 7) // 8
    level_count = 64
    skew_level = jax.random.randint(jax.random.fold_in(key, 12), (devices_all,), 0, level_count + 1)
    live_count = fewest + (TILE_CAP - fewest) * skew_level * skew_level * skew_level // (level_count * level_count * level_count)
    busiest = jnp.argmax(near_count)
    live_count = jnp.where(jnp.arange(devices_all) == busiest, TILE_CAP, live_count)
    live_count = jnp.minimum(live_count, near_count)
    slot_ids = jnp.arange(TILE_CAP)[None, :]
    live_slot = slot_ids < live_count[:, None]
    first_ids = jnp.where(live_slot, chosen // j_count, -1)
    second_ids = jnp.where(live_slot, chosen % j_count, -1)
    stacked = jnp.stack([first_ids, second_ids], axis=1)
    return stacked.reshape(N_ROW, N_COL, 2, TILE_CAP).astype(jnp.int32)


def lax_top(score):
    return jax.lax.top_k(score, TILE_CAP)


def plant(result, key, smallest, top_value):
    spot = [jax.random.randint(jax.random.fold_in(key, axis), (), 0, length) for axis, length in enumerate(result.shape)]
    longest = result.shape.index(max(result.shape))
    beside = spot[:longest] + [(spot[longest] + 1) % result.shape[longest]] + spot[longest + 1:]
    return result.at[tuple(spot)].set(smallest).at[tuple(beside)].set(top_value)


def levels(key, dims, cuts, least, largest):
    level = 1.0
    for position, blocks in cuts:
        steps = jax.random.uniform(jax.random.fold_in(jax.random.fold_in(key, 6), position), (blocks,), jnp.float32, least / len(cuts), largest / len(cuts))
        level = level * jnp.repeat(jnp.exp(steps), dims[position] // blocks).reshape((-1,) + (1,) * (len(dims) - 1 - position))
    return level


def scatter_about(key, dims, spread, bound, cuts=(), held_as=jnp.bfloat16):
    result = jax.random.normal(key, dims, jnp.float32) * spread
    if len(cuts) > 0:
        result = levels(key, dims, cuts, -0.22, 0.18) * result
    return jnp.clip(result, min=-bound, max=bound).astype(held_as)


def setup_inputs(seed: int = 0) -> dict:
    keys = jax.random.split(jax.random.key(seed), 8)
    return {
        "positions": draw_positions(jax.random.fold_in(keys[7], 71), 0),
        "velocities": scatter_about(keys[1], (3, ATOMS), 1.0, 6.0, ((1, 512),), jnp.float32),
        "old_forces": scatter_about(keys[2], (3, ATOMS), 1.0, 6.0, ((1, 512),), jnp.float32),
        "charges": scatter_about(keys[3], (ATOMS,), 0.5, 3.0, ((0, 512),), jnp.float32),
        "atom_types": plant(jax.random.randint(keys[4], (ATOMS,), 0, TYPES), jax.random.fold_in(keys[4], 1), 0, TYPES - 1).astype(jnp.int32),
        "type_table": draw_type_table(jax.random.fold_in(keys[7], 71), 0),
        "tile_pairs": draw_tile_pairs(jax.random.fold_in(keys[7], 71), 0),
    }


CUTOFF = 12.0
COULOMB = 32.0
TIMESTEP = 0.5
OFFSET = 0.09
NECK_GAP = 0.5
NECK_WIDTH = 16.0

def taper(dist_sq):
    taper_base = jnp.maximum(1.0 - dist_sq / (CUTOFF * CUTOFF), 0.0)
    return (taper_base * taper_base, -2.0 * taper_base / (CUTOFF * CUTOFF))

def screening(dist_sq, intrinsic, other_radius, other_scale, other_neck):
    soft_sq = dist_sq + intrinsic * intrinsic
    neck_gap = intrinsic + other_radius + NECK_GAP
    neck_off = dist_sq - neck_gap * neck_gap
    neck_bump = jnp.exp(-neck_off * neck_off / NECK_WIDTH)
    volume = other_scale * other_radius * other_radius * other_radius
    descreen = volume / (soft_sq * soft_sq) + other_neck * neck_bump
    slope = -2.0 * volume / (soft_sq * soft_sq * soft_sq) - other_neck * neck_bump * neck_off * (2.0 / NECK_WIDTH)
    weight, w_slope = taper(dist_sq)
    return (weight * descreen, w_slope * descreen + weight * slope)

def separation(coords_i, coords_j):
    offset_vec = coords_i[:, :, :, None] - coords_j[:, :, None, :]
    return (offset_vec, lax.optimization_barrier(jnp.sum(offset_vec * offset_vec, axis=1)))

def born_terms(side_i, side_j, mask):
    offset_vec, dist_sq = separation(side_i[:, 0:3], side_j[:, 0:3])
    value, slope = screening(dist_sq, side_i[:, 4][:, :, None], side_j[:, 4][:, None, :], side_j[:, 5][:, None, :], side_j[:, 6][:, None, :])
    return lax.optimization_barrier(jnp.sum(mask * value, axis=2))[:, None, :]

def pair_terms(side_i, side_j, mask):
    offset_vec, dist_sq = separation(side_i[:, 0:3], side_j[:, 0:3])
    charge_pair = side_i[:, 3][:, :, None] * side_j[:, 3][:, None, :]
    radius_j = side_j[:, -1][:, None, :]
    radii_prod = side_i[:, -1][:, :, None] * radius_j
    radii_exp = jnp.exp(-dist_sq / (4.0 * radii_prod))
    inv_eff = 1.0 / jnp.sqrt(dist_sq + radii_prod * radii_exp)
    inv_cube = inv_eff * inv_eff * inv_eff
    weight, w_slope = taper(dist_sq)
    d_dist = mask * charge_pair * (w_slope * inv_eff - 0.5 * weight * (1.0 - 0.25 * radii_exp) * inv_cube)
    d_radius = mask * -0.5 * weight * charge_pair * inv_cube * radii_exp * (1.0 + dist_sq / (4.0 * radii_prod)) * radius_j
    direct = 2.0 * COULOMB * lax.optimization_barrier(jnp.sum(d_dist[:, None] * offset_vec, axis=3))
    return jnp.concatenate([direct, lax.optimization_barrier(jnp.sum(d_radius, axis=2))[:, None, :]], axis=1)

def chain_terms(side_i, side_j, mask):
    offset_vec, dist_sq = separation(side_i[:, 0:3], side_j[:, 0:3])
    value_ij, slope_ij = screening(dist_sq, side_i[:, 4][:, :, None], side_j[:, 4][:, None, :], side_j[:, 5][:, None, :], side_j[:, 6][:, None, :])
    value_ji, slope_ji = screening(dist_sq, side_j[:, 4][:, None, :], side_i[:, 4][:, :, None], side_i[:, 5][:, :, None], side_i[:, 6][:, :, None])
    factor = mask * (side_i[:, -1][:, :, None] * slope_ij + side_j[:, -1][:, None, :] * slope_ji)
    return -2.0 * lax.optimization_barrier(jnp.sum(factor[:, None] * offset_vec, axis=3))

def radius_terms(born_sum, intrinsic, coef_alpha, coef_beta, coef_gamma):
    scaled = intrinsic * born_sum
    poly_arg = coef_alpha * scaled - coef_beta * scaled * scaled + coef_gamma * scaled * scaled * scaled
    squash = jnp.tanh(poly_arg)
    radius = 1.0 / (1.0 / intrinsic - squash / (intrinsic + OFFSET))
    poly_slope = coef_alpha - 2.0 * coef_beta * scaled + 3.0 * coef_gamma * scaled * scaled
    radius_rate = radius * radius * (1.0 - squash * squash) * poly_slope * intrinsic / (intrinsic + OFFSET)
    return (radius, radius_rate)

def reference(positions, velocities, old_forces, charges, atom_types, type_table, tile_pairs):
    type_ids = jnp.arange(TYPES, dtype=jnp.int32)
    onehot = (atom_types[None, :] == type_ids[:, None]).astype(jnp.float32)
    params = lax.optimization_barrier(jnp.sum(type_table[:, :, None] * onehot[None, :, :], axis=1))
    atom_mass = params[6]
    new_positions = positions + TIMESTEP * velocities + TIMESTEP * TIMESTEP / (2.0 * atom_mass) * old_forces
    attrs = jnp.concatenate([new_positions, charges[None, :], params[0:6]], axis=0)
    block_count = ATOMS // TILE
    row_ids = jnp.arange(N_ROW, dtype=jnp.int32)[:, None, None]
    col_ids = jnp.arange(N_COL, dtype=jnp.int32)[None, :, None]
    live_slot = tile_pairs[:, :, 0, :] >= 0
    tiles_i = jnp.maximum(tile_pairs[:, :, 0, :], 0)
    tiles_j = jnp.maximum(tile_pairs[:, :, 1, :], 0)
    block_i = (row_ids * I_BLOCKS + tiles_i).astype(jnp.int32).reshape(-1, TILE_CAP)
    block_j = ((tiles_j // BLK_DEV * N_COL + col_ids) * BLK_DEV + tiles_j % BLK_DEV).astype(jnp.int32).reshape(-1, TILE_CAP)
    live_f = live_slot.astype(jnp.float32).reshape(-1, TILE_CAP)
    diagonal = jnp.eye(TILE, dtype=jnp.float32)

    def all_tiles(func, rows, packed):
        blocks = packed.reshape(packed.shape[0], block_count, TILE)

        def per_device(item):
            list_i, list_j, live_row = item
            side_i = jnp.moveaxis(jnp.take(blocks, list_i, axis=1), 1, 0)
            side_j = jnp.moveaxis(jnp.take(blocks, list_j, axis=1), 1, 0)
            self_pair = (list_i == list_j).astype(jnp.float32)
            mask = live_row[:, None, None] * (1.0 - self_pair[:, None, None] * diagonal)
            return func(side_i, side_j, mask)
        partial_sums = lax.map(per_device, (block_i, block_j, live_f))
        summed = jnp.zeros((block_count, rows, TILE), jnp.float32).at[block_i.reshape(-1)].add(partial_sums.reshape(-1, rows, TILE))
        return jnp.moveaxis(summed, 1, 0).reshape(rows, ATOMS)
    born_part = all_tiles(born_terms, 1, attrs)[0]
    radius, radius_rate = radius_terms(born_part, params[0], params[3], params[4], params[5])
    pair_part = all_tiles(pair_terms, 4, jnp.concatenate([attrs, radius[None, :]], axis=0))
    chain = (COULOMB * charges * charges / (2.0 * radius * radius) - COULOMB * pair_part[3]) * radius_rate
    chain_part = all_tiles(chain_terms, 3, jnp.concatenate([attrs, chain[None, :]], axis=0))
    new_forces = pair_part[0:3] + chain_part
    new_velocities = velocities + TIMESTEP / (2.0 * atom_mass) * (old_forces + new_forces)
    return (new_positions, new_velocities, new_forces)
```

```python
import jax
import jax.numpy as jnp
from jax import lax
from jax.experimental import pallas as pl
from jax.experimental.pallas import tpu as pltpu
from jax.sharding import Mesh
from jax.sharding import PartitionSpec as P

TILE = 128
SLOTS = 32
CHUNK = 32

CUTOFF = 12.0
COULOMB = 32.0
TIMESTEP = 0.5
OFFSET = 0.09
NECK_GAP = 0.5
NECK_WIDTH = 16.0
INV_SQ = 1.0 / (CUTOFF * CUTOFF)

AXES = ("zh", "zl", "yh", "core", "x", "yl")
SIZES = (4, 4, 2, 2, 4, 2)
REP = ("zh",)
ROWS = ("zl", "yh", "core")
COLS = ("x", "yl")
N_REP, N_ROWS, N_COLS = 4, 16, 8
HELD = 2 * N_REP
I_BLOCKS = N_COLS * HELD
J_BLOCKS = N_ROWS * HELD
OWN_I = 2 * N_COLS

VMEM = pl.BlockSpec(memory_space=pltpu.VMEM)
SMEM = pl.BlockSpec(memory_space=pltpu.SMEM)


def given_to_all(shard, axes, count):
    copies = jnp.broadcast_to(shard, (count, *shard.shape))
    return lax.all_to_all(copies, axes, 0, 0, tiled=True)


def radius_terms(born_sum, intrinsic, coef_alpha, coef_beta, coef_gamma):
    scaled = intrinsic * born_sum
    poly_arg = (
        coef_alpha * scaled - coef_beta * scaled * scaled + coef_gamma * scaled * scaled * scaled
    )
    squash = jnp.tanh(poly_arg)
    radius = 1.0 / (1.0 / intrinsic - squash / (intrinsic + OFFSET))
    poly_slope = coef_alpha - 2.0 * coef_beta * scaled + 3.0 * coef_gamma * scaled * scaled
    radius_rate = (
        radius * radius * (1.0 - squash * squash) * poly_slope * intrinsic / (intrinsic + OFFSET)
    )
    return (radius, radius_rate)


def looked_up(table, types, row):
    found = jnp.zeros(types.shape, jnp.float32)
    for kind in range(table.shape[1]):
        found = jnp.where(types == float(kind), table[row, kind], found)
    return found


def folded(value):
    parts = [value[s : s + 8] for s in range(0, CHUNK, 8)]
    while len(parts) > 1:
        parts = [a + b for a, b in zip(parts[::2], parts[1::2])]
    return parts[0]


def write_mask(mask_ref):
    down = lax.broadcasted_iota(jnp.int32, (TILE, TILE), 0)
    across = lax.broadcasted_iota(jnp.int32, (TILE, TILE), 1)
    mask_ref[0] = jnp.ones((TILE, TILE), jnp.float32)
    mask_ref[1] = jnp.where(down == across, 0.0, 1.0)


def column(side_j, s, k):
    return side_j[s : s + CHUNK, k : k + 1]


def offsets(xi, yi, zi, side_j, s):
    dx = xi - column(side_j, s, 0)
    dy = yi - column(side_j, s, 1)
    dz = zi - column(side_j, s, 2)
    return dx, dy, dz, dx * dx + dy * dy + dz * dz


def born_kernel(meta, pack_i, pack_j, out_ref, acc, mask_ref):
    acc[...] = jnp.zeros_like(acc)
    write_mask(mask_ref)

    def one_list(z, _):
        def one_tile(k, _):
            ia, jb, same = meta[z, k], meta[z, SLOTS + k], meta[z, 2 * SLOTS + k]
            side_j = pack_j[jb].T
            xi, yi, zi, rho = (pack_i[ia, c : c + 1, :] for c in range(4))
            rho_sq, rho_gap = rho * rho, rho + NECK_GAP
            total = jnp.zeros((8, TILE), jnp.float32)
            for s in range(0, TILE, CHUNK):
                _, _, _, q = offsets(xi, yi, zi, side_j, s)
                base = jnp.maximum(1.0 - q * INV_SQ, 0.0)
                weight = base * base * mask_ref[same, s : s + CHUNK, :]
                soft = q + rho_sq
                gap = rho_gap + column(side_j, s, 3)
                off = q - gap * gap
                bump = jnp.exp(off * off * (-1.0 / NECK_WIDTH))
                value = column(side_j, s, 4) / (soft * soft) + column(side_j, s, 5) * bump
                total += folded(weight * value)
            acc[ia] += total
            return 0

        return lax.fori_loop(0, meta[z, 3 * SLOTS], one_tile, 0)

    lax.fori_loop(0, N_REP, one_list, 0)
    out_ref[...] = jnp.sum(acc[...], axis=1)


def pair_kernel(meta, pack_i, pack_j, rad_i, rad_j, grad_ref, direct_ref, acc, force, mask_ref):
    acc[...] = jnp.zeros_like(acc)
    force[...] = jnp.zeros_like(force)
    write_mask(mask_ref)
    own = meta[0, 3 * SLOTS + 1]

    def sweep(z, with_force):
        def one_tile(k, _):
            ia, jb, same = meta[z, k], meta[z, SLOTS + k], meta[z, 2 * SLOTS + k]
            radius_j = rad_j[0, pl.ds(jb, 1), :]
            charge_j = rad_j[1, pl.ds(jb, 1), :]
            side_j = jnp.concatenate(
                [
                    pack_j[jb, 0:3, :],
                    radius_j,
                    1.0 / radius_j,
                    charge_j,
                    charge_j * radius_j,
                    charge_j,
                ],
                axis=0,
            ).T
            xi, yi, zi = (pack_i[ia, c : c + 1, :] for c in range(3))
            radius_i = rad_i[pl.ds(ia, 1), :]
            quarter_i = 0.25 / radius_i
            total = jnp.zeros((8, TILE), jnp.float32)
            sums = [jnp.zeros((8, TILE), jnp.float32)] * 3
            for s in range(0, TILE, CHUNK):
                dx, dy, dz, q = offsets(xi, yi, zi, side_j, s)
                base = jnp.maximum(1.0 - q * INV_SQ, 0.0)
                weight = base * base * mask_ref[same, s : s + CHUNK, :]
                arg = q * (quarter_i * column(side_j, s, 4))
                decay = jnp.exp(-arg)
                inv = lax.rsqrt(q + radius_i * column(side_j, s, 3) * decay)
                weighted = weight * (inv * inv * inv)
                total += folded(weighted * (decay * (1.0 + arg) * column(side_j, s, 6)))
                if with_force:
                    slope = (-2.0 * INV_SQ) * base * inv - weighted * (0.5 - 0.125 * decay)
                    slope = slope * column(side_j, s, 5)
                    sums = [a + folded(slope * d) for a, d in zip(sums, (dx, dy, dz))]
            acc[ia] += total
            if with_force:
                at = ia // HELD * 2 + ia % 2
                for c in range(3):
                    force[at, c] += sums[c]
            return 0

        lax.fori_loop(0, meta[z, 3 * SLOTS], one_tile, 0)

    def one_list(z, _):
        @pl.when(z == own)
        def _():
            sweep(z, True)

        @pl.when(z != own)
        def _():
            sweep(z, False)

        return 0

    lax.fori_loop(0, N_REP, one_list, 0)
    grad_ref[...] = jnp.sum(acc[...], axis=1)
    direct_ref[...] = jnp.sum(force[...], axis=2)


def chain_kernel(meta, pack_i, pack_j, chain_j, out_ref, force, mask_ref):
    force[...] = jnp.zeros_like(force)
    own = meta[0, 3 * SLOTS + 1]

    def one_tile(k, _):
        ia, jb = meta[own, k], meta[own, SLOTS + k]
        rho_row = pack_j[jb, 3:4, :]
        side_j = jnp.concatenate(
            [pack_j[jb, 0:6, :], chain_j[pl.ds(jb, 1), :], rho_row * rho_row], axis=0
        ).T
        xi, yi, zi, rho, vol, neck = (pack_i[ia, c : c + 1, :] for c in range(6))
        rho_sq, rho_gap = rho * rho, rho + NECK_GAP
        sums = [jnp.zeros((8, TILE), jnp.float32)] * 6
        for s in range(0, TILE, CHUNK):
            dx, dy, dz, q = offsets(xi, yi, zi, side_j, s)
            base = jnp.maximum(1.0 - q * INV_SQ, 0.0)
            weight = base * base
            w_slope = (-2.0 * INV_SQ) * base
            gap = rho_gap + column(side_j, s, 3)
            off = q - gap * gap
            bump = jnp.exp(off * off * (-1.0 / NECK_WIDTH))
            bump_part = bump * (w_slope - weight * off * (2.0 / NECK_WIDTH))
            inv_i = 1.0 / (q + rho_sq)
            inv_j = 1.0 / (q + column(side_j, s, 7))
            slope_ij = column(side_j, s, 4) * (inv_i * inv_i) * (
                w_slope - 2.0 * weight * inv_i
            ) + column(side_j, s, 5) * bump_part
            slope_ji = vol * (inv_j * inv_j) * (w_slope - 2.0 * weight * inv_j) + neck * bump_part
            slope_ji = slope_ji * column(side_j, s, 6)
            parts = [slope_ji * d for d in (dx, dy, dz)] + [slope_ij * d for d in (dx, dy, dz)]
            sums = [a + folded(v) for a, v in zip(sums, parts)]
        at = ia // HELD * 2 + ia % 2
        for c in range(6):
            force[at, c] += sums[c]
        return 0

    lax.fori_loop(0, meta[own, 3 * SLOTS], one_tile, 0)
    out_ref[...] = jnp.sum(force[...], axis=2)


def called(kernel, shapes, scratch, *args):
    return pl.pallas_call(
        kernel,
        out_shape=[jax.ShapeDtypeStruct(s, jnp.float32) for s in shapes],
        in_specs=[SMEM] + [VMEM] * (len(args) - 1),
        out_specs=[VMEM] * len(shapes),
        scratch_shapes=[pltpu.VMEM(s, jnp.float32) for s in scratch]
        + [pltpu.VMEM((2, TILE, TILE), jnp.float32)],
        compiler_params=pltpu.CompilerParams(vmem_limit_bytes=32 * 1024 * 1024),
    )(*args)


def packed(blocks, table):
    types = blocks[:, 3:4, :]
    rho = looked_up(table, types, 0)
    scale = looked_up(table, types, 1)
    neck = looked_up(table, types, 2)
    fill = jnp.zeros(types.shape, jnp.float32)
    return jnp.concatenate(
        [blocks[:, 0:3, :], rho, scale * rho * rho * rho, neck, types, fill], axis=1
    )


def body(positions, velocities, old_forces, charges, atom_types, table, tile_pairs):
    rep_at = lax.axis_index(REP)
    row_at = lax.axis_index(ROWS)
    col_at = lax.axis_index(COLS)
    kinds = atom_types.astype(jnp.float32)
    atom_mass = looked_up(table, kinds, 6)
    new_positions = (
        positions + TIMESTEP * velocities + TIMESTEP * TIMESTEP / (2.0 * atom_mass) * old_forces
    )

    atoms = jnp.concatenate([new_positions, kinds[None, :]], axis=0)
    atoms = jnp.moveaxis(atoms.reshape(4, 2, TILE), 1, 0)
    listed = jnp.pad(tile_pairs.reshape(1, 2 * SLOTS).astype(jnp.float32), ((0, 1), (0, 64)))
    extra = jnp.concatenate([listed, charges.reshape(2, TILE)], axis=0)
    sent = jnp.concatenate([atoms, extra[None]], axis=0)
    held = given_to_all(sent, REP, N_REP)
    held_atoms = held[:, 0:2].reshape(HELD, 4, TILE)
    held_charges = held[:, 2, 2:4].reshape(HELD, TILE)
    lists = held[:, 2, 0, 0 : 2 * SLOTS].astype(jnp.int32)

    list_a, list_g = lists[:, :SLOTS], lists[:, SLOTS:]
    reps = jnp.arange(N_REP, dtype=jnp.int32)[:, None]
    live = jnp.sum((list_a >= 0).astype(jnp.int32), axis=1, keepdims=True)
    block_a, block_g = jnp.maximum(list_a, 0), jnp.maximum(list_g, 0)
    j_row = block_g // 2
    place_i = (block_a // 2 * N_REP + reps) * 2 + block_a % 2
    place_j = (j_row % N_ROWS * N_REP + j_row // N_ROWS) * 2 + block_g % 2
    same = (j_row == reps * N_ROWS + row_at) & (block_a == col_at * 2 + block_g % 2)
    tail = jnp.broadcast_to(rep_at, (N_REP, 1)).astype(jnp.int32)
    meta = jnp.concatenate([place_i, place_j, same.astype(jnp.int32), live, tail], axis=1)

    side_i = given_to_all(held_atoms, COLS, N_COLS).reshape(I_BLOCKS, 4, TILE)
    side_j = given_to_all(held_atoms, ROWS, N_ROWS).reshape(J_BLOCKS, 4, TILE)
    pack_i, pack_j = packed(side_i, table), packed(side_j, table)

    [born_part] = called(
        born_kernel, [(I_BLOCKS, TILE)], [(I_BLOCKS, 8, TILE)], meta, pack_i, pack_j
    )
    both = given_to_all(jnp.concatenate([born_part, held_charges]), COLS, N_COLS)
    born_all = jnp.sum(both[:, :I_BLOCKS], axis=0)
    charge_i = both[:, I_BLOCKS:].reshape(I_BLOCKS, TILE)
    types_i = pack_i[:, 6]
    radius_i, rate_i = radius_terms(
        born_all, pack_i[:, 3], *(looked_up(table, types_i, r) for r in (3, 4, 5))
    )
    radius_held = lax.dynamic_slice_in_dim(radius_i, col_at * HELD, HELD)
    rate_held = lax.dynamic_slice_in_dim(rate_i, col_at * HELD, HELD)
    rad_j = given_to_all(jnp.stack([radius_held, held_charges]), ROWS, N_ROWS)
    rad_j = jnp.moveaxis(rad_j, 1, 0).reshape(2, J_BLOCKS, TILE)

    grad_part, direct_part = called(
        pair_kernel,
        [(I_BLOCKS, TILE), (OWN_I, 3, TILE)],
        [(I_BLOCKS, 8, TILE), (OWN_I, 3, 8, TILE)],
        meta,
        pack_i,
        pack_j,
        radius_i,
        rad_j,
    )
    grads = lax.all_to_all(
        grad_part.reshape(N_COLS, HELD, TILE), COLS, 0, 0, tiled=True
    )
    grad_held = -0.5 * held_charges * jnp.sum(grads, axis=0)
    chain_held = (
        COULOMB * held_charges * held_charges / (2.0 * radius_held * radius_held)
        - COULOMB * grad_held
    ) * rate_held
    chain_j = given_to_all(chain_held, ROWS, N_ROWS).reshape(J_BLOCKS, TILE)

    [chain_part] = called(
        chain_kernel, [(OWN_I, 6, TILE)], [(OWN_I, 6, 8, TILE)], meta, pack_i, pack_j, chain_j
    )
    shared = jnp.concatenate([direct_part, chain_part], axis=1).reshape(N_COLS, 2, 9, TILE)
    sums = jnp.sum(lax.all_to_all(shared, COLS, 0, 0, tiled=True), axis=0)
    sums = jnp.moveaxis(sums, 0, 1).reshape(3, 3, 2 * TILE)
    chain_own = lax.dynamic_slice_in_dim(chain_held, rep_at * 2, 2).reshape(1, 2 * TILE)
    new_forces = (2.0 * COULOMB) * charges * sums[0] - 2.0 * (sums[1] + chain_own * sums[2])
    new_velocities = velocities + TIMESTEP / (2.0 * atom_mass) * (old_forces + new_forces)
    return (new_positions, new_velocities, new_forces)


def solution(mesh):
    split = Mesh(mesh.devices.reshape(SIZES), AXES)
    rows, cols = AXES[:4], AXES[4:]
    return jax.shard_map(
        body,
        mesh=split,
        in_specs=(
            P(None, AXES),
            P(None, AXES),
            P(None, AXES),
            P(AXES),
            P(AXES),
            P(),
            P(rows, cols, None, None),
        ),
        out_specs=(P(None, AXES), P(None, AXES), P(None, AXES)),
        check_vma=False,
    )
```

```python
import jax
import jax.numpy as jnp
from jax import lax
from jax.experimental import pallas as pl
from jax.experimental.pallas import tpu as pltpu
from jax.sharding import Mesh
from jax.sharding import PartitionSpec as P

TILE = 128
SLOTS = 32
CHUNK = 32
UNROLL = 4
LISTED = 128

CUTOFF = 12.0
COULOMB = 32.0
TIMESTEP = 0.5
OFFSET = 0.09
NECK_GAP = 0.5
NECK_WIDTH = 16.0
INV_SQ = 1.0 / (CUTOFF * CUTOFF)
LOG2E = 1.4426950408889634

AXES = ("zh", "zl", "yh", "core", "x", "yl")
SIZES = (4, 4, 2, 2, 4, 2)
REP = ("zh",)
ROWS = ("zl", "yh", "core")
COLS = ("x", "yl")
N_REP, N_ROWS, N_COLS = 4, 16, 8
HELD = 2 * N_REP
I_BLOCKS = N_COLS * HELD
J_BLOCKS = N_ROWS * HELD
OWN_I = 2 * N_COLS

VMEM = pl.BlockSpec(memory_space=pltpu.VMEM)
SMEM = pl.BlockSpec(memory_space=pltpu.SMEM)
F32 = jnp.float32


def given_to_all(shard, axes, count):
    copies = jnp.broadcast_to(shard, (count, *shard.shape))
    return lax.all_to_all(copies, axes, 0, 0, tiled=True)


def exchanged(pieces, axes):
    return lax.all_to_all(pieces, axes, 0, 0, tiled=True)


def called(kernel, outs, scratch, smem, vmem):
    return pl.pallas_call(
        kernel,
        out_shape=[jax.ShapeDtypeStruct(s, F32) for s in outs],
        in_specs=[SMEM] * len(smem) + [VMEM] * len(vmem),
        out_specs=[VMEM] * len(outs),
        scratch_shapes=[pltpu.VMEM(s, t) for s, t in scratch],
        compiler_params=pltpu.CompilerParams(vmem_limit_bytes=32 * 1024 * 1024),
    )(*smem, *vmem)


def looked_up(table, types, rows):
    found = [jnp.zeros(types.shape, F32) for _ in rows]
    for kind in range(8):
        here = types == float(kind)
        found = [jnp.where(here, table[r, kind], f) for r, f in zip(rows, found)]
    return found


def folded(value):
    parts = [value[s : s + 8] for s in range(0, CHUNK, 8)]
    while len(parts) > 1:
        parts = [a + b for a, b in zip(parts[::2], parts[1::2])]
    return parts[0]


def write_mask(mask_ref):
    down = lax.broadcasted_iota(jnp.int32, (TILE, TILE), 0)
    across = lax.broadcasted_iota(jnp.int32, (TILE, TILE), 1)
    mask_ref[0] = jnp.ones((TILE, TILE), F32)
    mask_ref[1] = jnp.where(down == across, 0.0, 1.0)


def write_spread(spread_ref):
    row = lax.broadcasted_iota(jnp.int32, spread_ref.shape, 0)
    lane = lax.broadcasted_iota(jnp.int32, spread_ref.shape, 1)
    hit = (row % 8 == lane // TILE) & (row < 24)
    spread_ref[...] = jnp.where(hit, 1.0, 0.0).astype(jnp.bfloat16)


def columns(rows, spread_ref, count):
    high = rows.astype(jnp.bfloat16).astype(F32)
    rest = rows - high
    middle = rest.astype(jnp.bfloat16).astype(F32)
    parts = jnp.concatenate([high, middle, rest - middle, jnp.zeros_like(rows)], axis=0)
    spread = lax.dot_general(
        parts.astype(jnp.bfloat16),
        spread_ref[...],
        (((0,), (0,)), ((), ())),
        preferred_element_type=F32,
    )
    return lambda s, c: spread[s : s + CHUNK, c * TILE : (c + 1) * TILE]


def offsets(xi, yi, zi, col, s):
    dx = xi - col(s, 0)
    dy = yi - col(s, 1)
    dz = zi - col(s, 2)
    return dx, dy, dz, dx * dx + dy * dy + dz * dz


def decoded(code):
    return code >> 8, (code >> 1) & 127, code & 1


def for_each_tile(meta, first, count, one_tile):
    def step(k, _):
        for add in [
            one_tile(*decoded(meta[first + k * UNROLL + u])) for u in range(UNROLL)
        ]:
            add()
        return 0

    lax.fori_loop(0, (count + UNROLL - 1) // UNROLL, step, 0)


def first_kernel(table, pos, vel, old, charge, kinds, pairs, new_ref, sent_ref, scale_ref):
    types = kinds[...].astype(F32)
    [mass] = looked_up(table, types, (6,))
    new = pos[...] + TIMESTEP * vel[...] + TIMESTEP * TIMESTEP / (2.0 * mass) * old[...]
    new_ref[...] = new
    scale_ref[...] = TIMESTEP / (2.0 * mass)
    lists = pairs[...].astype(F32)
    lists = jnp.concatenate([lists, jnp.zeros((2, TILE - SLOTS), F32)], axis=1)
    for n in range(N_REP):
        for b in range(2):
            here = slice(b * TILE, (b + 1) * TILE)
            sent_ref[n, b, 0:3, :] = new[:, here]
            sent_ref[n, b, 3:4, :] = types[:, here]
            sent_ref[n, 2, 2 + b : 3 + b, :] = charge[:, here]
        sent_ref[n, 2, 0:2, :] = lists


def born_kernel(
    meta, table, side_i, side_j, out_ref, pack_i, pack_j, acc, mask_ref, spread_ref
):
    acc[...] = jnp.zeros_like(acc)
    write_mask(mask_ref)
    write_spread(spread_ref)
    for side, pack, blocks in ((side_i, pack_i, I_BLOCKS), (side_j, pack_j, J_BLOCKS)):
        types = side[:, 3, :]
        rho, scale, neck = looked_up(table, types, (0, 1, 2))
        pack[0:blocks, 0:3, :] = side[:, 0:3, :]
        pack[0:blocks, 3, :] = rho
        pack[0:blocks, 4, :] = scale * rho * rho * rho
        pack[0:blocks, 5, :] = neck
        pack[0:blocks, 6, :] = types
        pack[0:blocks, 7, :] = types
    pack_i[I_BLOCKS] = jnp.ones((8, TILE), F32)

    def one_tile(ia, jb, same):
        col = columns(pack_j[jb], spread_ref, 6)
        xi, yi, zi, rho = (pack_i[ia, c : c + 1, :] for c in range(4))
        rho_sq, rho_gap = rho * rho, rho + NECK_GAP
        total = jnp.zeros((8, TILE), F32)
        for s in range(0, TILE, CHUNK):
            _, _, _, q = offsets(xi, yi, zi, col, s)
            base = jnp.maximum(1.0 - q * INV_SQ, 0.0)
            weight = base * base * mask_ref[same, s : s + CHUNK, :]
            inv = 1.0 / (q + rho_sq)
            gap = rho_gap + col(s, 3)
            off = q - gap * gap
            bump = jnp.exp2(off * off * (-LOG2E / NECK_WIDTH))
            total += folded(weight * (col(s, 4) * (inv * inv) + col(s, 5) * bump))

        def add():
            acc[ia] += total

        return add

    for_each_tile(meta, 0, meta[LISTED], one_tile)
    for_each_tile(meta, SLOTS, meta[LISTED + 1], one_tile)
    born = jnp.sum(acc[0:I_BLOCKS], axis=1)
    for n in range(N_COLS):
        out_ref[n] = born


def radius_kernel(meta, table, parts, pack_i, charge, radius_ref, sent_ref, rate_ref):
    col_at = meta[LISTED + 3]
    born = parts[0]
    for n in range(1, N_COLS):
        born = born + parts[n]
    rho = pack_i[0:I_BLOCKS, 3, :]
    alpha, beta, gamma = looked_up(table, pack_i[0:I_BLOCKS, 6, :], (3, 4, 5))
    scaled = rho * born
    poly = alpha * scaled - beta * scaled * scaled + gamma * scaled * scaled * scaled
    squash = jnp.tanh(poly)
    radius = 1.0 / (1.0 / rho - squash / (rho + OFFSET))
    slope = alpha - 2.0 * beta * scaled + 3.0 * gamma * scaled * scaled
    rate_ref[...] = radius * radius * (1.0 - squash * squash) * slope * rho / (rho + OFFSET)
    radius_ref[0:I_BLOCKS] = radius
    radius_ref[I_BLOCKS : I_BLOCKS + 8] = jnp.ones((8, TILE), F32)
    held = radius_ref[pl.ds(pl.multiple_of(col_at * HELD, HELD), HELD), :]
    for n in range(N_ROWS):
        sent_ref[n, 0] = held
        sent_ref[n, 1] = charge[...]


def pair_kernel(
    meta, pack_i, pack_j, rad_i, rad_j, grad_ref, direct_ref, acc, force, mask_ref, spread_ref, sides
):
    acc[...] = jnp.zeros_like(acc)
    force[...] = jnp.zeros_like(force)
    write_mask(mask_ref)
    write_spread(spread_ref)
    sides[...] = pack_j[...]
    for n in range(N_ROWS):
        here = slice(n * HELD, (n + 1) * HELD)
        sides[here, 3, :] = rad_j[n, 0]
        sides[here, 4, :] = 1.0 / rad_j[n, 0]
        sides[here, 5, :] = rad_j[n, 1]

    def one_tile(ia, jb, same, with_force):
        col = columns(sides[jb], spread_ref, 6)
        xi, yi, zi = (pack_i[ia, c : c + 1, :] for c in range(3))
        radius_i = rad_i[pl.ds(ia, 1), :]
        quarter_i = 0.25 / radius_i
        total = jnp.zeros((8, TILE), F32)
        sums = [jnp.zeros((8, TILE), F32)] * 3
        for s in range(0, TILE, CHUNK):
            dx, dy, dz, q = offsets(xi, yi, zi, col, s)
            base = jnp.maximum(1.0 - q * INV_SQ, 0.0)
            weight = base * base * mask_ref[same, s : s + CHUNK, :]
            arg = q * (quarter_i * col(s, 4))
            decay = jnp.exp2(arg * -LOG2E)
            inv = lax.rsqrt(q + radius_i * col(s, 3) * decay)
            weighted = weight * col(s, 5) * (inv * inv * inv)
            total += folded(weighted * col(s, 3) * (decay * (1.0 + arg)))
            if with_force:
                slope = (-2.0 * INV_SQ) * base * col(s, 5) * inv - weighted * (
                    0.5 - 0.125 * decay
                )
                sums = [a + folded(slope * d) for a, d in zip(sums, (dx, dy, dz))]

        def add():
            acc[ia] += total
            if with_force:
                at = ia // HELD * 2 + ia % 2
                for c in range(3):
                    force[at, c] += sums[c]

        return add

    for_each_tile(meta, 0, meta[LISTED], lambda *a: one_tile(*a, True))
    for_each_tile(meta, SLOTS, meta[LISTED + 1], lambda *a: one_tile(*a, False))
    grad_ref[...] = jnp.sum(acc[0:I_BLOCKS], axis=1)
    direct_ref[...] = jnp.sum(force[0:OWN_I], axis=2)


def factor_kernel(meta, grads, charge, radius, rate, held_ref, sent_ref):
    here = pl.ds(pl.multiple_of(meta[LISTED + 3] * HELD, HELD), HELD)
    total = grads[0]
    for n in range(1, N_COLS):
        total = total + grads[n]
    charges, radii = charge[...], radius[here, :]
    grad = -0.5 * charges * total
    held = (COULOMB * charges * charges / (2.0 * radii * radii) - COULOMB * grad) * rate[here, :]
    held_ref[...] = held
    for n in range(N_ROWS):
        sent_ref[n] = held


def chain_kernel(meta, pack_i, pack_j, chain_j, direct, out_ref, force, spread_ref, sides):
    force[...] = jnp.zeros_like(force)
    write_spread(spread_ref)
    sides[...] = pack_j[...]
    for n in range(N_ROWS):
        sides[n * HELD : (n + 1) * HELD, 6, :] = chain_j[n]

    def one_tile(ia, jb, same):
        col = columns(sides[jb], spread_ref, 7)
        xi, yi, zi, rho, vol, neck = (pack_i[ia, c : c + 1, :] for c in range(6))
        rho_sq, rho_gap = rho * rho, rho + NECK_GAP
        sums = [jnp.zeros((8, TILE), F32)] * 6
        for s in range(0, TILE, CHUNK):
            dx, dy, dz, q = offsets(xi, yi, zi, col, s)
            base = jnp.maximum(1.0 - q * INV_SQ, 0.0)
            weight = base * base
            w_slope = (-2.0 * INV_SQ) * base
            rho_j = col(s, 3)
            gap = rho_gap + rho_j
            off = q - gap * gap
            bump = jnp.exp2(off * off * (-LOG2E / NECK_WIDTH))
            bump = bump * (w_slope - weight * off * (2.0 / NECK_WIDTH))
            inv_i = 1.0 / (q + rho_sq)
            inv_j = 1.0 / (q + rho_j * rho_j)
            twice = 2.0 * weight
            slope_ij = col(s, 4) * (inv_i * inv_i) * (w_slope - twice * inv_i) + col(s, 5) * bump
            slope_ji = vol * (inv_j * inv_j) * (w_slope - twice * inv_j) + neck * bump
            slope_ji = slope_ji * col(s, 6)
            parts = [slope_ji * d for d in (dx, dy, dz)] + [slope_ij * d for d in (dx, dy, dz)]
            sums = [a + folded(v) for a, v in zip(sums, parts)]

        def add():
            at = ia // HELD * 2 + ia % 2
            for c in range(6):
                force[at, c] += sums[c]

        return add

    for_each_tile(meta, 0, meta[LISTED], one_tile)
    chain = jnp.sum(force[0:OWN_I], axis=2)
    for n in range(N_COLS):
        for b in range(2):
            out_ref[n, b, 0:3, :] = direct[2 * n + b]
            out_ref[n, b, 3:9, :] = chain[2 * n + b]


def last_kernel(meta, parts, chain, charge, vel, old, scale, vel_ref, force_ref):
    for b in range(2):
        here = slice(b * TILE, (b + 1) * TILE)
        total = parts[0, b]
        for n in range(1, N_COLS):
            total = total + parts[n, b]
        factor = chain[pl.ds(meta[LISTED + 2] * 2 + b, 1), :]
        force = (2.0 * COULOMB) * charge[:, here] * total[0:3] - 2.0 * (
            total[3:6] + factor * total[6:9]
        )
        force_ref[:, here] = force
        vel_ref[:, here] = vel[:, here] + scale[:, here] * (old[:, here] + force)


def tile_codes(lists, rep_at, row_at, col_at):
    list_a, list_g = lists[:, 0].astype(jnp.int32), lists[:, 1].astype(jnp.int32)
    reps = jnp.arange(N_REP, dtype=jnp.int32)[:, None]
    live = list_a >= 0
    counts = jnp.sum(live.astype(jnp.int32), axis=1)
    j_row = list_g // 2
    place_i = (list_a // 2 * N_REP + reps) * 2 + list_a % 2
    place_j = (j_row % N_ROWS * N_REP + j_row // N_ROWS) * 2 + list_g % 2
    same = (j_row == reps * N_ROWS + row_at) & (list_a == col_at * 2 + list_g % 2)
    none = I_BLOCKS * 256
    codes = jnp.where(live, place_i * 256 + place_j * 2 + same.astype(jnp.int32) - none, 0)
    other = jnp.arange(N_REP) != rep_at
    counted = jnp.where(other, counts, 0)
    before = jnp.sum(jnp.where(jnp.arange(N_REP)[:, None] < reps.T, counted[:, None], 0), axis=0)
    slot = jnp.arange(SLOTS, dtype=jnp.int32)[None, :]
    target = jnp.where(other[:, None], SLOTS + before[:, None] + slot, slot)
    hit = (target.reshape(1, LISTED) == jnp.arange(LISTED, dtype=jnp.int32)[:, None]) & live.reshape(1, LISTED)
    placed = none + jnp.sum(jnp.where(hit, codes.reshape(1, LISTED), 0), axis=1)
    own = jnp.sum(jnp.where(other, 0, counts))
    tail = jnp.stack([own, jnp.sum(counted), rep_at, col_at]).astype(jnp.int32)
    return jnp.concatenate([placed, tail])


def body(positions, velocities, old_forces, charges, atom_types, table, tile_pairs):
    rep_at = lax.axis_index(REP)
    row_at = lax.axis_index(ROWS)
    col_at = lax.axis_index(COLS)
    charge_row = charges.reshape(1, 2 * TILE)
    new_positions, sent, scale = called(
        first_kernel,
        [(3, 2 * TILE), (N_REP, 3, 4, TILE), (1, 2 * TILE)],
        [],
        [table],
        [
            positions,
            velocities,
            old_forces,
            charge_row,
            atom_types.reshape(1, 2 * TILE),
            tile_pairs.reshape(2, SLOTS),
        ],
    )
    held = exchanged(sent, REP)
    held_atoms = held[:, 0:2].reshape(HELD, 4, TILE)
    held_charges = held[:, 2, 2:4].reshape(HELD, TILE)
    meta = tile_codes(held[:, 2, 0:2, 0:SLOTS], rep_at, row_at, col_at)
    side_i = given_to_all(held_atoms, COLS, N_COLS).reshape(I_BLOCKS, 4, TILE)
    side_j = given_to_all(held_atoms, ROWS, N_ROWS).reshape(J_BLOCKS, 4, TILE)

    mask = ((2, TILE, TILE), F32)
    spread_6, spread_7 = (((32, n * TILE), jnp.bfloat16) for n in (6, 7))
    sums = ((I_BLOCKS + 1, 8, TILE), F32)
    sides = ((J_BLOCKS, 8, TILE), F32)
    born_parts, pack_i, pack_j = called(
        born_kernel,
        [(N_COLS, I_BLOCKS, TILE), (I_BLOCKS + 1, 8, TILE), (J_BLOCKS, 8, TILE)],
        [sums, mask, spread_6],
        [meta, table],
        [side_i, side_j],
    )
    born_parts = exchanged(born_parts, COLS)
    radius_i, sent, rate_i = called(
        radius_kernel,
        [(I_BLOCKS + 8, TILE), (N_ROWS, 2, HELD, TILE), (I_BLOCKS, TILE)],
        [],
        [meta, table],
        [born_parts, pack_i, held_charges],
    )
    rad_j = exchanged(sent, ROWS)
    grads, direct = called(
        pair_kernel,
        [(I_BLOCKS, TILE), (OWN_I, 3, TILE)],
        [sums, ((OWN_I + 1, 3, 8, TILE), F32), mask, spread_6, sides],
        [meta],
        [pack_i, pack_j, radius_i, rad_j],
    )
    grads = exchanged(grads.reshape(N_COLS, HELD, TILE), COLS)
    chain, sent = called(
        factor_kernel,
        [(HELD, TILE), (N_ROWS, HELD, TILE)],
        [],
        [meta],
        [grads, held_charges, radius_i, rate_i],
    )
    chain_j = exchanged(sent, ROWS)
    [shared] = called(
        chain_kernel,
        [(N_COLS, 2, 9, TILE)],
        [((OWN_I + 1, 6, 8, TILE), F32), spread_7, sides],
        [meta],
        [pack_i, pack_j, chain_j, direct],
    )
    parts = exchanged(shared, COLS)
    new_velocities, new_forces = called(
        last_kernel,
        [(3, 2 * TILE), (3, 2 * TILE)],
        [],
        [meta],
        [parts, chain, charge_row, velocities, old_forces, scale],
    )
    return (new_positions, new_velocities, new_forces)


def solution(mesh):
    split = Mesh(mesh.devices.reshape(SIZES), AXES)
    rows, cols = AXES[:4], AXES[4:]
    return jax.shard_map(
        body,
        mesh=split,
        in_specs=(
            P(None, AXES),
            P(None, AXES),
            P(None, AXES),
            P(AXES),
            P(AXES),
            P(),
            P(rows, cols, None, None),
        ),
        out_specs=(P(None, AXES), P(None, AXES), P(None, AXES)),
        check_vma=False,
    )
```

```python
import jax
import jax.numpy as jnp
from jax import lax
from jax.experimental import pallas as pl
from jax.experimental.pallas import tpu as pltpu
from jax.sharding import Mesh
from jax.sharding import PartitionSpec as P

TILE = 128
SLOTS = 32
CHUNK = 32
UNROLL = 4
LISTED = 128
PICKED = 2048

CUTOFF = 12.0
COULOMB = 32.0
TIMESTEP = 0.5
OFFSET = 0.09
NECK_GAP = 0.5
NECK_WIDTH = 16.0
INV_SQ = 1.0 / (CUTOFF * CUTOFF)
LOG2E = 1.4426950408889634
NO_KEY = 16777216.0

AXES = ("zh", "zl", "yh", "core", "x", "yl")
SIZES = (4, 4, 2, 2, 4, 2)
REP = ("zh",)
ROWS = ("zl", "yh", "core")
COLS = ("x", "yl")
N_REP, N_ROWS, N_COLS = 4, 16, 8
HELD = 2 * N_REP
I_BLOCKS = N_COLS * HELD
J_BLOCKS = N_ROWS * HELD
OWN_I = 2 * N_COLS

VMEM = pl.BlockSpec(memory_space=pltpu.VMEM)
SMEM = pl.BlockSpec(memory_space=pltpu.SMEM)
F32 = jnp.float32


def exchanged(pieces, axes):
    return lax.all_to_all(pieces, axes, 0, 0, tiled=True)


def called(kernel, outs, scratch, smem, vmem, inputs=VMEM, outputs=VMEM, kind=F32):
    return pl.pallas_call(
        kernel,
        out_shape=[jax.ShapeDtypeStruct(s, kind) for s in outs],
        in_specs=[SMEM] * len(smem) + [inputs] * len(vmem),
        out_specs=[outputs] * len(outs),
        scratch_shapes=[pltpu.VMEM(*s) if isinstance(s, tuple) else s for s in scratch],
        compiler_params=pltpu.CompilerParams(vmem_limit_bytes=32 * 1024 * 1024),
    )(*smem, *vmem)


def looked_up(table, types, rows):
    found = [jnp.zeros(types.shape, F32) for _ in rows]
    for kind in range(8):
        here = types == float(kind)
        found = [jnp.where(here, table[r, kind], f) for r, f in zip(rows, found)]
    return found


def folded(value):
    parts = [value[s : s + 8] for s in range(0, CHUNK, 8)]
    while len(parts) > 1:
        parts = [a + b for a, b in zip(parts[::2], parts[1::2])]
    return parts[0]


def write_mask(mask_ref):
    down = lax.broadcasted_iota(jnp.int32, (TILE, TILE), 0)
    across = lax.broadcasted_iota(jnp.int32, (TILE, TILE), 1)
    mask_ref[0] = jnp.ones((TILE, TILE), F32)
    mask_ref[1] = jnp.where(down == across, 0.0, 1.0)


def write_spread(spread_ref):
    row = lax.broadcasted_iota(jnp.int32, spread_ref.shape, 0)
    lane = lax.broadcasted_iota(jnp.int32, spread_ref.shape, 1)
    hit = (row % 8 == lane // TILE) & (row < 24)
    spread_ref[...] = jnp.where(hit, 1.0, 0.0).astype(jnp.bfloat16)


def columns(rows, spread_ref, count):
    high = rows.astype(jnp.bfloat16).astype(F32)
    rest = rows - high
    middle = rest.astype(jnp.bfloat16).astype(F32)
    parts = jnp.concatenate([high, middle, rest - middle, jnp.zeros_like(rows)], axis=0)
    spread = lax.dot_general(
        parts.astype(jnp.bfloat16),
        spread_ref[...],
        (((0,), (0,)), ((), ())),
        preferred_element_type=F32,
    )
    return lambda s, c: spread[s : s + CHUNK, c * TILE : (c + 1) * TILE]


def offsets(xi, yi, zi, col, s):
    dx = xi - col(s, 0)
    dy = yi - col(s, 1)
    dz = zi - col(s, 2)
    return dx, dy, dz, dx * dx + dy * dy + dz * dz


def decoded(code):
    return code >> 8, (code >> 1) & 127, code & 1


def for_each_tile(meta, first, count, one_tile):
    def step(k, _):
        for add in [
            one_tile(*decoded(meta[first + k * UNROLL + u])) for u in range(UNROLL)
        ]:
            add()
        return 0

    lax.fori_loop(0, (count + UNROLL - 1) // UNROLL, step, 0)


def first_kernel(
    table, pos_in, vel_in, old_in, charge_in, kinds_in, pairs_in, new_ref, sent_ref, kept_ref,
    pos, vel, old, charge, kinds, pairs, sems
):
    copies = [
        pltpu.make_async_copy(there, here, sems.at[n])
        for n, (there, here) in enumerate(
            (
                (pos_in, pos),
                (vel_in, vel),
                (old_in, old),
                (charge_in, charge),
                (kinds_in, kinds),
                (pairs_in, pairs),
            )
        )
    ]
    for copy in copies:
        copy.start()
    for copy in copies:
        copy.wait()
    types = kinds[...].astype(F32)
    [mass] = looked_up(table, types, (6,))
    new = pos[...] + TIMESTEP * vel[...] + TIMESTEP * TIMESTEP / (2.0 * mass) * old[...]
    scale = TIMESTEP / (2.0 * mass)
    new_ref[...] = new
    kept_ref[0:3] = vel[...] + scale * old[...]
    kept_ref[3:4] = scale
    kept_ref[4:5] = charge[...]
    lists = pairs[...].astype(F32)
    lists = jnp.concatenate([lists, jnp.zeros((2, TILE - SLOTS), F32)], axis=1)
    for n in range(N_REP):
        for b in range(2):
            here = slice(b * TILE, (b + 1) * TILE)
            sent_ref[n, b, 0:3, :] = new[:, here]
            sent_ref[n, b, 3:4, :] = types[:, here]
            sent_ref[n, 2, 2 + b : 3 + b, :] = charge[:, here]
        sent_ref[n, 2, 0:2, :] = lists


def col_kernel(places, held, sent_ref):
    lists = held[places[0], 2, 0:2, :]
    for n in range(N_COLS):
        for z in range(N_REP):
            sent_ref[n, 2 * z] = held[z, 0]
            sent_ref[n, 2 * z + 1] = held[z, 1]
            at = z % 2 * 2
            sent_ref[n, 8 + z // 2, at : at + 2, :] = held[z, 2, 2:4, :]
        sent_ref[n, 10, 0:2, :] = lists
        sent_ref[n, 10, 2:4, :] = lists


def row_kernel(places, side_i, sent_ref):
    rows = [
        jnp.concatenate(
            [side_i[4 * half + n, 10, r : r + 1, 0:SLOTS] for n in range(4)], axis=1
        )
        for r in range(2)
        for half in range(2)
    ]
    lists = jnp.concatenate(rows, axis=0)
    for n in range(N_ROWS):
        for b in range(HELD):
            sent_ref[n, b] = side_i[places[2], b]
        sent_ref[n, HELD] = lists


def pick_kernel(keys_ref, picked):
    keys = keys_ref[...]
    count = jnp.sum(jnp.where(keys < NO_KEY, 1.0, 0.0)).astype(jnp.int32)

    def step(k, keys):
        least = jnp.min(keys)
        place = least.astype(jnp.int32) >> 12
        picked[k] = (place >> 6) * 256 + (place & 63) * 2
        return jnp.where(keys == least, NO_KEY, keys)

    lax.fori_loop(0, count, step, keys)
    for n in range(UNROLL):
        picked[count + n] = 2 * N_ROWS * 256
    picked[PICKED + UNROLL] = count


def born_kernel(
    meta,
    table,
    side_i,
    side_j,
    out_ref,
    pack_i,
    pack_j,
    charge_i,
    acc,
    mask_ref,
    spread_ref,
):
    acc[...] = jnp.zeros_like(acc)
    write_mask(mask_ref)
    write_spread(spread_ref)
    for side, pack, groups in ((side_i, pack_i, N_COLS), (side_j, pack_j, N_ROWS)):
        for n in range(groups):
            here = slice(n * HELD, (n + 1) * HELD)
            types = side[n, 0:HELD, 3, :]
            rho, scale, neck = looked_up(table, types, (0, 1, 2))
            pack[here, 0:3, :] = side[n, 0:HELD, 0:3, :]
            pack[here, 3, :] = rho
            pack[here, 4, :] = scale * rho * rho * rho
            pack[here, 5, :] = neck
            pack[here, 6, :] = types
            pack[here, 7, :] = types
    pack_i[I_BLOCKS] = jnp.ones((8, TILE), F32)
    pack_j[J_BLOCKS] = jnp.ones((8, TILE), F32)
    for n in range(N_COLS):
        charge_i[n * HELD : n * HELD + 4] = side_i[n, 8]
        charge_i[n * HELD + 4 : (n + 1) * HELD] = side_i[n, 9]

    def one_tile(ia, jb, same):
        col = columns(pack_j[jb], spread_ref, 6)
        xi, yi, zi, rho = (pack_i[ia, c : c + 1, :] for c in range(4))
        rho_sq, rho_gap = rho * rho, rho + NECK_GAP
        total = jnp.zeros((8, TILE), F32)
        for s in range(0, TILE, CHUNK):
            _, _, _, q = offsets(xi, yi, zi, col, s)
            base = jnp.maximum(1.0 - q * INV_SQ, 0.0)
            weight = base * base * mask_ref[same, s : s + CHUNK, :]
            inv = 1.0 / (q + rho_sq)
            gap = rho_gap + col(s, 3)
            off = q - gap * gap
            bump = jnp.exp2(off * off * (-LOG2E / NECK_WIDTH))
            total += folded(weight * (col(s, 4) * (inv * inv) + col(s, 5) * bump))

        def add():
            acc[ia] += total

        return add

    for_each_tile(meta, 0, meta[LISTED], one_tile)
    for_each_tile(meta, SLOTS, meta[LISTED + 1], one_tile)
    born = jnp.sum(acc[0:I_BLOCKS], axis=1)
    for n in range(N_COLS):
        out_ref[n] = born


def radius_kernel(places, table, parts, pack_i, charge, radius_ref, sent_ref, rate_ref):
    col_at = places[2]
    born = parts[0]
    for n in range(1, N_COLS):
        born = born + parts[n]
    rho = pack_i[0:I_BLOCKS, 3, :]
    alpha, beta, gamma = looked_up(table, pack_i[0:I_BLOCKS, 6, :], (3, 4, 5))
    scaled = rho * born
    poly = alpha * scaled - beta * scaled * scaled + gamma * scaled * scaled * scaled
    squash = jnp.tanh(poly)
    radius = 1.0 / (1.0 / rho - squash / (rho + OFFSET))
    slope = alpha - 2.0 * beta * scaled + 3.0 * gamma * scaled * scaled
    rate_ref[...] = radius * radius * (1.0 - squash * squash) * slope * rho / (rho + OFFSET)
    radius_ref[0:I_BLOCKS] = radius
    radius_ref[I_BLOCKS : I_BLOCKS + 8] = jnp.ones((8, TILE), F32)
    here = pl.ds(pl.multiple_of(col_at * HELD, HELD), HELD)
    held, charges = radius_ref[here, :], charge[here, :]
    for n in range(N_ROWS):
        sent_ref[n, 0] = held
        sent_ref[n, 1] = charges


def slope_kernel(meta, pack_i, pack_j, out_ref, force, spread_ref):
    force[...] = jnp.zeros_like(force)
    write_spread(spread_ref)

    def one_tile(ia, jb, same):
        col = columns(pack_j[jb], spread_ref, 6)
        xi, yi, zi, rho = (pack_i[ia, c : c + 1, :] for c in range(4))
        rho_sq, rho_gap = rho * rho, rho + NECK_GAP
        sums = [jnp.zeros((8, TILE), F32)] * 3
        for s in range(0, TILE, CHUNK):
            dx, dy, dz, q = offsets(xi, yi, zi, col, s)
            base = jnp.maximum(1.0 - q * INV_SQ, 0.0)
            weight = base * base
            w_slope = (-2.0 * INV_SQ) * base
            gap = rho_gap + col(s, 3)
            off = q - gap * gap
            bump = jnp.exp2(off * off * (-LOG2E / NECK_WIDTH))
            bump = bump * (w_slope - weight * off * (2.0 / NECK_WIDTH))
            inv = 1.0 / (q + rho_sq)
            slope = col(s, 4) * (inv * inv) * (w_slope - 2.0 * weight * inv) + col(s, 5) * bump
            sums = [a + folded(slope * d) for a, d in zip(sums, (dx, dy, dz))]

        def add():
            at = ia // HELD * 2 + ia % 2
            for c in range(3):
                force[at, c] += sums[c]

        return add

    for_each_tile(meta, 0, meta[LISTED], one_tile)
    out_ref[...] = jnp.sum(force[0:OWN_I], axis=2)


def pair_kernel(
    meta, pack_i, pack_j, rad_i, rad_j, slopes, out_ref, acc, force, mask_ref, spread_ref, sides
):
    acc[...] = jnp.zeros_like(acc)
    force[...] = jnp.zeros_like(force)
    write_mask(mask_ref)
    write_spread(spread_ref)
    sides[...] = pack_j[0:J_BLOCKS]
    for n in range(N_ROWS):
        here = slice(n * HELD, (n + 1) * HELD)
        sides[here, 3, :] = rad_j[n, 0]
        sides[here, 4, :] = 1.0 / rad_j[n, 0]
        sides[here, 5, :] = rad_j[n, 1]

    def one_tile(ia, jb, same, with_force):
        col = columns(sides[jb], spread_ref, 6)
        xi, yi, zi = (pack_i[ia, c : c + 1, :] for c in range(3))
        radius_i = rad_i[pl.ds(ia, 1), :]
        quarter_i = 0.25 / radius_i
        total = jnp.zeros((8, TILE), F32)
        sums = [jnp.zeros((8, TILE), F32)] * 3
        for s in range(0, TILE, CHUNK):
            dx, dy, dz, q = offsets(xi, yi, zi, col, s)
            base = jnp.maximum(1.0 - q * INV_SQ, 0.0)
            weight = base * base * mask_ref[same, s : s + CHUNK, :]
            arg = q * (quarter_i * col(s, 4))
            decay = jnp.exp2(arg * -LOG2E)
            inv = lax.rsqrt(q + radius_i * col(s, 3) * decay)
            weighted = weight * col(s, 5) * (inv * inv * inv)
            total += folded(weighted * col(s, 3) * (decay * (1.0 + arg)))
            if with_force:
                slope = (-2.0 * INV_SQ) * base * col(s, 5) * inv - weighted * (
                    0.5 - 0.125 * decay
                )
                sums = [a + folded(slope * d) for a, d in zip(sums, (dx, dy, dz))]

        def add():
            acc[ia] += total
            if with_force:
                at = ia // HELD * 2 + ia % 2
                for c in range(3):
                    force[at, c] += sums[c]

        return add

    for_each_tile(meta, 0, meta[LISTED], lambda *a: one_tile(*a, True))
    for_each_tile(meta, SLOTS, meta[LISTED + 1], lambda *a: one_tile(*a, False))
    grads = jnp.sum(acc[0:I_BLOCKS], axis=1)
    direct = jnp.sum(force[0:OWN_I], axis=2)
    for n in range(N_COLS):
        out_ref[n, 0:I_BLOCKS] = grads
        for b in range(2):
            at = I_BLOCKS + 8 * b
            out_ref[n, at : at + 3, :] = direct[2 * n + b]
            out_ref[n, at + 3 : at + 6, :] = slopes[2 * n + b]
            out_ref[n, at + 6 : at + 8, :] = slopes[2 * n + b, 0:2, :]


def chain_kernel(
    picked, places, pack_i, pack_j, parts, charge, radius, rate, out_ref, own_ref, force, spread_ref, sides
):
    force[...] = jnp.zeros_like(force)
    write_spread(spread_ref)
    total = parts[0]
    for n in range(1, N_COLS):
        total = total + parts[n]
    charges, radii = charge[...], radius[0:I_BLOCKS]
    grad = -0.5 * charges * total[0:I_BLOCKS]
    chain = (COULOMB * charges * charges / (2.0 * radii * radii) - COULOMB * grad) * rate[...]
    sides[...] = pack_i[0:I_BLOCKS]
    sides[:, 4, :] = chain
    first = places[2] * HELD + places[0] * 2
    own_ref[0:16] = total[I_BLOCKS : I_BLOCKS + 16]
    for b in range(2):
        own_ref[16 + b : 17 + b] = sides[first + b, 4:5, :]

    def one_tile(at, jb, same):
        ib = jnp.where(at < 2 * N_ROWS, at // 2 * HELD + places[0] * 2 + at % 2, J_BLOCKS)
        col = columns(sides[jb], spread_ref, 5)
        xi, yi, zi, rho, vol, neck = (pack_j[ib, c : c + 1, :] for c in range(6))
        rho_gap = rho + NECK_GAP
        sums = [jnp.zeros((8, TILE), F32)] * 3
        for s in range(0, TILE, CHUNK):
            dx, dy, dz, q = offsets(xi, yi, zi, col, s)
            base = jnp.maximum(1.0 - q * INV_SQ, 0.0)
            weight = base * base
            w_slope = (-2.0 * INV_SQ) * base
            rho_j = col(s, 3)
            gap = rho_gap + rho_j
            off = q - gap * gap
            bump = jnp.exp2(off * off * (-LOG2E / NECK_WIDTH))
            bump = bump * (w_slope - weight * off * (2.0 / NECK_WIDTH))
            inv = 1.0 / (q + rho_j * rho_j)
            slope = vol * (inv * inv) * (w_slope - 2.0 * weight * inv) + neck * bump
            slope = slope * col(s, 4)
            sums = [a + folded(slope * d) for a, d in zip(sums, (dx, dy, dz))]

        def add():
            for c in range(3):
                force[at, c] += sums[c]

        return add

    for_each_tile(picked, 0, picked[PICKED + UNROLL], one_tile)
    out_ref[...] = jnp.sum(force[0 : 2 * N_ROWS], axis=2)


def last_kernel(parts, own, kept, vel_ref, force_ref):
    for b in range(2):
        here = slice(b * TILE, (b + 1) * TILE)
        total = parts[0, b]
        for n in range(1, N_ROWS):
            total = total + parts[n, b]
        force = (2.0 * COULOMB) * kept[4:5, here] * own[8 * b : 8 * b + 3, :] - 2.0 * (
            total + own[16 + b : 17 + b, :] * own[8 * b + 3 : 8 * b + 6, :]
        )
        force_ref[:, here] = force
        vel_ref[:, here] = kept[0:3, here] + kept[3:4, here] * force


def transposed_keys(lists, places):
    list_a, list_g = lists[:, 0:2].astype(jnp.int32), lists[:, 2:4].astype(jnp.int32)
    source, half, lane = (lax.broadcasted_iota(jnp.int32, list_a.shape, n) for n in range(3))
    j_col, j_row = half * 4 + lane // SLOTS, list_g // 2
    mine = (list_a >= 0) & (list_a // 2 == places[2]) & (j_row % N_ROWS == places[1])
    place_j = (j_col * N_REP + j_row // N_ROWS) * 2 + list_g % 2
    key = ((source * 2 + list_a % 2) * I_BLOCKS + place_j) * 4096
    key = key + (source * 2 + half) * TILE + lane
    return jnp.where(mine, key.astype(F32), NO_KEY).reshape(2 * N_ROWS, TILE)


def tile_codes(lists, rep_at, row_at, col_at):
    list_a, list_g = lists[:, 0].astype(jnp.int32), lists[:, 1].astype(jnp.int32)
    reps = jnp.arange(N_REP, dtype=jnp.int32)[:, None]
    live = list_a >= 0
    counts = jnp.sum(live.astype(jnp.int32), axis=1)
    j_row = list_g // 2
    place_i = (list_a // 2 * N_REP + reps) * 2 + list_a % 2
    place_j = (j_row % N_ROWS * N_REP + j_row // N_ROWS) * 2 + list_g % 2
    same = (j_row == reps * N_ROWS + row_at) & (list_a == col_at * 2 + list_g % 2)
    none = I_BLOCKS * 256
    codes = jnp.where(live, place_i * 256 + place_j * 2 + same.astype(jnp.int32) - none, 0)
    other = jnp.arange(N_REP) != rep_at
    counted = jnp.where(other, counts, 0)
    before = jnp.sum(jnp.where(jnp.arange(N_REP)[:, None] < reps.T, counted[:, None], 0), axis=0)
    slot = jnp.arange(SLOTS, dtype=jnp.int32)[None, :]
    target = jnp.where(other[:, None], SLOTS + before[:, None] + slot, slot)
    hit = (target.reshape(1, LISTED) == jnp.arange(LISTED, dtype=jnp.int32)[:, None]) & live.reshape(1, LISTED)
    placed = none + jnp.sum(jnp.where(hit, codes.reshape(1, LISTED), 0), axis=1)
    own = jnp.sum(jnp.where(other, 0, counts))
    tail = jnp.stack([own, jnp.sum(counted), rep_at, col_at]).astype(jnp.int32)
    return jnp.concatenate([placed, tail])


def body(positions, velocities, old_forces, charges, atom_types, table, tile_pairs):
    rep_at = lax.axis_index(REP)
    row_at = lax.axis_index(ROWS)
    col_at = lax.axis_index(COLS)
    places = jnp.stack([rep_at, row_at, col_at]).astype(jnp.int32)
    row = (1, 2 * TILE)
    new_positions, sent, kept = called(
        first_kernel,
        [(3, 2 * TILE), (N_REP, 3, 4, TILE), (5, 2 * TILE)],
        [((3, 2 * TILE), F32)] * 3
        + [(row, F32), (row, jnp.int32), ((2, SLOTS), jnp.int32), pltpu.SemaphoreType.DMA((6,))],
        [table],
        [
            positions,
            velocities,
            old_forces,
            charges.reshape(row),
            atom_types.reshape(row),
            tile_pairs.reshape(2, SLOTS),
        ],
        inputs=pl.BlockSpec(memory_space=pl.ANY),
    )
    held = exchanged(sent, REP)
    meta = tile_codes(held[:, 2, 0:2, 0:SLOTS], rep_at, row_at, col_at)
    [sent] = called(col_kernel, [(N_COLS, 11, 4, TILE)], [], [places], [held])
    side_i = exchanged(sent, COLS)
    [sent] = called(row_kernel, [(N_ROWS, 9, 4, TILE)], [], [places], [side_i])
    side_j = exchanged(sent, ROWS)

    mask = ((2, TILE, TILE), F32)
    spread_5, spread_6 = (((32, n * TILE), jnp.bfloat16) for n in (5, 6))
    sums = ((I_BLOCKS + 1, 8, TILE), F32)
    forces = ((OWN_I + 1, 3, 8, TILE), F32)
    born_parts, pack_i, pack_j, charge_i = called(
        born_kernel,
        [
            (N_COLS, I_BLOCKS, TILE),
            (I_BLOCKS + 1, 8, TILE),
            (J_BLOCKS + 1, 8, TILE),
            (I_BLOCKS, TILE),
        ],
        [sums, mask, spread_6],
        [meta, table],
        [side_i, side_j],
    )
    born_parts = exchanged(born_parts, COLS)
    [slopes] = called(
        slope_kernel, [(OWN_I, 3, TILE)], [forces, spread_6], [meta], [pack_i, pack_j]
    )
    [picked] = called(
        pick_kernel,
        [(PICKED + UNROLL + 1,)],
        [],
        [],
        [transposed_keys(side_j[:, HELD], places)],
        outputs=SMEM,
        kind=jnp.int32,
    )
    radius_i, sent, rate_i = called(
        radius_kernel,
        [(I_BLOCKS + 8, TILE), (N_ROWS, 2, HELD, TILE), (I_BLOCKS, TILE)],
        [],
        [places, table],
        [born_parts, pack_i, charge_i],
    )
    rad_j = exchanged(sent, ROWS)
    [parts] = called(
        pair_kernel,
        [(N_COLS, I_BLOCKS + 16, TILE)],
        [sums, forces, mask, spread_6, ((J_BLOCKS, 8, TILE), F32)],
        [meta],
        [pack_i, pack_j, radius_i, rad_j, slopes],
    )
    parts = exchanged(parts, COLS)
    forces_part, own = called(
        chain_kernel,
        [(2 * N_ROWS, 3, TILE), (18, TILE)],
        [
            ((2 * N_ROWS + 1, 3, 8, TILE), F32),
            spread_5,
            ((I_BLOCKS, 8, TILE), F32),
        ],
        [picked, places],
        [pack_i, pack_j, parts, charge_i, radius_i, rate_i],
    )
    parts = exchanged(forces_part.reshape(N_ROWS, 2, 3, TILE), ROWS)
    new_velocities, new_forces = called(
        last_kernel, [(3, 2 * TILE), (3, 2 * TILE)], [], [], [parts, own, kept]
    )
    return (new_positions, new_velocities, new_forces)


def solution(mesh):
    split = Mesh(mesh.devices.reshape(SIZES), AXES)
    rows, cols = AXES[:4], AXES[4:]
    return jax.shard_map(
        body,
        mesh=split,
        in_specs=(
            P(None, AXES),
            P(None, AXES),
            P(None, AXES),
            P(AXES),
            P(AXES),
            P(),
            P(rows, cols, None, None),
        ),
        out_specs=(P(None, AXES), P(None, AXES), P(None, AXES)),
        check_vma=False,
    )
```

```python
import jax
import jax.numpy as jnp
from jax import lax
from jax.experimental import pallas as pl
from jax.experimental.pallas import tpu as pltpu
from jax.sharding import Mesh
from jax.sharding import PartitionSpec as P

TILE = 128
SLOTS = 32
CHUNK = 32
UNROLL = 8
LISTED = 128
PICKED = 2048

CUTOFF = 12.0
COULOMB = 32.0
TIMESTEP = 0.5
OFFSET = 0.09
NECK_GAP = 0.5
NECK_WIDTH = 16.0
INV_SQ = 1.0 / (CUTOFF * CUTOFF)
LOG2E = 1.4426950408889634
NO_KEY = 16777216.0

AXES = ("zh", "zl", "yh", "core", "x", "yl")
SIZES = (4, 4, 2, 2, 4, 2)
REP = ("zh",)
ROWS = ("zl", "yh", "core")
COLS = ("x", "yl")
N_REP, N_ROWS, N_COLS = 4, 16, 8
HELD = 2 * N_REP
I_BLOCKS = N_COLS * HELD
J_BLOCKS = N_ROWS * HELD
OWN_I = 2 * N_COLS

VMEM = pl.BlockSpec(memory_space=pltpu.VMEM)
SMEM = pl.BlockSpec(memory_space=pltpu.SMEM)
F32 = jnp.float32


def exchanged(pieces, axes):
    return lax.all_to_all(pieces, axes, 0, 0, tiled=True)


def called(kernel, outs, scratch, smem, vmem, inputs=VMEM, outputs=VMEM, kind=F32):
    return pl.pallas_call(
        kernel,
        out_shape=[jax.ShapeDtypeStruct(s, kind) for s in outs],
        in_specs=[SMEM] * len(smem) + [inputs] * len(vmem),
        out_specs=[outputs] * len(outs),
        scratch_shapes=[pltpu.VMEM(*s) if isinstance(s, tuple) else s for s in scratch],
        compiler_params=pltpu.CompilerParams(vmem_limit_bytes=32 * 1024 * 1024),
    )(*smem, *vmem)


def looked_up(table, types, rows):
    found = [jnp.zeros(types.shape, F32) for _ in rows]
    for kind in range(8):
        here = types == float(kind)
        found = [jnp.where(here, table[r, kind], f) for r, f in zip(rows, found)]
    return found


def folded(value):
    parts = [value[s : s + 8] for s in range(0, CHUNK, 8)]
    while len(parts) > 1:
        parts = [a + b for a, b in zip(parts[::2], parts[1::2])]
    return parts[0]


def write_mask(mask_ref):
    down = lax.broadcasted_iota(jnp.int32, (TILE, TILE), 0)
    across = lax.broadcasted_iota(jnp.int32, (TILE, TILE), 1)
    mask_ref[0] = jnp.ones((TILE, TILE), F32)
    mask_ref[1] = jnp.where(down == across, 0.0, 1.0)


def write_spread(spread_ref):
    row = lax.broadcasted_iota(jnp.int32, spread_ref.shape, 0)
    lane = lax.broadcasted_iota(jnp.int32, spread_ref.shape, 1)
    hit = (row % 8 == lane // TILE) & (row < 24)
    spread_ref[...] = jnp.where(hit, 1.0, 0.0).astype(jnp.bfloat16)


def columns(rows, spread_ref, count):
    high = rows.astype(jnp.bfloat16).astype(F32)
    rest = rows - high
    middle = rest.astype(jnp.bfloat16).astype(F32)
    parts = jnp.concatenate([high, middle, rest - middle, jnp.zeros_like(rows)], axis=0)
    spread = lax.dot_general(
        parts.astype(jnp.bfloat16),
        spread_ref[...],
        (((0,), (0,)), ((), ())),
        preferred_element_type=F32,
    )
    return lambda s, c: spread[s : s + CHUNK, c * TILE : (c + 1) * TILE]


def offsets(xi, yi, zi, col, s):
    dx = xi - col(s, 0)
    dy = yi - col(s, 1)
    dz = zi - col(s, 2)
    return dx, dy, dz, dx * dx + dy * dy + dz * dz


def decoded(code):
    return code >> 8, (code >> 1) & 127, code & 1


def for_each_tile(meta, first, count, one_tile):
    def steps(begin, number, width):
        def step(k, _):
            at = begin + k * width
            for add in [one_tile(*decoded(meta[at + u])) for u in range(width)]:
                add()
            return 0

        lax.fori_loop(0, number, step, 0)

    half = UNROLL // 2
    whole = (count + half - 1) // UNROLL
    steps(first, whole, UNROLL)
    steps(first + whole * UNROLL, jnp.where(count > whole * UNROLL, 1, 0), half)


def typed_spread(table, spread_ref):
    row = lax.broadcasted_iota(jnp.int32, (48, TILE), 0)
    for c in range(3):
        hit = (row % 4 == c) & (row < 12)
        spread_ref[:, c * TILE : (c + 1) * TILE] = jnp.where(hit, 1.0, 0.0).astype(jnp.bfloat16)
    kind = (row % 8).astype(F32)
    rho, scale, neck = looked_up(table, kind, (0, 1, 2))
    for c, value in enumerate((rho, scale * rho * rho * rho, neck)):
        high = value.astype(jnp.bfloat16).astype(F32)
        rest = value - high
        middle = rest.astype(jnp.bfloat16).astype(F32)
        part = jnp.where(row < 24, high, jnp.where(row < 32, middle, rest - middle))
        part = jnp.where((row >= 16) & (row < 40), part, 0.0)
        spread_ref[:, (3 + c) * TILE : (4 + c) * TILE] = part.astype(jnp.bfloat16)


def typed_columns(atoms, spread_ref):
    high = atoms.astype(jnp.bfloat16).astype(F32)
    rest = atoms - high
    middle = rest.astype(jnp.bfloat16).astype(F32)
    kinds = lax.broadcasted_iota(jnp.int32, (8, TILE), 0).astype(F32)
    hot = jnp.where(atoms[3:4, :] == kinds, 1.0, 0.0)
    parts = jnp.concatenate(
        [high, middle, rest - middle, jnp.zeros((4, TILE), F32), hot, hot, hot, jnp.zeros((8, TILE), F32)],
        axis=0,
    )
    spread = lax.dot_general(
        parts.astype(jnp.bfloat16),
        spread_ref[...],
        (((0,), (0,)), ((), ())),
        preferred_element_type=F32,
    )
    return lambda s, c: spread[s : s + CHUNK, c * TILE : (c + 1) * TILE]


def j_atoms(side_j, jb):
    return side_j[jb // HELD, jb % HELD]


def first_kernel(
    table, pos_in, vel_in, old_in, charge_in, kinds_in, pairs_in, new_ref, sent_ref, kept_ref,
    pos, vel, old, charge, kinds, pairs, sems
):
    copies = [
        pltpu.make_async_copy(there, here, sems.at[n])
        for n, (there, here) in enumerate(
            (
                (pos_in, pos),
                (vel_in, vel),
                (old_in, old),
                (charge_in, charge),
                (kinds_in, kinds),
                (pairs_in, pairs),
            )
        )
    ]
    for copy in copies:
        copy.start()
    for copy in copies:
        copy.wait()
    types = kinds[...].astype(F32)
    [mass] = looked_up(table, types, (6,))
    new = pos[...] + TIMESTEP * vel[...] + TIMESTEP * TIMESTEP / (2.0 * mass) * old[...]
    scale = TIMESTEP / (2.0 * mass)
    new_ref[...] = new
    kept_ref[0:3] = vel[...] + scale * old[...]
    kept_ref[3:4] = scale
    kept_ref[4:5] = charge[...]
    lists = pairs[...].astype(F32)
    lists = jnp.concatenate([lists, jnp.zeros((2, TILE - SLOTS), F32)], axis=1)
    for n in range(N_REP):
        for b in range(2):
            here = slice(b * TILE, (b + 1) * TILE)
            sent_ref[n, b, 0:3, :] = new[:, here]
            sent_ref[n, b, 3:4, :] = types[:, here]
            sent_ref[n, 2, 2 + b : 3 + b, :] = charge[:, here]
        sent_ref[n, 2, 0:2, :] = lists


def row_kernel(places, side_i, sent_ref):
    rows = [
        jnp.concatenate(
            [
                side_i[4 * half + n, places[0], 2, r : r + 1, 0:SLOTS]
                for n in range(4)
            ],
            axis=1,

        )
        for r in range(2)
        for half in range(2)
    ]
    lists = jnp.concatenate(rows, axis=0)
    for n in range(N_ROWS):
        for b in range(HELD):
            sent_ref[n, b] = side_i[places[2], b // 2, b % 2]
        sent_ref[n, HELD] = lists


def pick_kernel(keys_ref, picked):
    keys = keys_ref[...]
    count = jnp.sum(jnp.where(keys < NO_KEY, 1.0, 0.0)).astype(jnp.int32)

    def step(k, keys):
        least = jnp.min(keys)
        place = least.astype(jnp.int32) >> 12
        picked[k] = (place >> 6) * 256 + (place & 63) * 2
        return jnp.where(keys == least, NO_KEY, keys)

    lax.fori_loop(0, count, step, keys)
    for n in range(UNROLL):
        picked[count + n] = 2 * N_ROWS * 256
    picked[PICKED + UNROLL] = count


def packed(table, pack, count, more):
    types = pack[0:count, 3, :]
    found = looked_up(table, types, (0, 1, 2) + more)
    rho = found[0]
    pack[0:count, 3, :] = rho
    pack[0:count, 4, :] = found[1] * rho * rho * rho
    pack[0:count, 5, :] = found[2]
    return rho, found[3:]


def pack_kernel(table, side_i, pack_i, charge_i, more_i):
    for n in range(N_COLS):
        for z in range(N_REP):
            at = n * HELD + 2 * z
            for b in range(2):
                pack_i[at + b, 0:4, :] = side_i[n, z, b]
                pack_i[at + b, 4:8, :] = side_i[n, z, b]
            charge_i[at : at + 2] = side_i[n, z, 2, 2:4, :]
    pack_i[I_BLOCKS] = jnp.ones((8, TILE), F32)
    rho, more = packed(table, pack_i, I_BLOCKS, (3, 4, 5))
    for n, value in enumerate((*more, 1.0 / rho, 1.0 / (rho + OFFSET))):
        more_i[n] = value


def born_kernel(meta, table, pack_i, side_j, out_ref, acc, mask_ref, spread_ref):
    acc[...] = jnp.zeros_like(acc)
    write_mask(mask_ref)
    typed_spread(table, spread_ref)

    def one_tile(ia, jb, same):
        col = typed_columns(j_atoms(side_j, jb), spread_ref)
        xi, yi, zi, rho = (pack_i[ia, c : c + 1, :] for c in range(4))
        rho_sq, rho_gap = rho * rho, rho + NECK_GAP
        total = jnp.zeros((8, TILE), F32)
        for s in range(0, TILE, CHUNK):
            _, _, _, q = offsets(xi, yi, zi, col, s)
            base = jnp.maximum(1.0 - q * INV_SQ, 0.0)
            weight = base * base * mask_ref[same, s : s + CHUNK, :]
            inv = 1.0 / (q + rho_sq)
            gap = rho_gap + col(s, 3)
            off = q - gap * gap
            bump = jnp.exp2(off * off * (-LOG2E / NECK_WIDTH))
            total += folded(weight * (col(s, 4) * (inv * inv) + col(s, 5) * bump))

        def add():
            acc[ia] += total

        return add

    for_each_tile(meta, 0, meta[LISTED], one_tile)
    for_each_tile(meta, SLOTS, meta[LISTED + 1], one_tile)
    born = jnp.sum(acc[0:I_BLOCKS], axis=1)
    for n in range(N_COLS):
        out_ref[n] = born


def radius_kernel(places, parts, pack_i, more_i, charge, radius_ref, sent_ref, rate_ref):
    born = parts[0]
    for n in range(1, N_COLS):
        born = born + parts[n]
    rho = pack_i[0:I_BLOCKS, 3, :]
    alpha, beta, gamma, inv_rho, inv_offset = (more_i[n] for n in range(5))
    scaled = rho * born
    poly = alpha * scaled - beta * scaled * scaled + gamma * scaled * scaled * scaled
    squash = jnp.tanh(poly)
    radius = 1.0 / (inv_rho - squash * inv_offset)
    slope = alpha - 2.0 * beta * scaled + 3.0 * gamma * scaled * scaled
    rate_ref[...] = radius * radius * (1.0 - squash * squash) * slope * rho * inv_offset
    radius_ref[0:I_BLOCKS] = radius
    radius_ref[I_BLOCKS : I_BLOCKS + 8] = jnp.ones((8, TILE), F32)
    here = pl.ds(pl.multiple_of(places[2] * HELD, HELD), HELD)
    held, charges = radius_ref[here, :], charge[here, :]
    for n in range(N_ROWS):
        sent_ref[n, 0] = held
        sent_ref[n, 1] = charges


def slope_kernel(meta, table, pack_i, side_j, out_ref, own_j, force, spread_ref):
    force[...] = jnp.zeros_like(force)
    typed_spread(table, spread_ref)
    for n in range(N_ROWS):
        for b in range(2):
            block = side_j[n, meta[LISTED + 2] * 2 + b]
            own_j[2 * n + b, 0:4, :] = block
            own_j[2 * n + b, 4:8, :] = block
    own_j[2 * N_ROWS] = jnp.ones((8, TILE), F32)
    packed(table, own_j, 2 * N_ROWS, ())

    def one_tile(ia, jb, same):
        col = typed_columns(j_atoms(side_j, jb), spread_ref)
        xi, yi, zi, rho = (pack_i[ia, c : c + 1, :] for c in range(4))
        rho_sq, rho_gap = rho * rho, rho + NECK_GAP
        sums = [jnp.zeros((8, TILE), F32)] * 3
        for s in range(0, TILE, CHUNK):
            dx, dy, dz, q = offsets(xi, yi, zi, col, s)
            base = jnp.maximum(1.0 - q * INV_SQ, 0.0)
            weight = base * base
            w_slope = (-2.0 * INV_SQ) * base
            gap = rho_gap + col(s, 3)
            off = q - gap * gap
            bump = jnp.exp2(off * off * (-LOG2E / NECK_WIDTH))
            bump = bump * (w_slope - weight * off * (2.0 / NECK_WIDTH))
            inv = 1.0 / (q + rho_sq)
            slope = col(s, 4) * (inv * inv) * (w_slope - 2.0 * weight * inv) + col(s, 5) * bump
            sums = [a + folded(slope * d) for a, d in zip(sums, (dx, dy, dz))]

        def add():
            at = ia // HELD * 2 + ia % 2
            for c in range(3):
                force[at, c] += sums[c]

        return add

    for_each_tile(meta, 0, meta[LISTED], one_tile)
    out_ref[...] = jnp.sum(force[0:OWN_I], axis=2)


def pair_kernel(
    meta, pack_i, side_j, rad_i, rad_j, slopes, out_ref, acc, force, mask_ref, spread_ref, sides
):
    acc[...] = jnp.zeros_like(acc)
    force[...] = jnp.zeros_like(force)
    write_mask(mask_ref)
    write_spread(spread_ref)
    for n in range(N_ROWS):
        here = slice(n * HELD, (n + 1) * HELD)
        sides[here, 0:4, :] = side_j[n, 0:HELD]
        sides[here, 4:8, :] = side_j[n, 0:HELD]
        sides[here, 3, :] = rad_j[n, 0]
        sides[here, 4, :] = 1.0 / rad_j[n, 0]
        sides[here, 5, :] = rad_j[n, 1]

    def one_tile(ia, jb, same, with_force):
        col = columns(sides[jb], spread_ref, 6)
        xi, yi, zi = (pack_i[ia, c : c + 1, :] for c in range(3))
        radius_i = rad_i[pl.ds(ia, 1), :]
        quarter_i = 0.25 / radius_i
        total = jnp.zeros((8, TILE), F32)
        sums = [jnp.zeros((8, TILE), F32)] * 3
        for s in range(0, TILE, CHUNK):
            dx, dy, dz, q = offsets(xi, yi, zi, col, s)
            base = jnp.maximum(1.0 - q * INV_SQ, 0.0)
            weight = base * base * mask_ref[same, s : s + CHUNK, :]
            arg = q * (quarter_i * col(s, 4))
            decay = jnp.exp2(arg * -LOG2E)
            inv = lax.rsqrt(q + radius_i * col(s, 3) * decay)
            weighted = weight * col(s, 5) * (inv * inv * inv)
            total += folded(weighted * col(s, 3) * (decay * (1.0 + arg)))
            if with_force:
                slope = (-2.0 * INV_SQ) * base * col(s, 5) * inv - weighted * (
                    0.5 - 0.125 * decay
                )
                sums = [a + folded(slope * d) for a, d in zip(sums, (dx, dy, dz))]

        def add():
            acc[ia] += total
            if with_force:
                at = ia // HELD * 2 + ia % 2
                for c in range(3):
                    force[at, c] += sums[c]

        return add

    for_each_tile(meta, 0, meta[LISTED], lambda *a: one_tile(*a, True))
    for_each_tile(meta, SLOTS, meta[LISTED + 1], lambda *a: one_tile(*a, False))
    grads = jnp.sum(acc[0:I_BLOCKS], axis=1)
    direct = jnp.sum(force[0:OWN_I], axis=2)
    for n in range(N_COLS):
        out_ref[n, 0:I_BLOCKS] = grads
        for b in range(2):
            at = I_BLOCKS + 8 * b
            out_ref[n, at : at + 3, :] = direct[2 * n + b]
            out_ref[n, at + 3 : at + 6, :] = slopes[2 * n + b]
            out_ref[n, at + 6 : at + 8, :] = slopes[2 * n + b, 0:2, :]


def chain_kernel(
    picked, places, pack_i, own_j, parts, charge, radius, rate, out_ref, own_ref, force, spread_ref, sides
):
    force[...] = jnp.zeros_like(force)
    write_spread(spread_ref)
    total = parts[0]
    for n in range(1, N_COLS):
        total = total + parts[n]
    charges, radii = charge[...], radius[0:I_BLOCKS]
    grad = -0.5 * charges * total[0:I_BLOCKS]
    chain = (COULOMB * charges * charges / (2.0 * radii * radii) - COULOMB * grad) * rate[...]
    sides[...] = pack_i[0:I_BLOCKS]
    sides[:, 4, :] = chain
    first = places[2] * HELD + places[0] * 2
    own_ref[0:16] = total[I_BLOCKS : I_BLOCKS + 16]
    for b in range(2):
        own_ref[16 + b : 17 + b] = sides[first + b, 4:5, :]

    def one_tile(at, jb, same):
        col = columns(sides[jb], spread_ref, 5)
        xi, yi, zi, rho, vol, neck = (own_j[at, c : c + 1, :] for c in range(6))
        rho_gap = rho + NECK_GAP
        sums = [jnp.zeros((8, TILE), F32)] * 3
        for s in range(0, TILE, CHUNK):
            dx, dy, dz, q = offsets(xi, yi, zi, col, s)
            base = jnp.maximum(1.0 - q * INV_SQ, 0.0)
            weight = base * base
            w_slope = (-2.0 * INV_SQ) * base
            rho_j = col(s, 3)
            gap = rho_gap + rho_j
            off = q - gap * gap
            bump = jnp.exp2(off * off * (-LOG2E / NECK_WIDTH))
            bump = bump * (w_slope - weight * off * (2.0 / NECK_WIDTH))
            inv = 1.0 / (q + rho_j * rho_j)
            slope = vol * (inv * inv) * (w_slope - 2.0 * weight * inv) + neck * bump
            slope = slope * col(s, 4)
            sums = [a + folded(slope * d) for a, d in zip(sums, (dx, dy, dz))]

        def add():
            for c in range(3):
                force[at, c] += sums[c]

        return add

    for_each_tile(picked, 0, picked[PICKED + UNROLL], one_tile)
    out_ref[...] = jnp.sum(force[0 : 2 * N_ROWS], axis=2)


def last_kernel(parts, own, kept, vel_ref, force_ref):
    for b in range(2):
        here = slice(b * TILE, (b + 1) * TILE)
        total = parts[0, b]
        for n in range(1, N_ROWS):
            total = total + parts[n, b]
        force = (2.0 * COULOMB) * kept[4:5, here] * own[8 * b : 8 * b + 3, :] - 2.0 * (
            total + own[16 + b : 17 + b, :] * own[8 * b + 3 : 8 * b + 6, :]
        )
        force_ref[:, here] = force
        vel_ref[:, here] = kept[0:3, here] + kept[3:4, here] * force


def transposed_keys(lists, places):
    list_a, list_g = lists[:, 0:2].astype(jnp.int32), lists[:, 2:4].astype(jnp.int32)
    source, half, lane = (lax.broadcasted_iota(jnp.int32, list_a.shape, n) for n in range(3))
    j_col, j_row = half * 4 + lane // SLOTS, list_g // 2
    mine = (list_a >= 0) & (list_a // 2 == places[2]) & (j_row % N_ROWS == places[1])
    place_j = (j_col * N_REP + j_row // N_ROWS) * 2 + list_g % 2
    key = ((source * 2 + list_a % 2) * I_BLOCKS + place_j) * 4096
    key = key + (source * 2 + half) * TILE + lane
    return jnp.where(mine, key.astype(F32), NO_KEY).reshape(2 * N_ROWS, TILE)


def tile_codes(lists, rep_at, row_at, col_at):
    list_a, list_g = lists[:, 0].astype(jnp.int32), lists[:, 1].astype(jnp.int32)
    reps = jnp.arange(N_REP, dtype=jnp.int32)[:, None]
    live = list_a >= 0
    counts = jnp.sum(live.astype(jnp.int32), axis=1)
    j_row = list_g // 2
    place_i = (list_a // 2 * N_REP + reps) * 2 + list_a % 2
    place_j = (j_row % N_ROWS * N_REP + j_row // N_ROWS) * 2 + list_g % 2
    same = (j_row == reps * N_ROWS + row_at) & (list_a == col_at * 2 + list_g % 2)
    none = I_BLOCKS * 256
    codes = jnp.where(live, place_i * 256 + place_j * 2 + same.astype(jnp.int32) - none, 0)
    other = jnp.arange(N_REP) != rep_at
    counted = jnp.where(other, counts, 0)
    before = jnp.sum(jnp.where(jnp.arange(N_REP)[:, None] < reps.T, counted[:, None], 0), axis=0)
    slot = jnp.arange(SLOTS, dtype=jnp.int32)[None, :]
    target = jnp.where(other[:, None], SLOTS + before[:, None] + slot, slot)
    hit = (target.reshape(1, LISTED) == jnp.arange(LISTED, dtype=jnp.int32)[:, None]) & live.reshape(1, LISTED)
    placed = none + jnp.sum(jnp.where(hit, codes.reshape(1, LISTED), 0), axis=1)
    own = jnp.sum(jnp.where(other, 0, counts))
    tail = jnp.stack([own, jnp.sum(counted), rep_at, col_at]).astype(jnp.int32)
    return jnp.concatenate([placed, tail])


def body(positions, velocities, old_forces, charges, atom_types, table, tile_pairs):
    rep_at = lax.axis_index(REP)
    row_at = lax.axis_index(ROWS)
    col_at = lax.axis_index(COLS)
    places = jnp.stack([rep_at, row_at, col_at]).astype(jnp.int32)
    row = (1, 2 * TILE)
    new_positions, sent, kept = called(
        first_kernel,
        [(3, 2 * TILE), (N_REP, 3, 4, TILE), (5, 2 * TILE)],
        [((3, 2 * TILE), F32)] * 3
        + [(row, F32), (row, jnp.int32), ((2, SLOTS), jnp.int32), pltpu.SemaphoreType.DMA((6,))],
        [table],
        [
            positions,
            velocities,
            old_forces,
            charges.reshape(row),
            atom_types.reshape(row),
            tile_pairs.reshape(2, SLOTS),
        ],
        inputs=pl.BlockSpec(memory_space=pltpu.HBM),
    )
    held = exchanged(sent, REP)
    meta = tile_codes(held[:, 2, 0:2, 0:SLOTS], rep_at, row_at, col_at)
    side_i = exchanged(jnp.broadcast_to(held, (N_COLS, *held.shape)), COLS)
    [sent] = called(row_kernel, [(N_ROWS, 9, 4, TILE)], [], [places], [side_i])
    side_j = exchanged(sent, ROWS)

    mask = ((2, TILE, TILE), F32)
    spread_5, spread_6 = (((32, n * TILE), jnp.bfloat16) for n in (5, 6))
    typed = ((48, 6 * TILE), jnp.bfloat16)
    sums = ((I_BLOCKS + 1, 8, TILE), F32)
    forces = ((OWN_I + 1, 3, 8, TILE), F32)
    pack_i, charge_i, more_i = called(
        pack_kernel,
        [(I_BLOCKS + 1, 8, TILE), (I_BLOCKS, TILE), (5, I_BLOCKS, TILE)],
        [],
        [table],
        [side_i],
    )
    [born_parts] = called(
        born_kernel,
        [(N_COLS, I_BLOCKS, TILE)],
        [sums, mask, typed],
        [meta, table],
        [pack_i, side_j],
    )
    born_parts = exchanged(born_parts, COLS)
    slopes, own_j = called(
        slope_kernel,
        [(OWN_I, 3, TILE), (2 * N_ROWS + 1, 8, TILE)],
        [forces, typed],
        [meta, table],
        [pack_i, side_j],
    )
    [picked] = called(
        pick_kernel,
        [(PICKED + UNROLL + 1,)],
        [],
        [],
        [transposed_keys(side_j[:, HELD], places)],
        outputs=SMEM,
        kind=jnp.int32,
    )
    radius_i, sent, rate_i = called(
        radius_kernel,
        [(I_BLOCKS + 8, TILE), (N_ROWS, 2, HELD, TILE), (I_BLOCKS, TILE)],
        [],
        [places],
        [born_parts, pack_i, more_i, charge_i],
    )
    rad_j = exchanged(sent, ROWS)
    [parts] = called(
        pair_kernel,
        [(N_COLS, I_BLOCKS + 16, TILE)],
        [sums, forces, mask, spread_6, ((J_BLOCKS, 8, TILE), F32)],
        [meta],
        [pack_i, side_j, radius_i, rad_j, slopes],
    )
    parts = exchanged(parts, COLS)
    forces_part, own = called(
        chain_kernel,
        [(2 * N_ROWS, 3, TILE), (18, TILE)],
        [
            ((2 * N_ROWS + 1, 3, 8, TILE), F32),
            spread_5,
            ((I_BLOCKS, 8, TILE), F32),
        ],
        [picked, places],
        [pack_i, own_j, parts, charge_i, radius_i, rate_i],
    )
    parts = exchanged(forces_part.reshape(N_ROWS, 2, 3, TILE), ROWS)
    new_velocities, new_forces = called(
        last_kernel, [(3, 2 * TILE), (3, 2 * TILE)], [], [], [parts, own, kept]
    )
    return (new_positions, new_velocities, new_forces)


def solution(mesh):
    split = Mesh(mesh.devices.reshape(SIZES), AXES)
    rows, cols = AXES[:4], AXES[4:]
    return jax.shard_map(
        body,
        mesh=split,
        in_specs=(
            P(None, AXES),
            P(None, AXES),
            P(None, AXES),
            P(AXES),
            P(AXES),
            P(),
            P(rows, cols, None, None),
        ),
        out_specs=(P(None, AXES), P(None, AXES), P(None, AXES)),
        check_vma=False,
    )
```

```python
import jax
import jax.numpy as jnp
from jax import lax
from jax.experimental import pallas as pl
from jax.experimental.pallas import tpu as pltpu
from jax.sharding import Mesh
from jax.sharding import PartitionSpec as P

TILE = 128
SLOTS = 32
CHUNK = 32
UNROLL = 8
LISTED = 128
PICKED = 2048

CUTOFF = 12.0
COULOMB = 32.0
TIMESTEP = 0.5
OFFSET = 0.09
NECK_GAP = 0.5
NECK_WIDTH = 16.0
INV_SQ = 1.0 / (CUTOFF * CUTOFF)
LOG2E = 1.4426950408889634
NO_KEY = 16777216.0

AXES = ("zh", "zl", "yh", "core", "x", "yl")
SIZES = (4, 4, 2, 2, 4, 2)
REP = ("zh",)
ROWS = ("zl", "yh", "core")
COLS = ("x", "yl")
N_REP, N_ROWS, N_COLS = 4, 16, 8
HELD = 2 * N_REP
I_BLOCKS = N_COLS * HELD
J_BLOCKS = N_ROWS * HELD

VMEM = pl.BlockSpec(memory_space=pltpu.VMEM)
SMEM = pl.BlockSpec(memory_space=pltpu.SMEM)
F32 = jnp.float32


def exchanged(pieces, axes):
    return lax.all_to_all(pieces, axes, 0, 0, tiled=True)


def called(kernel, outs, scratch, smem, vmem, inputs=VMEM, outputs=VMEM, kind=F32):
    return pl.pallas_call(
        kernel,
        out_shape=[jax.ShapeDtypeStruct(s, kind) for s in outs],
        in_specs=[SMEM] * len(smem) + [inputs] * len(vmem),
        out_specs=[outputs] * len(outs),
        scratch_shapes=[pltpu.VMEM(*s) if isinstance(s, tuple) else s for s in scratch],
        compiler_params=pltpu.CompilerParams(vmem_limit_bytes=32 * 1024 * 1024),
    )(*smem, *vmem)


def looked_up(table, types, rows):
    found = [jnp.zeros(types.shape, F32) for _ in rows]
    for kind in range(8):
        here = types == float(kind)
        found = [jnp.where(here, table[r, kind], f) for r, f in zip(rows, found)]
    return found


def folded(value):
    parts = [value[s : s + 8] for s in range(0, CHUNK, 8)]
    while len(parts) > 1:
        parts = [a + b for a, b in zip(parts[::2], parts[1::2])]
    return parts[0]


def write_mask(mask_ref):
    down = lax.broadcasted_iota(jnp.int32, (TILE, TILE), 0)
    across = lax.broadcasted_iota(jnp.int32, (TILE, TILE), 1)
    mask_ref[0] = jnp.ones((TILE, TILE), F32)
    mask_ref[1] = jnp.where(down == across, 0.0, 1.0)


def write_spread(spread_ref):
    row = lax.broadcasted_iota(jnp.int32, spread_ref.shape, 0)
    lane = lax.broadcasted_iota(jnp.int32, spread_ref.shape, 1)
    hit = (row % 8 == lane // TILE) & (row < 24)
    spread_ref[...] = jnp.where(hit, 1.0, 0.0).astype(jnp.bfloat16)


def columns(rows, spread_ref, count):
    high = rows.astype(jnp.bfloat16).astype(F32)
    rest = rows - high
    middle = rest.astype(jnp.bfloat16).astype(F32)
    parts = jnp.concatenate([high, middle, rest - middle, jnp.zeros_like(rows)], axis=0)
    spread = lax.dot_general(
        parts.astype(jnp.bfloat16),
        spread_ref[...],
        (((0,), (0,)), ((), ())),
        preferred_element_type=F32,
    )
    return lambda s, c: spread[s : s + CHUNK, c * TILE : (c + 1) * TILE]


def offsets(xi, yi, zi, col, s):
    dx = xi - col(s, 0)
    dy = yi - col(s, 1)
    dz = zi - col(s, 2)
    return dx, dy, dz, dx * dx + dy * dy + dz * dz


def decoded(code):
    return code >> 8, (code >> 1) & 127, code & 1


def for_each_tile(meta, first, count, one_tile):
    def steps(begin, number, width):
        def step(k, _):
            at = begin + k * width
            for add in [one_tile(*decoded(meta[at + u])) for u in range(width)]:
                add()
            return 0

        lax.fori_loop(0, number, step, 0)

    half = UNROLL // 2
    whole = (count + half - 1) // UNROLL
    steps(first, whole, UNROLL)
    steps(first + whole * UNROLL, jnp.where(count > whole * UNROLL, 1, 0), half)


def typed_spread(table, spread_ref):
    row = lax.broadcasted_iota(jnp.int32, (48, TILE), 0)
    for c in range(3):
        hit = (row % 4 == c) & (row < 12)
        spread_ref[:, c * TILE : (c + 1) * TILE] = jnp.where(hit, 1.0, 0.0).astype(jnp.bfloat16)
    kind = (row % 8).astype(F32)
    rho, scale, neck = looked_up(table, kind, (0, 1, 2))
    for c, value in enumerate((rho, scale * rho * rho * rho, neck)):
        high = value.astype(jnp.bfloat16).astype(F32)
        rest = value - high
        middle = rest.astype(jnp.bfloat16).astype(F32)
        part = jnp.where(row < 24, high, jnp.where(row < 32, middle, rest - middle))
        part = jnp.where((row >= 16) & (row < 40), part, 0.0)
        spread_ref[:, (3 + c) * TILE : (4 + c) * TILE] = part.astype(jnp.bfloat16)


def typed_columns(atoms, spread_ref):
    high = atoms.astype(jnp.bfloat16).astype(F32)
    rest = atoms - high
    middle = rest.astype(jnp.bfloat16).astype(F32)
    kinds = lax.broadcasted_iota(jnp.int32, (8, TILE), 0).astype(F32)
    hot = jnp.where(atoms[3:4, :] == kinds, 1.0, 0.0)
    parts = jnp.concatenate(
        [high, middle, rest - middle, jnp.zeros((4, TILE), F32), hot, hot, hot, jnp.zeros((8, TILE), F32)],
        axis=0,
    )
    spread = lax.dot_general(
        parts.astype(jnp.bfloat16),
        spread_ref[...],
        (((0,), (0,)), ((), ())),
        preferred_element_type=F32,
    )
    return lambda s, c: spread[s : s + CHUNK, c * TILE : (c + 1) * TILE]


def j_atoms(side_j, jb):
    return side_j[jb // HELD, jb % HELD]


def first_kernel(table, joined, new_ref, sent_ref, kept_ref):
    pos, vel, old = joined[0:3], joined[3:6], joined[6:9]
    charge, types, lists = joined[9:10], joined[10:11], joined[11:13, 0:TILE]
    [mass] = looked_up(table, types, (6,))
    new = pos + TIMESTEP * vel + TIMESTEP * TIMESTEP / (2.0 * mass) * old
    scale = TIMESTEP / (2.0 * mass)
    new_ref[...] = new
    kept_ref[0:3] = vel + scale * old
    kept_ref[3:4] = scale
    kept_ref[4:5] = charge
    for n in range(N_REP):
        for b in range(2):
            here = slice(b * TILE, (b + 1) * TILE)
            sent_ref[n, b, 0:3, :] = new[:, here]
            sent_ref[n, b, 3:4, :] = types[:, here]
            sent_ref[n, 2, 2 + b : 3 + b, :] = charge[:, here]
        sent_ref[n, 2, 0:2, :] = lists


def row_kernel(places, side_i, sent_ref):
    rows = [
        jnp.concatenate(
            [
                side_i[4 * half + n, places[0], 2, r : r + 1, 0:SLOTS]
                for n in range(4)
            ],
            axis=1,

        )
        for r in range(2)
        for half in range(2)
    ]
    lists = jnp.concatenate(rows, axis=0)
    for n in range(N_ROWS):
        for b in range(HELD):
            sent_ref[n, b] = side_i[places[2], b // 2, b % 2]
        sent_ref[n, HELD] = lists


def pick_kernel(keys_ref, picked):
    keys = keys_ref[...]
    count = jnp.sum(jnp.where(keys < NO_KEY, 1.0, 0.0)).astype(jnp.int32)

    def step(k, keys):
        least = jnp.min(keys)
        place = least.astype(jnp.int32) >> 12
        picked[k] = (place >> 6) * 256 + (place & 63) * 2
        return jnp.where(keys == least, NO_KEY, keys)

    lax.fori_loop(0, count, step, keys)
    for n in range(UNROLL):
        picked[count + n] = 2 * N_ROWS * 256
    picked[PICKED + UNROLL] = count


def packed(table, pack, count, more):
    types = pack[0:count, 3, :]
    found = looked_up(table, types, (0, 1, 2) + more)
    rho = found[0]
    pack[0:count, 3, :] = rho
    pack[0:count, 4, :] = found[1] * rho * rho * rho
    pack[0:count, 5, :] = found[2]
    return rho, found[3:]


def pack_kernel(table, side_i, pack_i, charge_i, more_i):
    for n in range(N_COLS):
        for z in range(N_REP):
            at = n * HELD + 2 * z
            for b in range(2):
                pack_i[at + b, 0:4, :] = side_i[n, z, b]
                pack_i[at + b, 4:8, :] = side_i[n, z, b]
            charge_i[at : at + 2] = side_i[n, z, 2, 2:4, :]
    pack_i[I_BLOCKS] = jnp.ones((8, TILE), F32)
    rho, more = packed(table, pack_i, I_BLOCKS, (3, 4, 5))
    for n, value in enumerate((*more, 1.0 / rho, 1.0 / (rho + OFFSET))):
        more_i[n] = value


def born_kernel(meta, table, pack_i, side_j, out_ref, acc, mask_ref, spread_ref):
    acc[...] = jnp.zeros_like(acc)
    write_mask(mask_ref)
    typed_spread(table, spread_ref)

    def one_tile(ia, jb, same):
        col = typed_columns(j_atoms(side_j, jb), spread_ref)
        xi, yi, zi, rho = (pack_i[ia, c : c + 1, :] for c in range(4))
        rho_sq, rho_gap = rho * rho, rho + NECK_GAP
        total = jnp.zeros((8, TILE), F32)
        for s in range(0, TILE, CHUNK):
            _, _, _, q = offsets(xi, yi, zi, col, s)
            base = jnp.maximum(1.0 - q * INV_SQ, 0.0)
            weight = base * base * mask_ref[same, s : s + CHUNK, :]
            inv = 1.0 / (q + rho_sq)
            gap = rho_gap + col(s, 3)
            off = q - gap * gap
            bump = jnp.exp2(off * off * (-LOG2E / NECK_WIDTH))
            total += folded(weight * (col(s, 4) * (inv * inv) + col(s, 5) * bump))

        def add():
            acc[ia] += total

        return add

    for_each_tile(meta, 0, meta[LISTED], one_tile)
    born = jnp.sum(acc[0:I_BLOCKS], axis=1)
    for n in range(N_COLS):
        out_ref[n] = born


def radius_kernel(places, parts, pack_i, more_i, charge, ready, radius_ref, sent_ref, rate_ref):
    born = parts[0]
    for n in range(1, N_COLS):
        born = born + parts[n]
    rho = pack_i[0:I_BLOCKS, 3, :]
    alpha, beta, gamma, inv_rho, inv_offset = (more_i[n] for n in range(5))
    scaled = rho * born
    poly = alpha * scaled - beta * scaled * scaled + gamma * scaled * scaled * scaled
    squash = jnp.tanh(poly)
    radius = 1.0 / (inv_rho - squash * inv_offset)
    slope = alpha - 2.0 * beta * scaled + 3.0 * gamma * scaled * scaled
    rate_ref[...] = radius * radius * (1.0 - squash * squash) * slope * rho * inv_offset
    radius_ref[0:I_BLOCKS] = radius
    radius_ref[I_BLOCKS : I_BLOCKS + 8] = jnp.ones((8, TILE), F32)
    here = pl.ds(pl.multiple_of(places[2] * HELD, HELD), HELD)
    held, charges = radius_ref[here, :], charge[here, :]
    for n in range(N_ROWS):
        sent_ref[n, 0] = held
        sent_ref[n, 1] = charges


def slope_kernel(picked, places, table, pack_i, side_j, out_ref, own_j, force, spread_ref):
    force[...] = jnp.zeros_like(force)
    write_spread(spread_ref)
    for n in range(N_ROWS):
        for b in range(2):
            block = side_j[n, places[0] * 2 + b]
            own_j[2 * n + b, 0:4, :] = block
            own_j[2 * n + b, 4:8, :] = block
    own_j[2 * N_ROWS] = jnp.ones((8, TILE), F32)
    packed(table, own_j, 2 * N_ROWS, ())

    def one_tile(at, jb, same):
        col = columns(pack_i[jb], spread_ref, 6)
        xi, yi, zi, rho = (own_j[at, c : c + 1, :] for c in range(4))
        rho_sq, rho_gap = rho * rho, rho + NECK_GAP
        sums = [jnp.zeros((8, TILE), F32)] * 3
        for s in range(0, TILE, CHUNK):
            dx, dy, dz, q = offsets(xi, yi, zi, col, s)
            base = jnp.maximum(1.0 - q * INV_SQ, 0.0)
            weight = base * base
            w_slope = (-2.0 * INV_SQ) * base
            gap = rho_gap + col(s, 3)
            off = q - gap * gap
            bump = jnp.exp2(off * off * (-LOG2E / NECK_WIDTH))
            bump = bump * (w_slope - weight * off * (2.0 / NECK_WIDTH))
            inv = 1.0 / (q + rho_sq)
            slope = col(s, 4) * (inv * inv) * (w_slope - 2.0 * weight * inv) + col(s, 5) * bump
            sums = [a + folded(slope * d) for a, d in zip(sums, (dx, dy, dz))]

        def add():
            for c in range(3):
                force[at, c] += sums[c]

        return add

    for_each_tile(picked, 0, picked[PICKED + UNROLL], one_tile)
    out_ref[...] = jnp.sum(force[0 : 2 * N_ROWS], axis=2)


def direct_kernel(
    picked, places, own_j, pack_i, rad_j, radius_i, charge_i, out_ref, force, spread_ref, sides, own
):
    force[...] = jnp.zeros_like(force)
    write_spread(spread_ref)
    sides[...] = pack_i[0:I_BLOCKS]
    radii = radius_i[0:I_BLOCKS]
    sides[:, 3, :] = radii
    sides[:, 4, :] = 1.0 / radii
    sides[:, 5, :] = charge_i[...]
    own[...] = jnp.ones_like(own)
    for n in range(N_ROWS):
        own[2 * n : 2 * n + 2] = rad_j[n, 0, pl.ds(places[0] * 2, 2), :]

    def one_tile(at, jb, same):
        col = columns(sides[jb], spread_ref, 6)
        xi, yi, zi = (own_j[at, c : c + 1, :] for c in range(3))
        radius = own[pl.ds(at, 1), :]
        quarter = 0.25 / radius
        sums = [jnp.zeros((8, TILE), F32)] * 3
        for s in range(0, TILE, CHUNK):
            dx, dy, dz, q = offsets(xi, yi, zi, col, s)
            base = jnp.maximum(1.0 - q * INV_SQ, 0.0)
            decay = jnp.exp2(q * (quarter * col(s, 4)) * -LOG2E)
            inv = lax.rsqrt(q + radius * col(s, 3) * decay)
            slope = (-2.0 * INV_SQ) * base - base * base * (inv * inv) * (0.5 - 0.125 * decay)
            slope = slope * (inv * col(s, 5))
            sums = [a + folded(slope * d) for a, d in zip(sums, (dx, dy, dz))]

        def add():
            for c in range(3):
                force[at, c] += sums[c]

        return add

    for_each_tile(picked, 0, picked[PICKED + UNROLL], one_tile)
    out_ref[...] = jnp.sum(force[0 : 2 * N_ROWS], axis=2)


def pair_kernel(
    meta, pack_i, side_j, rad_i, rad_j, ready, out_ref, acc, mask_ref, spread_ref, sides
):
    acc[...] = jnp.zeros_like(acc)
    write_mask(mask_ref)
    write_spread(spread_ref)
    for n in range(N_ROWS):
        here = slice(n * HELD, (n + 1) * HELD)
        sides[here, 0:4, :] = side_j[n, 0:HELD]
        sides[here, 4:8, :] = side_j[n, 0:HELD]
        sides[here, 3, :] = rad_j[n, 0]
        sides[here, 4, :] = 1.0 / rad_j[n, 0]
        sides[here, 5, :] = rad_j[n, 1]

    def one_tile(ia, jb, same):
        col = columns(sides[jb], spread_ref, 6)
        xi, yi, zi = (pack_i[ia, c : c + 1, :] for c in range(3))
        radius_i = rad_i[pl.ds(ia, 1), :]
        quarter_i = 0.25 / radius_i
        total = jnp.zeros((8, TILE), F32)
        for s in range(0, TILE, CHUNK):
            _, _, _, q = offsets(xi, yi, zi, col, s)
            base = jnp.maximum(1.0 - q * INV_SQ, 0.0)
            weight = base * base * mask_ref[same, s : s + CHUNK, :]
            arg = q * (quarter_i * col(s, 4))
            decay = jnp.exp2(arg * -LOG2E)
            inv = lax.rsqrt(q + radius_i * col(s, 3) * decay)
            weighted = weight * col(s, 5) * (inv * inv * inv)
            total += folded(weighted * col(s, 3) * (decay * (1.0 + arg)))

        def add():
            acc[ia] += total

        return add

    for_each_tile(meta, 0, meta[LISTED], one_tile)
    grads = jnp.sum(acc[0:I_BLOCKS], axis=1)
    for n in range(N_COLS):
        out_ref[n] = grads


def chain_kernel(
    picked, places, pack_i, own_j, parts, charge, radius, rate, direct, slopes, out_ref, own_ref, force, spread_ref, sides
):
    force[...] = jnp.zeros_like(force)
    write_spread(spread_ref)
    total = parts[0]
    for n in range(1, N_COLS):
        total = total + parts[n]
    charges, radii = charge[...], radius[0:I_BLOCKS]
    grad = -0.5 * charges * total
    chain = (COULOMB * charges * charges / (2.0 * radii * radii) - COULOMB * grad) * rate[...]
    sides[...] = pack_i[0:I_BLOCKS]
    sides[:, 4, :] = chain
    first = places[2] * HELD + places[0] * 2
    for b in range(2):
        own_ref[b : b + 1] = sides[first + b, 4:5, :]

    def one_tile(at, jb, same):
        col = columns(sides[jb], spread_ref, 5)
        xi, yi, zi, rho, vol, neck = (own_j[at, c : c + 1, :] for c in range(6))
        rho_gap = rho + NECK_GAP
        sums = [jnp.zeros((8, TILE), F32)] * 3
        for s in range(0, TILE, CHUNK):
            dx, dy, dz, q = offsets(xi, yi, zi, col, s)
            base = jnp.maximum(1.0 - q * INV_SQ, 0.0)
            weight = base * base
            w_slope = (-2.0 * INV_SQ) * base
            rho_j = col(s, 3)
            gap = rho_gap + rho_j
            off = q - gap * gap
            bump = jnp.exp2(off * off * (-LOG2E / NECK_WIDTH))
            bump = bump * (w_slope - weight * off * (2.0 / NECK_WIDTH))
            inv = 1.0 / (q + rho_j * rho_j)
            slope = vol * (inv * inv) * (w_slope - 2.0 * weight * inv) + neck * bump
            slope = slope * col(s, 4)
            sums = [a + folded(slope * d) for a, d in zip(sums, (dx, dy, dz))]

        def add():
            for c in range(3):
                force[at, c] += sums[c]

        return add

    for_each_tile(picked, 0, picked[PICKED + UNROLL], one_tile)
    chained = jnp.sum(force[0 : 2 * N_ROWS], axis=2)
    for n in range(N_ROWS):
        for b in range(2):
            at = 2 * n + b
            for c, value in enumerate((chained, direct, slopes)):
                out_ref[n, 12 * b + 4 * c : 12 * b + 4 * c + 3, :] = value[at]
                out_ref[n, 12 * b + 4 * c + 3 : 12 * b + 4 * c + 4, :] = value[at, 0:1, :]


def last_kernel(parts, own, kept, vel_ref, force_ref):
    total = parts[0]
    for n in range(1, N_ROWS):
        total = total + parts[n]
    for b in range(2):
        here = slice(b * TILE, (b + 1) * TILE)
        chained, direct, slopes = (total[12 * b + 4 * c : 12 * b + 4 * c + 3] for c in range(3))
        force = (2.0 * COULOMB) * kept[4:5, here] * direct - 2.0 * (
            chained + own[b : b + 1, :] * slopes
        )
        force_ref[:, here] = force
        vel_ref[:, here] = kept[0:3, here] + kept[3:4, here] * force


def transposed_keys(lists, places):
    list_a, list_g = lists[:, 0:2].astype(jnp.int32), lists[:, 2:4].astype(jnp.int32)
    source, half, lane = (lax.broadcasted_iota(jnp.int32, list_a.shape, n) for n in range(3))
    j_col, j_row = half * 4 + lane // SLOTS, list_g // 2
    mine = (list_a >= 0) & (list_a // 2 == places[2]) & (j_row % N_ROWS == places[1])
    place_j = (j_col * N_REP + j_row // N_ROWS) * 2 + list_g % 2
    key = ((source * 2 + list_a % 2) * I_BLOCKS + place_j) * 4096
    key = key + (source * 2 + half) * TILE + lane
    return jnp.where(mine, key.astype(F32), NO_KEY).reshape(2 * N_ROWS, TILE)


def tile_codes(lists, row_at, col_at):
    list_a, list_g = lists[:, 0].astype(jnp.int32), lists[:, 1].astype(jnp.int32)
    reps = jnp.arange(N_REP, dtype=jnp.int32)[:, None]
    live = list_a >= 0
    counts = jnp.sum(live.astype(jnp.int32), axis=1)
    j_row = list_g // 2
    place_i = (list_a // 2 * N_REP + reps) * 2 + list_a % 2
    place_j = (j_row % N_ROWS * N_REP + j_row // N_ROWS) * 2 + list_g % 2
    same = (j_row == reps * N_ROWS + row_at) & (list_a == col_at * 2 + list_g % 2)
    none = I_BLOCKS * 256
    codes = place_i * 256 + place_j * 2 + same.astype(jnp.int32) - none
    before = jnp.sum(jnp.where(reps < reps.T, counts[:, None], 0), axis=0)
    target = before[:, None] + jnp.arange(SLOTS, dtype=jnp.int32)[None, :]
    target = jnp.where(live, target, -1).reshape(1, LISTED)
    hit = target == jnp.arange(LISTED, dtype=jnp.int32)[:, None]
    placed = none + jnp.sum(jnp.where(hit, codes.reshape(1, LISTED), 0), axis=1)
    return jnp.concatenate([placed, jnp.sum(counts)[None]]).astype(jnp.int32)


def body(positions, velocities, old_forces, charges, atom_types, table, tile_pairs):
    rep_at = lax.axis_index(REP)
    row_at = lax.axis_index(ROWS)
    col_at = lax.axis_index(COLS)
    places = jnp.stack([rep_at, row_at, col_at]).astype(jnp.int32)
    row = (1, 2 * TILE)
    joined = jnp.concatenate(
        [
            positions,
            velocities,
            old_forces,
            charges.reshape(row),
            atom_types.reshape(row).astype(F32),
            jnp.pad(tile_pairs.reshape(2, SLOTS).astype(F32), ((0, 0), (0, 2 * TILE - SLOTS))),
        ],
        axis=0,
    )
    new_positions, sent, kept = called(
        first_kernel,
        [(3, 2 * TILE), (N_REP, 3, 4, TILE), (5, 2 * TILE)],
        [],
        [table],
        [joined],
    )
    held = exchanged(sent, REP)
    meta = tile_codes(held[:, 2, 0:2, 0:SLOTS], row_at, col_at)
    side_i = exchanged(jnp.broadcast_to(held, (N_COLS, *held.shape)), COLS)
    [sent] = called(row_kernel, [(N_ROWS, 9, 4, TILE)], [], [places], [side_i])
    side_j = exchanged(sent, ROWS)

    mask = ((2, TILE, TILE), F32)
    spread_5, spread_6 = (((32, n * TILE), jnp.bfloat16) for n in (5, 6))
    typed = ((48, 6 * TILE), jnp.bfloat16)
    sums = ((I_BLOCKS + 1, 8, TILE), F32)
    forces = ((2 * N_ROWS + 1, 3, 8, TILE), F32)
    held_sides = ((I_BLOCKS, 8, TILE), F32)
    pack_i, charge_i, more_i = called(
        pack_kernel,
        [(I_BLOCKS + 1, 8, TILE), (I_BLOCKS, TILE), (5, I_BLOCKS, TILE)],
        [],
        [table],
        [side_i],
    )
    [born_parts] = called(
        born_kernel,
        [(N_COLS, I_BLOCKS, TILE)],
        [sums, mask, typed],
        [meta, table],
        [pack_i, side_j],
    )
    born_parts = exchanged(born_parts, COLS)
    [picked] = called(
        pick_kernel,
        [(PICKED + UNROLL + 1,)],
        [],
        [],
        [transposed_keys(side_j[:, HELD], places)],
        outputs=SMEM,
        kind=jnp.int32,
    )
    radius_i, sent, rate_i = called(
        radius_kernel,
        [(I_BLOCKS + 8, TILE), (N_ROWS, 2, HELD, TILE), (I_BLOCKS, TILE)],
        [],
        [places],
        [born_parts, pack_i, more_i, charge_i, picked],
    )
    rad_j = exchanged(sent, ROWS)
    slopes, own_j = called(
        slope_kernel,
        [(2 * N_ROWS, 3, TILE), (2 * N_ROWS + 1, 8, TILE)],
        [forces, spread_6],
        [picked, places, table],
        [pack_i, side_j],
    )
    [grads] = called(
        pair_kernel,
        [(N_COLS, I_BLOCKS, TILE)],
        [sums, mask, spread_6, ((J_BLOCKS, 8, TILE), F32)],
        [meta],
        [pack_i, side_j, radius_i, rad_j, slopes],
    )
    grads = exchanged(grads, COLS)
    [direct] = called(
        direct_kernel,
        [(2 * N_ROWS, 3, TILE)],
        [forces, spread_6, held_sides, ((2 * N_ROWS + 8, TILE), F32)],
        [picked, places],
        [own_j, pack_i, rad_j, radius_i, charge_i],
    )
    parts, own = called(
        chain_kernel,
        [(N_ROWS, 24, TILE), (2, TILE)],
        [forces, spread_5, held_sides],
        [picked, places],
        [pack_i, own_j, grads, charge_i, radius_i, rate_i, direct, slopes],
    )
    parts = exchanged(parts, ROWS)
    new_velocities, new_forces = called(
        last_kernel, [(3, 2 * TILE), (3, 2 * TILE)], [], [], [parts, own, kept]
    )
    return (new_positions, new_velocities, new_forces)


def solution(mesh):
    split = Mesh(mesh.devices.reshape(SIZES), AXES)
    rows, cols = AXES[:4], AXES[4:]
    return jax.shard_map(
        body,
        mesh=split,
        in_specs=(
            P(None, AXES),
            P(None, AXES),
            P(None, AXES),
            P(AXES),
            P(AXES),
            P(),
            P(rows, cols, None, None),
        ),
        out_specs=(P(None, AXES), P(None, AXES), P(None, AXES)),
        check_vma=False,
    )
```

```python
import jax
import jax.numpy as jnp
from jax import lax
from jax.experimental import pallas as pl
from jax.experimental.pallas import tpu as pltpu
from jax.sharding import Mesh
from jax.sharding import PartitionSpec as P

TILE = 128
SLOTS = 32
CHUNK = 32
UNROLL = 8
LISTED = 128
PICKED = 2048

CUTOFF = 12.0
COULOMB = 32.0
TIMESTEP = 0.5
OFFSET = 0.09
NECK_GAP = 0.5
NECK_WIDTH = 16.0
INV_SQ = 1.0 / (CUTOFF * CUTOFF)
LOG2E = 1.4426950408889634
NO_KEY = 16777216.0

AXES = ("zh", "zl", "yh", "core", "x", "yl")
SIZES = (4, 4, 2, 2, 4, 2)
REP = ("zh",)
ROWS = ("zl", "yh", "core")
COLS = ("x", "yl")
N_REP, N_ROWS, N_COLS = 4, 16, 8
HELD = 2 * N_REP
I_BLOCKS = N_COLS * HELD
J_BLOCKS = N_ROWS * HELD

VMEM = pl.BlockSpec(memory_space=pltpu.VMEM)
SMEM = pl.BlockSpec(memory_space=pltpu.SMEM)
F32 = jnp.float32


def exchanged(pieces, axes):
    return lax.all_to_all(pieces, axes, 0, 0, tiled=True)


def called(kernel, outs, scratch, smem, vmem, inputs=VMEM, outputs=VMEM, kind=F32):
    return pl.pallas_call(
        kernel,
        out_shape=[
            jax.ShapeDtypeStruct(*s) if isinstance(s[0], tuple) else jax.ShapeDtypeStruct(s, kind)
            for s in outs
        ],
        in_specs=[SMEM] * len(smem) + [inputs] * len(vmem),
        out_specs=[outputs] * len(outs),
        scratch_shapes=[pltpu.VMEM(*s) if isinstance(s, tuple) else s for s in scratch],
        compiler_params=pltpu.CompilerParams(vmem_limit_bytes=32 * 1024 * 1024),
    )(*smem, *vmem)


def looked_up(table, types, rows):
    found = [jnp.zeros(types.shape, F32) for _ in rows]
    for kind in range(8):
        here = types == float(kind)
        found = [jnp.where(here, table[r, kind], f) for r, f in zip(rows, found)]
    return found


def folded(value):
    parts = [value[s : s + 8] for s in range(0, CHUNK, 8)]
    while len(parts) > 1:
        parts = [a + b for a, b in zip(parts[::2], parts[1::2])]
    return parts[0]


def write_mask(mask_ref):
    down = lax.broadcasted_iota(jnp.int32, (TILE, TILE), 0)
    across = lax.broadcasted_iota(jnp.int32, (TILE, TILE), 1)
    mask_ref[0] = jnp.ones((TILE, TILE), F32)
    mask_ref[1] = jnp.where(down == across, 0.0, 1.0)


def write_spread(spread_ref, rows):
    at = lax.broadcasted_iota(jnp.int32, (32, TILE), 0)
    for c, row in enumerate(rows):
        hit = (at % 8 == row) & (at < 24)
        spread_ref[:, c * TILE : (c + 1) * TILE] = jnp.where(hit, 1.0, 0.0).astype(jnp.bfloat16)


def columns(rows, spread_ref):
    high = rows.astype(jnp.bfloat16).astype(F32)
    rest = rows - high
    middle = rest.astype(jnp.bfloat16).astype(F32)
    parts = jnp.concatenate([high, middle, rest - middle, jnp.zeros_like(rows)], axis=0)
    spread = lax.dot_general(
        parts.astype(jnp.bfloat16),
        spread_ref[...],
        (((0,), (0,)), ((), ())),
        preferred_element_type=F32,
    )
    return lambda s, c: spread[s : s + CHUNK, c * TILE : (c + 1) * TILE]


def offsets(xi, yi, zi, col, s):
    dx = xi - col(s, 0)
    dy = yi - col(s, 1)
    dz = zi - col(s, 2)
    return dx, dy, dz, dx * dx + dy * dy + dz * dz


def decoded(code):
    return code >> 8, (code >> 1) & 127, code & 1


def for_each_tile(meta, first, count, one_tile):
    def steps(begin, number, width):
        def step(k, _):
            at = begin + k * width
            for add in [one_tile(*decoded(meta[at + u])) for u in range(width)]:
                add()
            return 0

        lax.fori_loop(0, number, step, 0)

    half = UNROLL // 2
    whole = (count + half - 1) // UNROLL
    steps(first, whole, UNROLL)
    steps(first + whole * UNROLL, jnp.where(count > whole * UNROLL, 1, 0), half)


def typed_spread(table, spread_ref):
    row = lax.broadcasted_iota(jnp.int32, (48, TILE), 0)
    for c in range(3):
        hit = (row % 4 == c) & (row < 12)
        spread_ref[:, c * TILE : (c + 1) * TILE] = jnp.where(hit, 1.0, 0.0).astype(jnp.bfloat16)
    kind = (row % 8).astype(F32)
    rho, scale, neck = looked_up(table, kind, (0, 1, 2))
    for c, value in enumerate((rho, scale * rho * rho * rho, neck)):
        high = value.astype(jnp.bfloat16).astype(F32)
        rest = value - high
        middle = rest.astype(jnp.bfloat16).astype(F32)
        part = jnp.where(row < 24, high, jnp.where(row < 32, middle, rest - middle))
        part = jnp.where((row >= 16) & (row < 40), part, 0.0)
        spread_ref[:, (3 + c) * TILE : (4 + c) * TILE] = part.astype(jnp.bfloat16)


def typed_columns(atoms, spread_ref):
    high = atoms.astype(jnp.bfloat16).astype(F32)
    rest = atoms - high
    middle = rest.astype(jnp.bfloat16).astype(F32)
    kinds = lax.broadcasted_iota(jnp.int32, (8, TILE), 0).astype(F32)
    hot = jnp.where(atoms[3:4, :] == kinds, 1.0, 0.0)
    parts = jnp.concatenate(
        [high, middle, rest - middle, jnp.zeros((4, TILE), F32), hot, hot, hot, jnp.zeros((8, TILE), F32)],
        axis=0,
    )
    spread = lax.dot_general(
        parts.astype(jnp.bfloat16),
        spread_ref[...],
        (((0,), (0,)), ((), ())),
        preferred_element_type=F32,
    )
    return lambda s, c: spread[s : s + CHUNK, c * TILE : (c + 1) * TILE]


def j_atoms(side_j, jb):
    return side_j[jb // HELD, jb % HELD]


def first_kernel(table, joined, new_ref, sent_ref, kept_ref):
    pos, vel, old = joined[0:3], joined[3:6], joined[6:9]
    charge, types, lists = joined[9:10], joined[10:11], joined[11:13, 0:TILE]
    [mass] = looked_up(table, types, (6,))
    new = pos + TIMESTEP * vel + TIMESTEP * TIMESTEP / (2.0 * mass) * old
    scale = TIMESTEP / (2.0 * mass)
    new_ref[...] = new
    kept_ref[0:3] = vel + scale * old
    kept_ref[3:4] = scale
    kept_ref[4:5] = charge
    for n in range(N_REP):
        for b in range(2):
            here = slice(b * TILE, (b + 1) * TILE)
            sent_ref[n, b, 0:3, :] = new[:, here]
            sent_ref[n, b, 3:4, :] = types[:, here]
            sent_ref[n, 2, 2 + b : 3 + b, :] = charge[:, here]
        sent_ref[n, 2, 0:2, :] = lists


def row_kernel(places, side_i, sent_ref):
    rows = [
        jnp.concatenate(
            [
                side_i[4 * half + n, places[0], 2, r : r + 1, 0:SLOTS]
                for n in range(4)
            ],
            axis=1,

        )
        for r in range(2)
        for half in range(2)
    ]
    lists = jnp.concatenate(rows, axis=0)
    for n in range(N_ROWS):
        for b in range(HELD):
            sent_ref[n, b] = side_i[places[2], b // 2, b % 2]
        sent_ref[n, HELD] = lists


def pick_kernel(keys_ref, picked):
    keys = keys_ref[...]
    count = jnp.sum(jnp.where(keys < NO_KEY, 1.0, 0.0)).astype(jnp.int32)

    def step(k, keys):
        least = jnp.min(keys)
        place = least.astype(jnp.int32) >> 12
        picked[k] = (place >> 6) * 256 + (place & 63) * 2
        return jnp.where(keys == least, NO_KEY, keys)

    lax.fori_loop(0, count, step, keys)
    for n in range(UNROLL):
        picked[count + n] = 2 * N_ROWS * 256
    picked[PICKED + UNROLL] = count


def packed(table, pack, count, more):
    types = pack[0:count, 3, :]
    found = looked_up(table, types, (0, 1, 2) + more)
    rho = found[0]
    pack[0:count, 3, :] = rho
    pack[0:count, 4, :] = found[1] * rho * rho * rho
    pack[0:count, 5, :] = found[2]
    return rho, found[3:]


def pack_kernel(
    table, side_i, pack_i, charge_i, more_i, mask_ref, typed_ref, plain_ref, pair_ref
):
    write_mask(mask_ref)
    typed_spread(table, typed_ref)
    write_spread(plain_ref, range(6))
    write_spread(pair_ref, (0, 1, 2, 4, 5, 6))
    for n in range(N_COLS):
        for z in range(N_REP):
            at = n * HELD + 2 * z
            for b in range(2):
                pack_i[at + b, 0:4, :] = side_i[n, z, b]
                pack_i[at + b, 4:8, :] = side_i[n, z, b]
            charge_i[at : at + 2] = side_i[n, z, 2, 2:4, :]
    pack_i[I_BLOCKS] = jnp.ones((8, TILE), F32)
    rho, more = packed(table, pack_i, I_BLOCKS, (3, 4, 5))
    for n, value in enumerate((*more, 1.0 / rho, 1.0 / (rho + OFFSET))):
        more_i[n] = value


def born_kernel(meta, pack_i, side_j, mask_ref, spread_ref, out_ref, acc):
    acc[...] = jnp.zeros_like(acc)

    def one_tile(ia, jb, same):
        col = typed_columns(j_atoms(side_j, jb), spread_ref)
        xi, yi, zi, rho = (pack_i[ia, c : c + 1, :] for c in range(4))
        rho_sq, rho_gap = rho * rho, rho + NECK_GAP
        total = jnp.zeros((8, TILE), F32)
        for s in range(0, TILE, CHUNK):
            _, _, _, q = offsets(xi, yi, zi, col, s)
            base = jnp.maximum(1.0 - q * INV_SQ, 0.0)
            weight = base * base * mask_ref[same, s : s + CHUNK, :]
            inv = 1.0 / (q + rho_sq)
            gap = rho_gap + col(s, 3)
            off = q - gap * gap
            bump = jnp.exp2(off * off * (-LOG2E / NECK_WIDTH))
            total += folded(weight * (col(s, 4) * (inv * inv) + col(s, 5) * bump))

        def add():
            acc[ia] += total

        return add

    for_each_tile(meta, 0, meta[LISTED], one_tile)
    born = jnp.sum(acc[0:I_BLOCKS], axis=1)
    for n in range(N_COLS):
        out_ref[n] = born


def radius_kernel(places, parts, pack_i, more_i, charge, ready, radius_ref, sent_ref, rate_ref):
    born = parts[0]
    for n in range(1, N_COLS):
        born = born + parts[n]
    rho = pack_i[0:I_BLOCKS, 3, :]
    alpha, beta, gamma, inv_rho, inv_offset = (more_i[n] for n in range(5))
    scaled = rho * born
    poly = alpha * scaled - beta * scaled * scaled + gamma * scaled * scaled * scaled
    squash = jnp.tanh(poly)
    radius = 1.0 / (inv_rho - squash * inv_offset)
    slope = alpha - 2.0 * beta * scaled + 3.0 * gamma * scaled * scaled
    rate_ref[...] = radius * radius * (1.0 - squash * squash) * slope * rho * inv_offset
    radius_ref[0:I_BLOCKS] = radius
    radius_ref[I_BLOCKS : I_BLOCKS + 8] = jnp.ones((8, TILE), F32)
    here = pl.ds(pl.multiple_of(places[2] * HELD, HELD), HELD)
    held, charges = radius_ref[here, :], charge[here, :]
    for n in range(N_ROWS):
        sent_ref[n, 0] = held
        sent_ref[n, 1] = charges


def slope_kernel(meta, places, table, pack_i, side_j, spread_ref, out_ref, own_j, force):
    force[...] = jnp.zeros_like(force)
    for n in range(N_ROWS):
        for b in range(2):
            block = side_j[n, places[0] * 2 + b]
            own_j[2 * n + b, 0:4, :] = block
            own_j[2 * n + b, 4:8, :] = block
    own_j[2 * N_ROWS] = jnp.ones((8, TILE), F32)
    packed(table, own_j, 2 * N_ROWS, ())

    def one_tile(ia, jb, same):
        col = typed_columns(j_atoms(side_j, jb), spread_ref)
        xi, yi, zi, rho = (pack_i[ia, c : c + 1, :] for c in range(4))
        rho_sq, rho_gap = rho * rho, rho + NECK_GAP
        sums = [jnp.zeros((8, TILE), F32)] * 3
        for s in range(0, TILE, CHUNK):
            dx, dy, dz, q = offsets(xi, yi, zi, col, s)
            base = jnp.maximum(1.0 - q * INV_SQ, 0.0)
            weight = base * base
            w_slope = (-2.0 * INV_SQ) * base
            gap = rho_gap + col(s, 3)
            off = q - gap * gap
            bump = jnp.exp2(off * off * (-LOG2E / NECK_WIDTH))
            bump = bump * (w_slope - weight * off * (2.0 / NECK_WIDTH))
            inv = 1.0 / (q + rho_sq)
            slope = col(s, 4) * (inv * inv) * (w_slope - 2.0 * weight * inv) + col(s, 5) * bump
            sums = [a + folded(slope * d) for a, d in zip(sums, (dx, dy, dz))]

        def add():
            for c in range(3):
                force[ia, c] += sums[c]

        return add

    for_each_tile(meta, 0, meta[LISTED + 1], one_tile)
    for n in range(N_COLS):
        for b in range(2):
            total = jnp.sum(force[n * HELD + places[0] * 2 + b], axis=1)
            out_ref[n, 3 * b : 3 * b + 3, :] = total
        out_ref[n, 6:8, :] = total[0:2]


def direct_kernel(
    picked, places, own_j, pack_i, rad_j, radius_i, charge_i, spread_ref, out_ref, force, sides, own, own_q
):
    force[...] = jnp.zeros_like(force)
    sides[...] = pack_i[0:I_BLOCKS]
    radii = radius_i[0:I_BLOCKS]
    sides[:, 3, :] = radii
    sides[:, 4, :] = 1.0 / radii
    sides[:, 5, :] = charge_i[...]
    own[...] = jnp.ones_like(own)
    for n in range(N_ROWS):
        own[2 * n : 2 * n + 2] = rad_j[n, 0, pl.ds(places[0] * 2, 2), :]
        own_q[2 * n : 2 * n + 2] = rad_j[n, 1, pl.ds(places[0] * 2, 2), :]

    def one_tile(at, jb, same):
        col = columns(sides[jb], spread_ref)
        xi, yi, zi = (own_j[at, c : c + 1, :] for c in range(3))
        radius = own[pl.ds(at, 1), :]
        quarter = 0.25 / radius
        sums = [jnp.zeros((8, TILE), F32)] * 3
        for s in range(0, TILE, CHUNK):
            dx, dy, dz, q = offsets(xi, yi, zi, col, s)
            base = jnp.maximum(1.0 - q * INV_SQ, 0.0)
            decay = jnp.exp2(q * (quarter * col(s, 4)) * -LOG2E)
            inv = lax.rsqrt(q + radius * col(s, 3) * decay)
            slope = (-2.0 * INV_SQ) * base - base * base * (inv * inv) * (0.5 - 0.125 * decay)
            slope = slope * (inv * col(s, 5))
            sums = [a + folded(slope * d) for a, d in zip(sums, (dx, dy, dz))]

        def add():
            for c in range(3):
                force[at, c] += sums[c]

        return add

    for_each_tile(picked, 0, picked[PICKED + UNROLL], one_tile)
    scale = (2.0 * COULOMB) * own_q[...]
    for c in range(3):
        out_ref[c] = scale * jnp.sum(force[0 : 2 * N_ROWS, c], axis=1)


def pair_kernel(
    meta, pack_i, side_j, rad_i, rad_j, slopes, mask_ref, spread_ref, out_ref, acc
):
    acc[...] = jnp.zeros_like(acc)

    def one_tile(ia, jb, same):
        n, b = jb // HELD, jb % HELD
        radius_j, charge_j = (rad_j[n, k, pl.ds(b, 1), :] for k in range(2))
        col = columns(
            jnp.concatenate(
                [side_j[n, b], radius_j, 1.0 / radius_j, charge_j, charge_j], axis=0
            ),
            spread_ref,
        )
        xi, yi, zi = (pack_i[ia, c : c + 1, :] for c in range(3))
        radius_i = rad_i[pl.ds(ia, 1), :]
        quarter_i = 0.25 / radius_i
        total = jnp.zeros((8, TILE), F32)
        for s in range(0, TILE, CHUNK):
            _, _, _, q = offsets(xi, yi, zi, col, s)
            base = jnp.maximum(1.0 - q * INV_SQ, 0.0)
            weight = base * base * mask_ref[same, s : s + CHUNK, :]
            arg = q * (quarter_i * col(s, 4))
            decay = jnp.exp2(arg * -LOG2E)
            inv = lax.rsqrt(q + radius_i * col(s, 3) * decay)
            weighted = weight * col(s, 5) * (inv * inv * inv)
            total += folded(weighted * col(s, 3) * (decay * (1.0 + arg)))

        def add():
            acc[ia] += total

        return add

    for_each_tile(meta, 0, meta[LISTED], one_tile)
    grads = jnp.sum(acc[0:I_BLOCKS], axis=1)
    for n in range(N_COLS):
        out_ref[n, 0:I_BLOCKS] = grads
        out_ref[n, I_BLOCKS : I_BLOCKS + 8] = slopes[n]


def chain_kernel(
    picked, places, pack_i, own_j, parts, charge, radius, rate, direct, spread_ref, out_ref, own_ref, force, chain_ref
):
    force[...] = jnp.zeros_like(force)
    total = parts[0]
    for n in range(1, N_COLS):
        total = total + parts[n]
    charges, radii = charge[...], radius[0:I_BLOCKS]
    grad = -0.5 * charges * total[0:I_BLOCKS]
    chain = (COULOMB * charges * charges / (2.0 * radii * radii) - COULOMB * grad) * rate[...]
    chain_ref[...] = chain
    own_ref[0:8] = total[I_BLOCKS : I_BLOCKS + 8]
    for b in range(2):
        own_ref[8 + b : 9 + b] = chain_ref[pl.ds(places[2] * HELD + places[0] * 2 + b, 1), :]
    fifth = lax.broadcasted_iota(jnp.int32, (8, TILE), 0) == 4

    def one_tile(at, jb, same):
        col = columns(jnp.where(fifth, chain_ref[pl.ds(jb, 1), :], pack_i[jb]), spread_ref)
        xi, yi, zi, rho, vol, neck = (own_j[at, c : c + 1, :] for c in range(6))
        rho_gap = rho + NECK_GAP
        sums = [jnp.zeros((8, TILE), F32)] * 3
        for s in range(0, TILE, CHUNK):
            dx, dy, dz, q = offsets(xi, yi, zi, col, s)
            base = jnp.maximum(1.0 - q * INV_SQ, 0.0)
            weight = base * base
            w_slope = (-2.0 * INV_SQ) * base
            rho_j = col(s, 3)
            gap = rho_gap + rho_j
            off = q - gap * gap
            bump = jnp.exp2(off * off * (-LOG2E / NECK_WIDTH))
            bump = bump * (w_slope - weight * off * (2.0 / NECK_WIDTH))
            inv = 1.0 / (q + rho_j * rho_j)
            slope = vol * (inv * inv) * (w_slope - 2.0 * weight * inv) + neck * bump
            slope = slope * col(s, 4)
            sums = [a + folded(slope * d) for a, d in zip(sums, (dx, dy, dz))]

        def add():
            for c in range(3):
                force[at, c] += sums[c]

        return add

    for_each_tile(picked, 0, picked[PICKED + UNROLL], one_tile)
    for k in range(3):
        value = direct[k] - 2.0 * jnp.sum(force[0 : 2 * N_ROWS, k], axis=1)
        for n in range(N_ROWS):
            out_ref[n, 2 * k : 2 * k + 2, :] = value[2 * n : 2 * n + 2]
            if k == 2:
                out_ref[n, 6:8, :] = value[2 * n : 2 * n + 2]


def last_kernel(parts, own, kept, vel_ref, force_ref):
    total = parts[0]
    for n in range(1, N_ROWS):
        total = total + parts[n]
    for b in range(2):
        here = slice(b * TILE, (b + 1) * TILE)
        for k in range(3):
            row = slice(k, k + 1)
            force = total[2 * k + b : 2 * k + b + 1] - 2.0 * (
                own[8 + b : 9 + b, :] * own[3 * b + k : 3 * b + k + 1, :]
            )
            force_ref[row, here] = force
            vel_ref[row, here] = kept[row, here] + kept[3:4, here] * force


def transposed_keys(lists, places):
    list_a, list_g = lists[:, 0:2].astype(jnp.int32), lists[:, 2:4].astype(jnp.int32)
    source, half, lane = (lax.broadcasted_iota(jnp.int32, list_a.shape, n) for n in range(3))
    j_col, j_row = half * 4 + lane // SLOTS, list_g // 2
    mine = (list_a >= 0) & (list_a // 2 == places[2]) & (j_row % N_ROWS == places[1])
    place_j = (j_col * N_REP + j_row // N_ROWS) * 2 + list_g % 2
    key = ((source * 2 + list_a % 2) * I_BLOCKS + place_j) * 4096
    key = key + (source * 2 + half) * TILE + lane
    return jnp.where(mine, key.astype(F32), NO_KEY).reshape(2 * N_ROWS, TILE)


def tile_codes(lists, rep_at, row_at, col_at):
    list_a, list_g = lists[:, 0].astype(jnp.int32), lists[:, 1].astype(jnp.int32)
    reps = jnp.arange(N_REP, dtype=jnp.int32)[:, None]
    live = list_a >= 0
    counts = jnp.sum(live.astype(jnp.int32), axis=1)
    j_row = list_g // 2
    place_i = (list_a // 2 * N_REP + reps) * 2 + list_a % 2
    place_j = (j_row % N_ROWS * N_REP + j_row // N_ROWS) * 2 + list_g % 2
    same = (j_row == reps * N_ROWS + row_at) & (list_a == col_at * 2 + list_g % 2)
    none = I_BLOCKS * 256
    codes = place_i * 256 + place_j * 2 + same.astype(jnp.int32) - none
    turn = (reps - rep_at) & (N_REP - 1)
    before = jnp.sum(jnp.where(turn < turn.T, counts[:, None], 0), axis=0)
    target = before[:, None] + jnp.arange(SLOTS, dtype=jnp.int32)[None, :]
    target = jnp.where(live, target, -1).reshape(1, LISTED)
    hit = target == jnp.arange(LISTED, dtype=jnp.int32)[:, None]
    placed = none + jnp.sum(jnp.where(hit, codes.reshape(1, LISTED), 0), axis=1)
    own = jnp.sum(jnp.where(turn[:, 0] == 0, counts, 0))
    return jnp.concatenate([placed, jnp.stack([jnp.sum(counts), own])]).astype(jnp.int32)


def body(positions, velocities, old_forces, charges, atom_types, table, tile_pairs):
    rep_at = lax.axis_index(REP)
    row_at = lax.axis_index(ROWS)
    col_at = lax.axis_index(COLS)
    places = jnp.stack([rep_at, row_at, col_at]).astype(jnp.int32)
    row = (1, 2 * TILE)
    joined = jnp.concatenate(
        [
            positions,
            velocities,
            old_forces,
            charges.reshape(row),
            atom_types.reshape(row).astype(F32),
            jnp.pad(tile_pairs.reshape(2, SLOTS).astype(F32), ((0, 0), (0, 2 * TILE - SLOTS))),
        ],
        axis=0,
    )
    new_positions, sent, kept = called(
        first_kernel,
        [(3, 2 * TILE), (N_REP, 3, 4, TILE), (5, 2 * TILE)],
        [],
        [table],
        [joined],
    )
    held = exchanged(sent, REP)
    meta = tile_codes(held[:, 2, 0:2, 0:SLOTS], rep_at, row_at, col_at)
    side_i = exchanged(jnp.broadcast_to(held, (N_COLS, *held.shape)), COLS)
    [sent] = called(row_kernel, [(N_ROWS, 9, 4, TILE)], [], [places], [side_i])
    side_j = exchanged(sent, ROWS)

    sums = ((I_BLOCKS + 1, 8, TILE), F32)
    forces = ((2 * N_ROWS + 1, 3, 8, TILE), F32)
    bf16 = jnp.bfloat16
    pack_i, charge_i, more_i, mask, typed, plain, paired = called(
        pack_kernel,
        [
            (I_BLOCKS + 1, 8, TILE),
            (I_BLOCKS, TILE),
            (5, I_BLOCKS, TILE),
            (2, TILE, TILE),
            ((48, 6 * TILE), bf16),
            ((32, 6 * TILE), bf16),
            ((32, 6 * TILE), bf16),
        ],
        [],
        [table],
        [side_i],
    )
    [born_parts] = called(
        born_kernel,
        [(N_COLS, I_BLOCKS, TILE)],
        [sums],
        [meta],
        [pack_i, side_j, mask, typed],
    )
    born_parts = exchanged(born_parts, COLS)
    [picked] = called(
        pick_kernel,
        [(PICKED + UNROLL + 1,)],
        [],
        [],
        [transposed_keys(side_j[:, HELD], places)],
        outputs=SMEM,
        kind=jnp.int32,
    )
    radius_i, sent, rate_i = called(
        radius_kernel,
        [(I_BLOCKS + 8, TILE), (N_ROWS, 2, HELD, TILE), (I_BLOCKS, TILE)],
        [],
        [places],
        [born_parts, pack_i, more_i, charge_i, picked],
    )
    rad_j = exchanged(sent, ROWS)
    slopes, own_j = called(
        slope_kernel,
        [(N_COLS, 8, TILE), (2 * N_ROWS + 1, 8, TILE)],
        [((I_BLOCKS + 1, 3, 8, TILE), F32)],
        [meta, places, table],
        [pack_i, side_j, typed],
    )
    [grads] = called(
        pair_kernel,
        [(N_COLS, I_BLOCKS + 8, TILE)],
        [sums],
        [meta],
        [pack_i, side_j, radius_i, rad_j, slopes, mask, paired],
    )
    grads = exchanged(grads, COLS)
    [direct] = called(
        direct_kernel,
        [(3, 2 * N_ROWS, TILE)],
        [
            forces,
            ((I_BLOCKS, 8, TILE), F32),
            ((2 * N_ROWS + 8, TILE), F32),
            ((2 * N_ROWS, TILE), F32),
        ],
        [picked, places],
        [own_j, pack_i, rad_j, radius_i, charge_i, plain],
    )
    parts, own = called(
        chain_kernel,
        [(N_ROWS, 8, TILE), (10, TILE)],
        [forces, ((I_BLOCKS, TILE), F32)],
        [picked, places],
        [pack_i, own_j, grads, charge_i, radius_i, rate_i, direct, plain],
    )
    parts = exchanged(parts, ROWS)
    new_velocities, new_forces = called(
        last_kernel, [(3, 2 * TILE), (3, 2 * TILE)], [], [], [parts, own, kept]
    )
    return (new_positions, new_velocities, new_forces)


def solution(mesh):
    split = Mesh(mesh.devices.reshape(SIZES), AXES)
    rows, cols = AXES[:4], AXES[4:]
    return jax.shard_map(
        body,
        mesh=split,
        in_specs=(
            P(None, AXES),
            P(None, AXES),
            P(None, AXES),
            P(AXES),
            P(AXES),
            P(),
            P(rows, cols, None, None),
        ),
        out_specs=(P(None, AXES), P(None, AXES), P(None, AXES)),
        check_vma=False,
    )
```

```python
import jax
import jax.numpy as jnp
from jax import lax
from jax.experimental import pallas as pl
from jax.experimental.pallas import tpu as pltpu
from jax.sharding import Mesh
from jax.sharding import PartitionSpec as P

TILE = 128
SLOTS = 32
CHUNK = 32
UNROLL = 8
LISTED = 128
PICKED = 2048

CUTOFF = 12.0
COULOMB = 32.0
TIMESTEP = 0.5
OFFSET = 0.09
NECK_GAP = 0.5
NECK_WIDTH = 16.0
INV_SQ = 1.0 / (CUTOFF * CUTOFF)
LOG2E = 1.4426950408889634
NO_KEY = 16777216.0

AXES = ("zh", "zl", "yh", "core", "x", "yl")
SIZES = (4, 4, 2, 2, 4, 2)
REP = ("zh",)
ROWS = ("zl", "yh", "core")
COLS = ("x", "yl")
N_REP, N_ROWS, N_COLS = 4, 16, 8
HELD = 2 * N_REP
I_BLOCKS = N_COLS * HELD
J_BLOCKS = N_ROWS * HELD

VMEM = pl.BlockSpec(memory_space=pltpu.VMEM)
SMEM = pl.BlockSpec(memory_space=pltpu.SMEM)
F32 = jnp.float32


def exchanged(pieces, axes):
    return lax.all_to_all(pieces, axes, 0, 0, tiled=True)


def called(kernel, outs, scratch, smem, vmem, inputs=VMEM, outputs=VMEM, kind=F32):
    return pl.pallas_call(
        kernel,
        out_shape=[
            jax.ShapeDtypeStruct(*s) if isinstance(s[0], tuple) else jax.ShapeDtypeStruct(s, kind)
            for s in outs
        ],
        in_specs=[SMEM] * len(smem) + [inputs] * len(vmem),
        out_specs=[outputs] * len(outs),
        scratch_shapes=[pltpu.VMEM(*s) if isinstance(s, tuple) else s for s in scratch],
        compiler_params=pltpu.CompilerParams(vmem_limit_bytes=32 * 1024 * 1024),
    )(*smem, *vmem)


def looked_up(table, types, rows):
    found = [jnp.zeros(types.shape, F32) for _ in rows]
    for kind in range(8):
        here = types == float(kind)
        found = [jnp.where(here, table[r, kind], f) for r, f in zip(rows, found)]
    return found


def folded(value):
    parts = [value[s : s + 8] for s in range(0, CHUNK, 8)]
    while len(parts) > 1:
        parts = [a + b for a, b in zip(parts[::2], parts[1::2])]
    return parts[0]


def write_mask(mask_ref):
    down = lax.broadcasted_iota(jnp.int32, (TILE, TILE), 0)
    across = lax.broadcasted_iota(jnp.int32, (TILE, TILE), 1)
    mask_ref[0] = jnp.ones((TILE, TILE), F32)
    mask_ref[1] = jnp.where(down == across, 0.0, 1.0)


def write_spread(spread_ref, rows):
    at = lax.broadcasted_iota(jnp.int32, (32, TILE), 0)
    for c, row in enumerate(rows):
        hit = (at % 8 == row) & (at < 24)
        spread_ref[:, c * TILE : (c + 1) * TILE] = jnp.where(hit, 1.0, 0.0).astype(jnp.bfloat16)


def columns(rows, spread_ref):
    high = rows.astype(jnp.bfloat16).astype(F32)
    rest = rows - high
    middle = rest.astype(jnp.bfloat16).astype(F32)
    parts = jnp.concatenate([high, middle, rest - middle, jnp.zeros_like(rows)], axis=0)
    spread = lax.dot_general(
        parts.astype(jnp.bfloat16),
        spread_ref[...],
        (((0,), (0,)), ((), ())),
        preferred_element_type=F32,
    )
    return lambda s, c: spread[s : s + CHUNK, c * TILE : (c + 1) * TILE]


def offsets(xi, yi, zi, col, s):
    dx = xi - col(s, 0)
    dy = yi - col(s, 1)
    dz = zi - col(s, 2)
    return dx, dy, dz, dx * dx + dy * dy + dz * dz


def decoded(code):
    return code >> 8, (code >> 1) & 127, code & 1


def for_each_tile(meta, first, count, one_tile):
    def steps(begin, number, width):
        def step(k, _):
            at = begin + k * width
            for add in [one_tile(*decoded(meta[at + u])) for u in range(width)]:
                add()
            return 0

        lax.fori_loop(0, number, step, 0)

    half = UNROLL // 2
    whole = (count + half - 1) // UNROLL
    steps(first, whole, UNROLL)
    steps(first + whole * UNROLL, jnp.where(count > whole * UNROLL, 1, 0), half)


def typed_spread(table, spread_ref):
    row = lax.broadcasted_iota(jnp.int32, (48, TILE), 0)
    for c in range(3):
        hit = (row % 4 == c) & (row < 12)
        spread_ref[:, c * TILE : (c + 1) * TILE] = jnp.where(hit, 1.0, 0.0).astype(jnp.bfloat16)
    kind = (row % 8).astype(F32)
    rho, scale, neck = looked_up(table, kind, (0, 1, 2))
    for c, value in enumerate((rho, scale * rho * rho * rho, neck)):
        high = value.astype(jnp.bfloat16).astype(F32)
        rest = value - high
        middle = rest.astype(jnp.bfloat16).astype(F32)
        part = jnp.where(row < 24, high, jnp.where(row < 32, middle, rest - middle))
        part = jnp.where((row >= 16) & (row < 40), part, 0.0)
        spread_ref[:, (3 + c) * TILE : (4 + c) * TILE] = part.astype(jnp.bfloat16)


def typed_columns(atoms, spread_ref):
    high = atoms.astype(jnp.bfloat16).astype(F32)
    rest = atoms - high
    middle = rest.astype(jnp.bfloat16).astype(F32)
    kinds = lax.broadcasted_iota(jnp.int32, (8, TILE), 0).astype(F32)
    hot = jnp.where(atoms[3:4, :] == kinds, 1.0, 0.0)
    parts = jnp.concatenate(
        [high, middle, rest - middle, jnp.zeros((4, TILE), F32), hot, hot, hot, jnp.zeros((8, TILE), F32)],
        axis=0,
    )
    spread = lax.dot_general(
        parts.astype(jnp.bfloat16),
        spread_ref[...],
        (((0,), (0,)), ((), ())),
        preferred_element_type=F32,
    )
    return lambda s, c: spread[s : s + CHUNK, c * TILE : (c + 1) * TILE]


def j_atoms(side_j, jb):
    return side_j[jb // HELD, jb % HELD]


def first_kernel(table, joined, new_ref, sent_ref, kept_ref):
    pos, vel, old = joined[0:3], joined[3:6], joined[6:9]
    charge, types, lists = joined[9:10], joined[10:11], joined[11:13, 0:TILE]
    [mass] = looked_up(table, types, (6,))
    new = pos + TIMESTEP * vel + TIMESTEP * TIMESTEP / (2.0 * mass) * old
    scale = TIMESTEP / (2.0 * mass)
    new_ref[...] = new
    kept_ref[0:3] = vel + scale * old
    kept_ref[3:4] = scale
    kept_ref[4:5] = charge
    for n in range(N_REP):
        for b in range(2):
            here = slice(b * TILE, (b + 1) * TILE)
            sent_ref[n, b, 0:3, :] = new[:, here]
            sent_ref[n, b, 3:4, :] = types[:, here]
            sent_ref[n, 2, 2 + b : 3 + b, :] = charge[:, here]
        sent_ref[n, 2, 0:2, :] = lists


def row_kernel(places, side_i, sent_ref):
    rows = [
        jnp.concatenate(
            [
                side_i[4 * half + n, places[0], 2, r : r + 1, 0:SLOTS]
                for n in range(4)
            ],
            axis=1,

        )
        for r in range(2)
        for half in range(2)
    ]
    lists = jnp.concatenate(rows, axis=0)
    for n in range(N_ROWS):
        for b in range(HELD):
            sent_ref[n, b] = side_i[places[2], b // 2, b % 2]
        sent_ref[n, HELD] = lists


def pick_kernel(keys_ref, picked):
    keys = keys_ref[...]
    count = jnp.sum(jnp.where(keys < NO_KEY, 1.0, 0.0)).astype(jnp.int32)

    def step(k, keys):
        least = jnp.min(keys)
        place = least.astype(jnp.int32) >> 12
        picked[k] = (place >> 6) * 256 + (place & 63) * 2
        return jnp.where(keys == least, NO_KEY, keys)

    lax.fori_loop(0, count, step, keys)
    for n in range(UNROLL):
        picked[count + n] = 2 * N_ROWS * 256
    picked[PICKED + UNROLL] = count


def packed(table, pack, count, more):
    types = pack[0:count, 3, :]
    found = looked_up(table, types, (0, 1, 2) + more)
    rho = found[0]
    pack[0:count, 3, :] = rho
    pack[0:count, 4, :] = found[1] * rho * rho * rho
    pack[0:count, 5, :] = found[2]
    return rho, found[3:]


def pack_kernel(
    table, side_i, pack_i, charge_i, more_i, mask_ref, typed_ref, plain_ref, pair_ref
):
    write_mask(mask_ref)
    typed_spread(table, typed_ref)
    write_spread(plain_ref, range(6))
    write_spread(pair_ref, (0, 1, 2, 4, 5, 6))
    for n in range(N_COLS):
        for z in range(N_REP):
            at = n * HELD + 2 * z
            for b in range(2):
                pack_i[at + b, 0:4, :] = side_i[n, z, b]
                pack_i[at + b, 4:8, :] = side_i[n, z, b]
            charge_i[at : at + 2] = side_i[n, z, 2, 2:4, :]
    pack_i[I_BLOCKS] = jnp.ones((8, TILE), F32)
    rho, more = packed(table, pack_i, I_BLOCKS, (3, 4, 5))
    for n, value in enumerate((*more, 1.0 / rho, 1.0 / (rho + OFFSET))):
        more_i[n] = value


def keep_kernel(meta, read, kept):
    def step(k, count):
        code = meta[k]
        kept[count] = code
        return count + read[code >> 8]

    count = lax.fori_loop(0, meta[LISTED], step, 0)
    for n in range(UNROLL):
        kept[count + n] = I_BLOCKS * 256
    kept[LISTED + UNROLL] = count


def born_kernel(meta, pack_i, side_j, mask_ref, spread_ref, out_ref, acc):
    acc[...] = jnp.zeros_like(acc)

    def one_tile(ia, jb, same):
        col = typed_columns(j_atoms(side_j, jb), spread_ref)
        xi, yi, zi, rho = (pack_i[ia, c : c + 1, :] for c in range(4))
        rho_sq, rho_gap = rho * rho, rho + NECK_GAP
        total = jnp.zeros((8, TILE), F32)
        for s in range(0, TILE, CHUNK):
            _, _, _, q = offsets(xi, yi, zi, col, s)
            base = jnp.maximum(1.0 - q * INV_SQ, 0.0)
            weight = base * base * mask_ref[same, s : s + CHUNK, :]
            inv = 1.0 / (q + rho_sq)
            gap = rho_gap + col(s, 3)
            off = q - gap * gap
            bump = jnp.exp2(off * off * (-LOG2E / NECK_WIDTH))
            total += folded(weight * (col(s, 4) * (inv * inv) + col(s, 5) * bump))

        def add():
            acc[ia] += total

        return add

    for_each_tile(meta, 0, meta[LISTED], one_tile)
    born = jnp.sum(acc[0:I_BLOCKS], axis=1)
    for n in range(N_COLS):
        out_ref[n] = born


def radius_kernel(places, parts, pack_i, more_i, charge, ready, ready_too, radius_ref, sent_ref, rate_ref):
    born = parts[0]
    for n in range(1, N_COLS):
        born = born + parts[n]
    rho = pack_i[0:I_BLOCKS, 3, :]
    alpha, beta, gamma, inv_rho, inv_offset = (more_i[n] for n in range(5))
    scaled = rho * born
    poly = alpha * scaled - beta * scaled * scaled + gamma * scaled * scaled * scaled
    squash = jnp.tanh(poly)
    radius = 1.0 / (inv_rho - squash * inv_offset)
    slope = alpha - 2.0 * beta * scaled + 3.0 * gamma * scaled * scaled
    rate_ref[...] = radius * radius * (1.0 - squash * squash) * slope * rho * inv_offset
    radius_ref[0:I_BLOCKS] = radius
    radius_ref[I_BLOCKS : I_BLOCKS + 8] = jnp.ones((8, TILE), F32)
    here = pl.ds(pl.multiple_of(places[2] * HELD, HELD), HELD)
    held, charges = radius_ref[here, :], charge[here, :]
    for n in range(N_ROWS):
        sent_ref[n, 0] = held
        sent_ref[n, 1] = charges


def slope_kernel(meta, places, table, pack_i, side_j, spread_ref, out_ref, own_j, force):
    force[...] = jnp.zeros_like(force)
    for n in range(N_ROWS):
        for b in range(2):
            block = side_j[n, places[0] * 2 + b]
            own_j[2 * n + b, 0:4, :] = block
            own_j[2 * n + b, 4:8, :] = block
    own_j[2 * N_ROWS] = jnp.ones((8, TILE), F32)
    packed(table, own_j, 2 * N_ROWS, ())

    def one_tile(ia, jb, same):
        col = typed_columns(j_atoms(side_j, jb), spread_ref)
        xi, yi, zi, rho = (pack_i[ia, c : c + 1, :] for c in range(4))
        rho_sq, rho_gap = rho * rho, rho + NECK_GAP
        sums = [jnp.zeros((8, TILE), F32)] * 3
        for s in range(0, TILE, CHUNK):
            dx, dy, dz, q = offsets(xi, yi, zi, col, s)
            base = jnp.maximum(1.0 - q * INV_SQ, 0.0)
            weight = base * base
            w_slope = (-2.0 * INV_SQ) * base
            gap = rho_gap + col(s, 3)
            off = q - gap * gap
            bump = jnp.exp2(off * off * (-LOG2E / NECK_WIDTH))
            bump = bump * (w_slope - weight * off * (2.0 / NECK_WIDTH))
            inv = 1.0 / (q + rho_sq)
            slope = col(s, 4) * (inv * inv) * (w_slope - 2.0 * weight * inv) + col(s, 5) * bump
            sums = [a + folded(slope * d) for a, d in zip(sums, (dx, dy, dz))]

        def add():
            for c in range(3):
                force[ia, c] += sums[c]

        return add

    for_each_tile(meta, 0, meta[LISTED + 1], one_tile)
    for n in range(N_COLS):
        for b in range(2):
            total = jnp.sum(force[n * HELD + places[0] * 2 + b], axis=1)
            out_ref[n, 3 * b : 3 * b + 3, :] = total
        out_ref[n, 6:8, :] = total[0:2]


def direct_kernel(
    picked, places, own_j, pack_i, rad_j, radius_i, charge_i, spread_ref, out_ref, force, sides, own, own_q
):
    force[...] = jnp.zeros_like(force)
    sides[...] = pack_i[0:I_BLOCKS]
    radii = radius_i[0:I_BLOCKS]
    sides[:, 3, :] = radii
    sides[:, 4, :] = 1.0 / radii
    sides[:, 5, :] = charge_i[...]
    own[...] = jnp.ones_like(own)
    for n in range(N_ROWS):
        own[2 * n : 2 * n + 2] = rad_j[n, 0, pl.ds(places[0] * 2, 2), :]
        own_q[2 * n : 2 * n + 2] = rad_j[n, 1, pl.ds(places[0] * 2, 2), :]

    def one_tile(at, jb, same):
        col = columns(sides[jb], spread_ref)
        xi, yi, zi = (own_j[at, c : c + 1, :] for c in range(3))
        radius = own[pl.ds(at, 1), :]
        quarter = 0.25 / radius
        sums = [jnp.zeros((8, TILE), F32)] * 3
        for s in range(0, TILE, CHUNK):
            dx, dy, dz, q = offsets(xi, yi, zi, col, s)
            base = jnp.maximum(1.0 - q * INV_SQ, 0.0)
            decay = jnp.exp2(q * (quarter * col(s, 4)) * -LOG2E)
            inv = lax.rsqrt(q + radius * col(s, 3) * decay)
            slope = (-2.0 * INV_SQ) * base - base * base * (inv * inv) * (0.5 - 0.125 * decay)
            slope = slope * (inv * col(s, 5))
            sums = [a + folded(slope * d) for a, d in zip(sums, (dx, dy, dz))]

        def add():
            for c in range(3):
                force[at, c] += sums[c]

        return add

    for_each_tile(picked, 0, picked[PICKED + UNROLL], one_tile)
    scale = (2.0 * COULOMB) * own_q[...]
    for c in range(3):
        out_ref[c] = scale * jnp.sum(force[0 : 2 * N_ROWS, c], axis=1)


def pair_kernel(
    meta, pack_i, side_j, rad_i, rad_j, slopes, mask_ref, spread_ref, out_ref, acc
):
    acc[...] = jnp.zeros_like(acc)

    def one_tile(ia, jb, same):
        n, b = jb // HELD, jb % HELD
        radius_j, charge_j = (rad_j[n, k, pl.ds(b, 1), :] for k in range(2))
        col = columns(
            jnp.concatenate(
                [side_j[n, b], radius_j, 1.0 / radius_j, charge_j, charge_j], axis=0
            ),
            spread_ref,
        )
        xi, yi, zi = (pack_i[ia, c : c + 1, :] for c in range(3))
        radius_i = rad_i[pl.ds(ia, 1), :]
        quarter_i = 0.25 / radius_i
        total = jnp.zeros((8, TILE), F32)
        for s in range(0, TILE, CHUNK):
            _, _, _, q = offsets(xi, yi, zi, col, s)
            base = jnp.maximum(1.0 - q * INV_SQ, 0.0)
            weight = base * base * mask_ref[same, s : s + CHUNK, :]
            arg = q * (quarter_i * col(s, 4))
            decay = jnp.exp2(arg * -LOG2E)
            inv = lax.rsqrt(q + radius_i * col(s, 3) * decay)
            weighted = weight * col(s, 5) * (inv * inv * inv)
            total += folded(weighted * col(s, 3) * (decay * (1.0 + arg)))

        def add():
            acc[ia] += total

        return add

    for_each_tile(meta, 0, meta[LISTED + UNROLL], one_tile)
    grads = jnp.sum(acc[0:I_BLOCKS], axis=1)
    for n in range(N_COLS):
        out_ref[n, 0:I_BLOCKS] = grads
        out_ref[n, I_BLOCKS : I_BLOCKS + 8] = slopes[n]


def chain_kernel(
    picked, places, pack_i, own_j, parts, charge, radius, rate, direct, spread_ref, out_ref, own_ref, force, chain_ref
):
    force[...] = jnp.zeros_like(force)
    total = parts[0]
    for n in range(1, N_COLS):
        total = total + parts[n]
    charges, radii = charge[...], radius[0:I_BLOCKS]
    grad = -0.5 * charges * total[0:I_BLOCKS]
    chain = (COULOMB * charges * charges / (2.0 * radii * radii) - COULOMB * grad) * rate[...]
    chain_ref[...] = chain
    own_ref[0:8] = total[I_BLOCKS : I_BLOCKS + 8]
    for b in range(2):
        own_ref[8 + b : 9 + b] = chain_ref[pl.ds(places[2] * HELD + places[0] * 2 + b, 1), :]
    fifth = lax.broadcasted_iota(jnp.int32, (8, TILE), 0) == 4

    def one_tile(at, jb, same):
        col = columns(jnp.where(fifth, chain_ref[pl.ds(jb, 1), :], pack_i[jb]), spread_ref)
        xi, yi, zi, rho, vol, neck = (own_j[at, c : c + 1, :] for c in range(6))
        rho_gap = rho + NECK_GAP
        sums = [jnp.zeros((8, TILE), F32)] * 3
        for s in range(0, TILE, CHUNK):
            dx, dy, dz, q = offsets(xi, yi, zi, col, s)
            base = jnp.maximum(1.0 - q * INV_SQ, 0.0)
            weight = base * base
            w_slope = (-2.0 * INV_SQ) * base
            rho_j = col(s, 3)
            gap = rho_gap + rho_j
            off = q - gap * gap
            bump = jnp.exp2(off * off * (-LOG2E / NECK_WIDTH))
            bump = bump * (w_slope - weight * off * (2.0 / NECK_WIDTH))
            inv = 1.0 / (q + rho_j * rho_j)
            slope = vol * (inv * inv) * (w_slope - 2.0 * weight * inv) + neck * bump
            slope = slope * col(s, 4)
            sums = [a + folded(slope * d) for a, d in zip(sums, (dx, dy, dz))]

        def add():
            for c in range(3):
                force[at, c] += sums[c]

        return add

    for_each_tile(picked, 0, picked[PICKED + UNROLL], one_tile)
    for k in range(3):
        value = direct[k] - 2.0 * jnp.sum(force[0 : 2 * N_ROWS, k], axis=1)
        for n in range(N_ROWS):
            out_ref[n, 2 * k : 2 * k + 2, :] = value[2 * n : 2 * n + 2]
            if k == 2:
                out_ref[n, 6:8, :] = value[2 * n : 2 * n + 2]


def last_kernel(parts, own, kept, vel_ref, force_ref):
    total = parts[0]
    for n in range(1, N_ROWS):
        total = total + parts[n]
    for b in range(2):
        here = slice(b * TILE, (b + 1) * TILE)
        for k in range(3):
            row = slice(k, k + 1)
            force = total[2 * k + b : 2 * k + b + 1] - 2.0 * (
                own[8 + b : 9 + b, :] * own[3 * b + k : 3 * b + k + 1, :]
            )
            force_ref[row, here] = force
            vel_ref[row, here] = kept[row, here] + kept[3:4, here] * force


def transposed_keys(lists, places):
    list_a, list_g = lists[:, 0:2].astype(jnp.int32), lists[:, 2:4].astype(jnp.int32)
    source, half, lane = (lax.broadcasted_iota(jnp.int32, list_a.shape, n) for n in range(3))
    j_col, j_row = half * 4 + lane // SLOTS, list_g // 2
    known = (list_a >= 0) & (j_row % N_ROWS == places[1])
    place_j = (j_col * N_REP + j_row // N_ROWS) * 2 + list_g % 2
    key = ((source * 2 + list_a % 2) * I_BLOCKS + place_j) * 4096
    key = key + (source * 2 + half) * TILE + lane
    keys = jnp.where(known & (list_a // 2 == places[2]), key.astype(F32), NO_KEY)
    named = jnp.where(known, place_j, -1).reshape(1, 2 * N_ROWS, TILE)
    blocks = jnp.arange(I_BLOCKS, dtype=jnp.int32)
    read = jnp.any(named == blocks[:, None, None], axis=(1, 2)) | (blocks // 2 % N_REP == places[0])
    return keys.reshape(2 * N_ROWS, TILE), read.astype(jnp.int32)


def tile_codes(lists, rep_at, row_at, col_at):
    list_a, list_g = lists[:, 0].astype(jnp.int32), lists[:, 1].astype(jnp.int32)
    reps = jnp.arange(N_REP, dtype=jnp.int32)[:, None]
    live = list_a >= 0
    counts = jnp.sum(live.astype(jnp.int32), axis=1)
    j_row = list_g // 2
    place_i = (list_a // 2 * N_REP + reps) * 2 + list_a % 2
    place_j = (j_row % N_ROWS * N_REP + j_row // N_ROWS) * 2 + list_g % 2
    same = (j_row == reps * N_ROWS + row_at) & (list_a == col_at * 2 + list_g % 2)
    none = I_BLOCKS * 256
    codes = place_i * 256 + place_j * 2 + same.astype(jnp.int32) - none
    turn = (reps - rep_at) & (N_REP - 1)
    before = jnp.sum(jnp.where(turn < turn.T, counts[:, None], 0), axis=0)
    target = before[:, None] + jnp.arange(SLOTS, dtype=jnp.int32)[None, :]
    target = jnp.where(live, target, -1).reshape(1, LISTED)
    hit = target == jnp.arange(LISTED, dtype=jnp.int32)[:, None]
    placed = none + jnp.sum(jnp.where(hit, codes.reshape(1, LISTED), 0), axis=1)
    own = jnp.sum(jnp.where(turn[:, 0] == 0, counts, 0))
    return jnp.concatenate([placed, jnp.stack([jnp.sum(counts), own])]).astype(jnp.int32)


def body(positions, velocities, old_forces, charges, atom_types, table, tile_pairs):
    rep_at = lax.axis_index(REP)
    row_at = lax.axis_index(ROWS)
    col_at = lax.axis_index(COLS)
    places = jnp.stack([rep_at, row_at, col_at]).astype(jnp.int32)
    row = (1, 2 * TILE)
    joined = jnp.concatenate(
        [
            positions,
            velocities,
            old_forces,
            charges.reshape(row),
            atom_types.reshape(row).astype(F32),
            jnp.pad(tile_pairs.reshape(2, SLOTS).astype(F32), ((0, 0), (0, 2 * TILE - SLOTS))),
        ],
        axis=0,
    )
    new_positions, sent, kept = called(
        first_kernel,
        [(3, 2 * TILE), (N_REP, 3, 4, TILE), (5, 2 * TILE)],
        [],
        [table],
        [joined],
    )
    held = exchanged(sent, REP)
    meta = tile_codes(held[:, 2, 0:2, 0:SLOTS], rep_at, row_at, col_at)
    side_i = exchanged(jnp.broadcast_to(held, (N_COLS, *held.shape)), COLS)
    [sent] = called(row_kernel, [(N_ROWS, 9, 4, TILE)], [], [places], [side_i])
    side_j = exchanged(sent, ROWS)

    sums = ((I_BLOCKS + 1, 8, TILE), F32)
    forces = ((2 * N_ROWS + 1, 3, 8, TILE), F32)
    bf16 = jnp.bfloat16
    pack_i, charge_i, more_i, mask, typed, plain, paired = called(
        pack_kernel,
        [
            (I_BLOCKS + 1, 8, TILE),
            (I_BLOCKS, TILE),
            (5, I_BLOCKS, TILE),
            (2, TILE, TILE),
            ((48, 6 * TILE), bf16),
            ((32, 6 * TILE), bf16),
            ((32, 6 * TILE), bf16),
        ],
        [],
        [table],
        [side_i],
    )
    [born_parts] = called(
        born_kernel,
        [(N_COLS, I_BLOCKS, TILE)],
        [sums],
        [meta],
        [pack_i, side_j, mask, typed],
    )
    born_parts = exchanged(born_parts, COLS)
    keys, read = transposed_keys(side_j[:, HELD], places)
    [kept_tiles] = called(
        keep_kernel, [(LISTED + UNROLL + 1,)], [], [meta, read], [], outputs=SMEM, kind=jnp.int32
    )
    [picked] = called(
        pick_kernel,
        [(PICKED + UNROLL + 1,)],
        [],
        [],
        [keys],
        outputs=SMEM,
        kind=jnp.int32,
    )
    radius_i, sent, rate_i = called(
        radius_kernel,
        [(I_BLOCKS + 8, TILE), (N_ROWS, 2, HELD, TILE), (I_BLOCKS, TILE)],
        [],
        [places],
        [born_parts, pack_i, more_i, charge_i, picked, kept_tiles],
    )
    rad_j = exchanged(sent, ROWS)
    slopes, own_j = called(
        slope_kernel,
        [(N_COLS, 8, TILE), (2 * N_ROWS + 1, 8, TILE)],
        [((I_BLOCKS + 1, 3, 8, TILE), F32)],
        [meta, places, table],
        [pack_i, side_j, typed],
    )
    [grads] = called(
        pair_kernel,
        [(N_COLS, I_BLOCKS + 8, TILE)],
        [sums],
        [kept_tiles],
        [pack_i, side_j, radius_i, rad_j, slopes, mask, paired],
    )
    grads = exchanged(grads, COLS)
    [direct] = called(
        direct_kernel,
        [(3, 2 * N_ROWS, TILE)],
        [
            forces,
            ((I_BLOCKS, 8, TILE), F32),
            ((2 * N_ROWS + 8, TILE), F32),
            ((2 * N_ROWS, TILE), F32),
        ],
        [picked, places],
        [own_j, pack_i, rad_j, radius_i, charge_i, plain],
    )
    parts, own = called(
        chain_kernel,
        [(N_ROWS, 8, TILE), (10, TILE)],
        [forces, ((I_BLOCKS, TILE), F32)],
        [picked, places],
        [pack_i, own_j, grads, charge_i, radius_i, rate_i, direct, plain],
    )
    parts = exchanged(parts, ROWS)
    new_velocities, new_forces = called(
        last_kernel, [(3, 2 * TILE), (3, 2 * TILE)], [], [], [parts, own, kept]
    )
    return (new_positions, new_velocities, new_forces)


def solution(mesh):
    split = Mesh(mesh.devices.reshape(SIZES), AXES)
    rows, cols = AXES[:4], AXES[4:]
    return jax.shard_map(
        body,
        mesh=split,
        in_specs=(
            P(None, AXES),
            P(None, AXES),
            P(None, AXES),
            P(AXES),
            P(AXES),
            P(),
            P(rows, cols, None, None),
        ),
        out_specs=(P(None, AXES), P(None, AXES), P(None, AXES)),
        check_vma=False,
    )
```

```python
import jax
import jax.numpy as jnp
from jax import lax
from jax.experimental import pallas as pl
from jax.experimental.pallas import tpu as pltpu
from jax.sharding import Mesh
from jax.sharding import PartitionSpec as P

TILE = 128
SLOTS = 32
CHUNK = 32
UNROLL = 8
LISTED = 128
PICKED = 2048

CUTOFF = 12.0
COULOMB = 32.0
TIMESTEP = 0.5
OFFSET = 0.09
NECK_GAP = 0.5
NECK_WIDTH = 16.0
CUT_SQ = CUTOFF * CUTOFF
TAPER = 1.0 / (CUT_SQ * CUT_SQ)
LOG2E = 1.4426950408889634
NO_KEY = 16777216.0

AXES = ("zh", "zl", "yh", "core", "x", "yl")
SIZES = (4, 4, 2, 2, 4, 2)
REP = ("zh",)
ROWS = ("zl", "yh", "core")
COLS = ("x", "yl")
N_REP, N_ROWS, N_COLS = 4, 16, 8
HELD = 2 * N_REP
I_BLOCKS = N_COLS * HELD
J_BLOCKS = N_ROWS * HELD

VMEM = pl.BlockSpec(memory_space=pltpu.VMEM)
SMEM = pl.BlockSpec(memory_space=pltpu.SMEM)
F32 = jnp.float32


def exchanged(pieces, axes):
    return lax.all_to_all(pieces, axes, 0, 0, tiled=True)


def called(kernel, outs, scratch, smem, vmem, inputs=VMEM, outputs=VMEM, kind=F32):
    return pl.pallas_call(
        kernel,
        out_shape=[
            jax.ShapeDtypeStruct(*s) if isinstance(s[0], tuple) else jax.ShapeDtypeStruct(s, kind)
            for s in outs
        ],
        in_specs=[SMEM] * len(smem) + [inputs] * len(vmem),
        out_specs=[outputs] * len(outs),
        scratch_shapes=[pltpu.VMEM(*s) if isinstance(s, tuple) else s for s in scratch],
        compiler_params=pltpu.CompilerParams(vmem_limit_bytes=32 * 1024 * 1024),
    )(*smem, *vmem)


def looked_up(table, types, rows):
    found = [jnp.zeros(types.shape, F32) for _ in rows]
    for kind in range(8):
        here = types == float(kind)
        found = [jnp.where(here, table[r, kind], f) for r, f in zip(rows, found)]
    return found


def folded(value):
    parts = [value[s : s + 8] for s in range(0, CHUNK, 8)]
    while len(parts) > 1:
        parts = [a + b for a, b in zip(parts[::2], parts[1::2])]
    return parts[0]


def write_mask(mask_ref):
    down = lax.broadcasted_iota(jnp.int32, (TILE, TILE), 0)
    across = lax.broadcasted_iota(jnp.int32, (TILE, TILE), 1)
    mask_ref[0] = jnp.ones((TILE, TILE), F32)
    mask_ref[1] = jnp.where(down == across, 0.0, 1.0)


def write_spread(spread_ref, rows):
    at = lax.broadcasted_iota(jnp.int32, (32, TILE), 0)
    for c, row in enumerate(rows):
        hit = (at % 8 == row) & (at < 24)
        spread_ref[:, c * TILE : (c + 1) * TILE] = jnp.where(hit, 1.0, 0.0).astype(jnp.bfloat16)


def columns(rows, spread_ref):
    high = rows.astype(jnp.bfloat16).astype(F32)
    rest = rows - high
    middle = rest.astype(jnp.bfloat16).astype(F32)
    parts = jnp.concatenate([high, middle, rest - middle, jnp.zeros_like(rows)], axis=0)
    spread = lax.dot_general(
        parts.astype(jnp.bfloat16),
        spread_ref[...],
        (((0,), (0,)), ((), ())),
        preferred_element_type=F32,
    )
    return lambda s, c: spread[s : s + CHUNK, c * TILE : (c + 1) * TILE]


def offsets(xi, yi, zi, col, s):
    dx = xi - col(s, 0)
    dy = yi - col(s, 1)
    dz = zi - col(s, 2)
    return dx, dy, dz, dx * dx + dy * dy + dz * dz


def decoded(code):
    return code >> 8, (code >> 1) & 127, code & 1


def for_each_tile(meta, first, count, one_tile):
    def steps(begin, number, width):
        def step(k, _):
            at = begin + k * width
            for add in [one_tile(*decoded(meta[at + u])) for u in range(width)]:
                add()
            return 0

        lax.fori_loop(0, number, step, 0)

    half = UNROLL // 2
    whole = (count + half - 1) // UNROLL
    steps(first, whole, UNROLL)
    steps(first + whole * UNROLL, jnp.where(count > whole * UNROLL, 1, 0), half)


def typed_spread(table, spread_ref):
    row = lax.broadcasted_iota(jnp.int32, (48, TILE), 0)
    for c in range(3):
        hit = (row % 4 == c) & (row < 12)
        spread_ref[:, c * TILE : (c + 1) * TILE] = jnp.where(hit, 1.0, 0.0).astype(jnp.bfloat16)
    kind = (row % 8).astype(F32)
    rho, scale, neck = looked_up(table, kind, (0, 1, 2))
    for c, value in enumerate((rho, scale * rho * rho * rho, neck)):
        high = value.astype(jnp.bfloat16).astype(F32)
        rest = value - high
        middle = rest.astype(jnp.bfloat16).astype(F32)
        part = jnp.where(row < 24, high, jnp.where(row < 32, middle, rest - middle))
        part = jnp.where((row >= 16) & (row < 40), part, 0.0)
        spread_ref[:, (3 + c) * TILE : (4 + c) * TILE] = part.astype(jnp.bfloat16)


def typed_columns(atoms, spread_ref):
    high = atoms.astype(jnp.bfloat16).astype(F32)
    rest = atoms - high
    middle = rest.astype(jnp.bfloat16).astype(F32)
    kinds = lax.broadcasted_iota(jnp.int32, (8, TILE), 0).astype(F32)
    hot = jnp.where(atoms[3:4, :] == kinds, 1.0, 0.0)
    parts = jnp.concatenate(
        [high, middle, rest - middle, jnp.zeros((4, TILE), F32), hot, hot, hot, jnp.zeros((8, TILE), F32)],
        axis=0,
    )
    spread = lax.dot_general(
        parts.astype(jnp.bfloat16),
        spread_ref[...],
        (((0,), (0,)), ((), ())),
        preferred_element_type=F32,
    )
    return lambda s, c: spread[s : s + CHUNK, c * TILE : (c + 1) * TILE]


def j_atoms(side_j, jb):
    return side_j[jb // HELD, jb % HELD]


def first_kernel(table, joined, new_ref, sent_ref, kept_ref):
    pos, vel, old = joined[0:3], joined[3:6], joined[6:9]
    charge, types, lists = joined[9:10], joined[10:11], joined[11:13, 0:TILE]
    [mass] = looked_up(table, types, (6,))
    new = pos + TIMESTEP * vel + TIMESTEP * TIMESTEP / (2.0 * mass) * old
    scale = TIMESTEP / (2.0 * mass)
    new_ref[...] = new
    kept_ref[0:3] = vel + scale * old
    kept_ref[3:4] = scale
    kept_ref[4:5] = charge
    for n in range(N_REP):
        for b in range(2):
            here = slice(b * TILE, (b + 1) * TILE)
            sent_ref[n, b, 0:3, :] = new[:, here]
            sent_ref[n, b, 3:4, :] = types[:, here]
            sent_ref[n, 2, 2 + b : 3 + b, :] = charge[:, here]
        sent_ref[n, 2, 0:2, :] = lists


def row_kernel(places, side_i, sent_ref):
    rows = [
        jnp.concatenate(
            [
                side_i[4 * half + n, places[0], 2, r : r + 1, 0:SLOTS]
                for n in range(4)
            ],
            axis=1,

        )
        for r in range(2)
        for half in range(2)
    ]
    lists = jnp.concatenate(rows, axis=0)
    for n in range(N_ROWS):
        for b in range(HELD):
            sent_ref[n, b] = side_i[places[2], b // 2, b % 2]
        sent_ref[n, HELD] = lists


def pick_kernel(keys_ref, picked):
    keys = keys_ref[...]
    count = jnp.sum(jnp.where(keys < NO_KEY, 1.0, 0.0)).astype(jnp.int32)

    def step(k, keys):
        least = jnp.min(keys)
        place = least.astype(jnp.int32) >> 12
        picked[k] = (place >> 6) * 256 + (place & 63) * 2
        return jnp.where(keys == least, NO_KEY, keys)

    lax.fori_loop(0, count, step, keys)
    for n in range(UNROLL):
        picked[count + n] = 2 * N_ROWS * 256
    picked[PICKED + UNROLL] = count


def packed(table, pack, count, more):
    types = pack[0:count, 3, :]
    found = looked_up(table, types, (0, 1, 2) + more)
    rho = found[0]
    pack[0:count, 3, :] = rho
    pack[0:count, 4, :] = found[1] * rho * rho * rho
    pack[0:count, 5, :] = found[2]
    return rho, found[3:]


def pack_kernel(
    table, side_i, pack_i, charge_i, more_i, mask_ref, typed_ref, plain_ref, pair_ref
):
    write_mask(mask_ref)
    typed_spread(table, typed_ref)
    write_spread(plain_ref, range(6))
    write_spread(pair_ref, (0, 1, 2, 4, 5, 6))
    for n in range(N_COLS):
        for z in range(N_REP):
            at = n * HELD + 2 * z
            for b in range(2):
                pack_i[at + b, 0:4, :] = side_i[n, z, b]
                pack_i[at + b, 4:8, :] = side_i[n, z, b]
            charge_i[at : at + 2] = side_i[n, z, 2, 2:4, :]
    pack_i[I_BLOCKS] = jnp.ones((8, TILE), F32)
    rho, more = packed(table, pack_i, I_BLOCKS, (3, 4, 5))
    for n, value in enumerate((*more, 1.0 / rho, 1.0 / (rho + OFFSET))):
        more_i[n] = value


def keep_kernel(meta, read, kept):
    def step(k, count):
        code = meta[k]
        kept[count] = code
        return count + read[code >> 8]

    count = lax.fori_loop(0, meta[LISTED], step, 0)
    for n in range(UNROLL):
        kept[count + n] = I_BLOCKS * 256
    kept[LISTED + UNROLL] = count


def born_kernel(meta, pack_i, side_j, mask_ref, spread_ref, out_ref, acc):
    acc[...] = jnp.zeros_like(acc)

    def one_tile(ia, jb, same):
        col = typed_columns(j_atoms(side_j, jb), spread_ref)
        xi, yi, zi, rho = (pack_i[ia, c : c + 1, :] for c in range(4))
        rho_sq, rho_gap = rho * rho, rho + NECK_GAP
        total = jnp.zeros((8, TILE), F32)
        for s in range(0, TILE, CHUNK):
            _, _, _, q = offsets(xi, yi, zi, col, s)
            base = jnp.maximum(CUT_SQ - q, 0.0)
            weight = base * base * mask_ref[same, s : s + CHUNK, :]
            inv = 1.0 / (q + rho_sq)
            gap = rho_gap + col(s, 3)
            off = q - gap * gap
            bump = jnp.exp2(off * off * (-LOG2E / NECK_WIDTH))
            total += folded(weight * (col(s, 4) * (inv * inv) + col(s, 5) * bump))

        def add():
            acc[ia] += total

        return add

    for_each_tile(meta, 0, meta[LISTED], one_tile)
    born = TAPER * jnp.sum(acc[0:I_BLOCKS], axis=1)
    for n in range(N_COLS):
        out_ref[n] = born


def radius_kernel(places, parts, pack_i, more_i, charge, ready, radius_ref, sent_ref, rate_ref):
    born = parts[0]
    for n in range(1, N_COLS):
        born = born + parts[n]
    rho = pack_i[0:I_BLOCKS, 3, :]
    alpha, beta, gamma, inv_rho, inv_offset = (more_i[n] for n in range(5))
    scaled = rho * born
    poly = alpha * scaled - beta * scaled * scaled + gamma * scaled * scaled * scaled
    squash = jnp.tanh(poly)
    radius = 1.0 / (inv_rho - squash * inv_offset)
    slope = alpha - 2.0 * beta * scaled + 3.0 * gamma * scaled * scaled
    rate_ref[...] = radius * radius * (1.0 - squash * squash) * slope * rho * inv_offset
    radius_ref[0:I_BLOCKS] = radius
    radius_ref[I_BLOCKS : I_BLOCKS + 8] = jnp.ones((8, TILE), F32)
    here = pl.ds(pl.multiple_of(places[2] * HELD, HELD), HELD)
    held, charges = radius_ref[here, :], charge[here, :]
    for n in range(N_ROWS):
        sent_ref[n, 0] = held
        sent_ref[n, 1] = charges


def slope_kernel(meta, places, table, pack_i, side_j, spread_ref, out_ref, own_j, force):
    force[...] = jnp.zeros_like(force)
    for n in range(N_ROWS):
        for b in range(2):
            block = side_j[n, places[0] * 2 + b]
            own_j[2 * n + b, 0:4, :] = block
            own_j[2 * n + b, 4:8, :] = block
    own_j[2 * N_ROWS] = jnp.ones((8, TILE), F32)
    packed(table, own_j, 2 * N_ROWS, ())

    def one_tile(ia, jb, same):
        col = typed_columns(j_atoms(side_j, jb), spread_ref)
        xi, yi, zi, rho = (pack_i[ia, c : c + 1, :] for c in range(4))
        rho_sq, rho_gap = rho * rho, rho + NECK_GAP
        sums = [jnp.zeros((8, TILE), F32)] * 3
        for s in range(0, TILE, CHUNK):
            dx, dy, dz, q = offsets(xi, yi, zi, col, s)
            base = jnp.maximum(CUT_SQ - q, 0.0)
            gap = rho_gap + col(s, 3)
            off = q - gap * gap
            bump = jnp.exp2(off * off * (-LOG2E / NECK_WIDTH))
            bump = bump * (2.0 + base * off * (2.0 / NECK_WIDTH))
            inv = 1.0 / (q + rho_sq)
            slope = col(s, 4) * (inv * inv) * (2.0 + (base + base) * inv) + col(s, 5) * bump
            slope = slope * base
            sums = [a + folded(slope * d) for a, d in zip(sums, (dx, dy, dz))]

        def add():
            for c in range(3):
                force[ia, c] += sums[c]

        return add

    for_each_tile(meta, 0, meta[LISTED + 1], one_tile)
    for n in range(N_COLS):
        for b in range(2):
            total = jnp.sum(force[n * HELD + places[0] * 2 + b], axis=1)
            total = -TAPER * total
            out_ref[n, 3 * b : 3 * b + 3, :] = total
        out_ref[n, 6:8, :] = total[0:2]


def direct_kernel(
    picked, places, own_j, pack_i, rad_j, radius_i, charge_i, spread_ref, out_ref, force, sides, own, own_q
):
    force[...] = jnp.zeros_like(force)
    sides[...] = pack_i[0:I_BLOCKS]
    radii = radius_i[0:I_BLOCKS]
    sides[:, 3, :] = radii
    sides[:, 4, :] = 1.0 / radii
    sides[:, 5, :] = charge_i[...]
    own[...] = jnp.ones_like(own)
    for n in range(N_ROWS):
        own[2 * n : 2 * n + 2] = rad_j[n, 0, pl.ds(places[0] * 2, 2), :]
        own_q[2 * n : 2 * n + 2] = rad_j[n, 1, pl.ds(places[0] * 2, 2), :]

    def one_tile(at, jb, same):
        col = columns(sides[jb], spread_ref)
        xi, yi, zi = (own_j[at, c : c + 1, :] for c in range(3))
        radius = own[pl.ds(at, 1), :]
        quarter = 0.25 / radius
        sums = [jnp.zeros((8, TILE), F32)] * 3
        for s in range(0, TILE, CHUNK):
            dx, dy, dz, q = offsets(xi, yi, zi, col, s)
            base = jnp.maximum(CUT_SQ - q, 0.0)
            decay = jnp.exp2(q * (quarter * col(s, 4)) * -LOG2E)
            inv = lax.rsqrt(q + radius * col(s, 3) * decay)
            slope = 2.0 + base * (inv * inv) * (0.5 - 0.125 * decay)
            slope = slope * (base * (inv * col(s, 5)))
            sums = [a + folded(slope * d) for a, d in zip(sums, (dx, dy, dz))]

        def add():
            for c in range(3):
                force[at, c] += sums[c]

        return add

    for_each_tile(picked, 0, picked[PICKED + UNROLL], one_tile)
    scale = (-2.0 * COULOMB * TAPER) * own_q[...]
    for c in range(3):
        out_ref[c] = scale * jnp.sum(force[0 : 2 * N_ROWS, c], axis=1)


def pair_kernel(
    meta, pack_i, side_j, rad_i, rad_j, slopes, ready, mask_ref, spread_ref, out_ref, acc
):
    acc[...] = jnp.zeros_like(acc)

    def one_tile(ia, jb, same):
        n, b = jb // HELD, jb % HELD
        radius_j, charge_j = (rad_j[n, k, pl.ds(b, 1), :] for k in range(2))
        col = columns(
            jnp.concatenate(
                [side_j[n, b], radius_j, 1.0 / radius_j, charge_j, charge_j], axis=0
            ),
            spread_ref,
        )
        xi, yi, zi = (pack_i[ia, c : c + 1, :] for c in range(3))
        radius_i = rad_i[pl.ds(ia, 1), :]
        quarter_i = 0.25 / radius_i
        total = jnp.zeros((8, TILE), F32)
        for s in range(0, TILE, CHUNK):
            _, _, _, q = offsets(xi, yi, zi, col, s)
            base = jnp.maximum(CUT_SQ - q, 0.0)
            weight = base * base * mask_ref[same, s : s + CHUNK, :]
            arg = q * (quarter_i * col(s, 4))
            decay = jnp.exp2(arg * -LOG2E)
            inv = lax.rsqrt(q + radius_i * col(s, 3) * decay)
            weighted = weight * col(s, 5) * (inv * inv * inv)
            total += folded(weighted * col(s, 3) * (decay * (1.0 + arg)))

        def add():
            acc[ia] += total

        return add

    for_each_tile(meta, 0, meta[LISTED + UNROLL], one_tile)
    grads = TAPER * jnp.sum(acc[0:I_BLOCKS], axis=1)
    for n in range(N_COLS):
        out_ref[n, 0:I_BLOCKS] = grads
        out_ref[n, I_BLOCKS : I_BLOCKS + 8] = slopes[n]


def chain_kernel(
    picked, places, pack_i, own_j, parts, charge, radius, rate, direct, spread_ref, out_ref, own_ref, force, chain_ref
):
    force[...] = jnp.zeros_like(force)
    total = parts[0]
    for n in range(1, N_COLS):
        total = total + parts[n]
    charges, radii = charge[...], radius[0:I_BLOCKS]
    grad = -0.5 * charges * total[0:I_BLOCKS]
    chain = (COULOMB * charges * charges / (2.0 * radii * radii) - COULOMB * grad) * rate[...]
    chain_ref[...] = chain
    own_ref[0:8] = total[I_BLOCKS : I_BLOCKS + 8]
    for b in range(2):
        own_ref[8 + b : 9 + b] = chain_ref[pl.ds(places[2] * HELD + places[0] * 2 + b, 1), :]
    fifth = lax.broadcasted_iota(jnp.int32, (8, TILE), 0) == 4

    def one_tile(at, jb, same):
        col = columns(jnp.where(fifth, chain_ref[pl.ds(jb, 1), :], pack_i[jb]), spread_ref)
        xi, yi, zi, rho, vol, neck = (own_j[at, c : c + 1, :] for c in range(6))
        rho_gap = rho + NECK_GAP
        sums = [jnp.zeros((8, TILE), F32)] * 3
        for s in range(0, TILE, CHUNK):
            dx, dy, dz, q = offsets(xi, yi, zi, col, s)
            base = jnp.maximum(CUT_SQ - q, 0.0)
            rho_j = col(s, 3)
            gap = rho_gap + rho_j
            off = q - gap * gap
            bump = jnp.exp2(off * off * (-LOG2E / NECK_WIDTH))
            bump = bump * (2.0 + base * off * (2.0 / NECK_WIDTH))
            inv = 1.0 / (q + rho_j * rho_j)
            slope = vol * (inv * inv) * (2.0 + (base + base) * inv) + neck * bump
            slope = slope * (base * col(s, 4))
            sums = [a + folded(slope * d) for a, d in zip(sums, (dx, dy, dz))]

        def add():
            for c in range(3):
                force[at, c] += sums[c]

        return add

    for_each_tile(picked, 0, picked[PICKED + UNROLL], one_tile)
    for k in range(3):
        value = direct[k] + (2.0 * TAPER) * jnp.sum(force[0 : 2 * N_ROWS, k], axis=1)
        for n in range(N_ROWS):
            out_ref[n, 2 * k : 2 * k + 2, :] = value[2 * n : 2 * n + 2]
            if k == 2:
                out_ref[n, 6:8, :] = value[2 * n : 2 * n + 2]


def last_kernel(parts, own, kept, vel_ref, force_ref):
    total = parts[0]
    for n in range(1, N_ROWS):
        total = total + parts[n]
    for b in range(2):
        here = slice(b * TILE, (b + 1) * TILE)
        for k in range(3):
            row = slice(k, k + 1)
            force = total[2 * k + b : 2 * k + b + 1] - 2.0 * (
                own[8 + b : 9 + b, :] * own[3 * b + k : 3 * b + k + 1, :]
            )
            force_ref[row, here] = force
            vel_ref[row, here] = kept[row, here] + kept[3:4, here] * force


def transposed_keys(lists, places):
    list_a, list_g = lists[:, 0:2].astype(jnp.int32), lists[:, 2:4].astype(jnp.int32)
    source, half, lane = (lax.broadcasted_iota(jnp.int32, list_a.shape, n) for n in range(3))
    j_col, j_row = half * 4 + lane // SLOTS, list_g // 2
    known = (list_a >= 0) & (j_row % N_ROWS == places[1])
    place_j = (j_col * N_REP + j_row // N_ROWS) * 2 + list_g % 2
    key = ((source * 2 + list_a % 2) * I_BLOCKS + place_j) * 4096
    key = key + (source * 2 + half) * TILE + lane
    keys = jnp.where(known & (list_a // 2 == places[2]), key.astype(F32), NO_KEY)
    named = jnp.where(known, place_j, -1).reshape(1, 2 * N_ROWS, TILE)
    blocks = jnp.arange(I_BLOCKS, dtype=jnp.int32)
    read = jnp.any(named == blocks[:, None, None], axis=(1, 2)) | (blocks // 2 % N_REP == places[0])
    return keys.reshape(2 * N_ROWS, TILE), read.astype(jnp.int32)


def tile_codes(lists, rep_at, row_at, col_at):
    list_a, list_g = lists[:, 0].astype(jnp.int32), lists[:, 1].astype(jnp.int32)
    reps = jnp.arange(N_REP, dtype=jnp.int32)[:, None]
    live = list_a >= 0
    counts = jnp.sum(live.astype(jnp.int32), axis=1)
    j_row = list_g // 2
    place_i = (list_a // 2 * N_REP + reps) * 2 + list_a % 2
    place_j = (j_row % N_ROWS * N_REP + j_row // N_ROWS) * 2 + list_g % 2
    same = (j_row == reps * N_ROWS + row_at) & (list_a == col_at * 2 + list_g % 2)
    none = I_BLOCKS * 256
    codes = place_i * 256 + place_j * 2 + same.astype(jnp.int32) - none
    turn = (reps - rep_at) & (N_REP - 1)
    before = jnp.sum(jnp.where(turn < turn.T, counts[:, None], 0), axis=0)
    target = before[:, None] + jnp.arange(SLOTS, dtype=jnp.int32)[None, :]
    target = jnp.where(live, target, -1).reshape(1, LISTED)
    hit = target == jnp.arange(LISTED, dtype=jnp.int32)[:, None]
    placed = none + jnp.sum(jnp.where(hit, codes.reshape(1, LISTED), 0), axis=1)
    own = jnp.sum(jnp.where(turn[:, 0] == 0, counts, 0))
    return jnp.concatenate([placed, jnp.stack([jnp.sum(counts), own])]).astype(jnp.int32)


def body(positions, velocities, old_forces, charges, atom_types, table, tile_pairs):
    rep_at = lax.axis_index(REP)
    row_at = lax.axis_index(ROWS)
    col_at = lax.axis_index(COLS)
    places = jnp.stack([rep_at, row_at, col_at]).astype(jnp.int32)
    row = (1, 2 * TILE)
    joined = jnp.concatenate(
        [
            positions,
            velocities,
            old_forces,
            charges.reshape(row),
            atom_types.reshape(row).astype(F32),
            jnp.pad(tile_pairs.reshape(2, SLOTS).astype(F32), ((0, 0), (0, 2 * TILE - SLOTS))),
        ],
        axis=0,
    )
    new_positions, sent, kept = called(
        first_kernel,
        [(3, 2 * TILE), (N_REP, 3, 4, TILE), (5, 2 * TILE)],
        [],
        [table],
        [joined],
    )
    held = exchanged(sent, REP)
    meta = tile_codes(held[:, 2, 0:2, 0:SLOTS], rep_at, row_at, col_at)
    side_i = exchanged(jnp.broadcast_to(held, (N_COLS, *held.shape)), COLS)
    [sent] = called(row_kernel, [(N_ROWS, 9, 4, TILE)], [], [places], [side_i])
    side_j = exchanged(sent, ROWS)

    sums = ((I_BLOCKS + 1, 8, TILE), F32)
    forces = ((2 * N_ROWS + 1, 3, 8, TILE), F32)
    bf16 = jnp.bfloat16
    pack_i, charge_i, more_i, mask, typed, plain, paired = called(
        pack_kernel,
        [
            (I_BLOCKS + 1, 8, TILE),
            (I_BLOCKS, TILE),
            (5, I_BLOCKS, TILE),
            (2, TILE, TILE),
            ((48, 6 * TILE), bf16),
            ((32, 6 * TILE), bf16),
            ((32, 6 * TILE), bf16),
        ],
        [],
        [table],
        [side_i],
    )
    [born_parts] = called(
        born_kernel,
        [(N_COLS, I_BLOCKS, TILE)],
        [sums],
        [meta],
        [pack_i, side_j, mask, typed],
    )
    born_parts = exchanged(born_parts, COLS)
    keys, read = transposed_keys(side_j[:, HELD], places)
    [kept_tiles] = called(
        keep_kernel, [(LISTED + UNROLL + 1,)], [], [meta, read], [], outputs=SMEM, kind=jnp.int32
    )
    [picked] = called(
        pick_kernel,
        [(PICKED + UNROLL + 1,)],
        [],
        [],
        [keys],
        outputs=SMEM,
        kind=jnp.int32,
    )
    radius_i, sent, rate_i = called(
        radius_kernel,
        [(I_BLOCKS + 8, TILE), (N_ROWS, 2, HELD, TILE), (I_BLOCKS, TILE)],
        [],
        [places],
        [born_parts, pack_i, more_i, charge_i, kept_tiles],
    )
    rad_j = exchanged(sent, ROWS)
    slopes, own_j = called(
        slope_kernel,
        [(N_COLS, 8, TILE), (2 * N_ROWS + 1, 8, TILE)],
        [((I_BLOCKS + 1, 3, 8, TILE), F32)],
        [meta, places, table],
        [pack_i, side_j, typed],
    )
    [grads] = called(
        pair_kernel,
        [(N_COLS, I_BLOCKS + 8, TILE)],
        [sums],
        [kept_tiles],
        [pack_i, side_j, radius_i, rad_j, slopes, picked, mask, paired],
    )
    grads = exchanged(grads, COLS)
    [direct] = called(
        direct_kernel,
        [(3, 2 * N_ROWS, TILE)],
        [
            forces,
            ((I_BLOCKS, 8, TILE), F32),
            ((2 * N_ROWS + 8, TILE), F32),
            ((2 * N_ROWS, TILE), F32),
        ],
        [picked, places],
        [own_j, pack_i, rad_j, radius_i, charge_i, plain],
    )
    parts, own = called(
        chain_kernel,
        [(N_ROWS, 8, TILE), (10, TILE)],
        [forces, ((I_BLOCKS, TILE), F32)],
        [picked, places],
        [pack_i, own_j, grads, charge_i, radius_i, rate_i, direct, plain],
    )
    parts = exchanged(parts, ROWS)
    new_velocities, new_forces = called(
        last_kernel, [(3, 2 * TILE), (3, 2 * TILE)], [], [], [parts, own, kept]
    )
    return (new_positions, new_velocities, new_forces)


def solution(mesh):
    split = Mesh(mesh.devices.reshape(SIZES), AXES)
    rows, cols = AXES[:4], AXES[4:]
    return jax.shard_map(
        body,
        mesh=split,
        in_specs=(
            P(None, AXES),
            P(None, AXES),
            P(None, AXES),
            P(AXES),
            P(AXES),
            P(),
            P(rows, cols, None, None),
        ),
        out_specs=(P(None, AXES), P(None, AXES), P(None, AXES)),
        check_vma=False,
    )
```

```python
import jax
import jax.numpy as jnp
from jax import lax
from jax.experimental import pallas as pl
from jax.experimental.pallas import tpu as pltpu
from jax.sharding import Mesh
from jax.sharding import PartitionSpec as P

TILE = 128
SLOTS = 32
CHUNK = 32
UNROLL = 8
LISTED = 128
PICKED = 2048

CUTOFF = 12.0
COULOMB = 32.0
TIMESTEP = 0.5
OFFSET = 0.09
NECK_GAP = 0.5
NECK_WIDTH = 16.0
CUT_SQ = CUTOFF * CUTOFF
TAPER = 1.0 / (CUT_SQ * CUT_SQ)
LOG2E = 1.4426950408889634
NO_KEY = 16777216.0

AXES = ("zh", "zl", "yh", "core", "x", "yl")
SIZES = (4, 4, 2, 2, 4, 2)
REP = ("zh",)
ROWS = ("zl", "yh", "core")
COLS = ("x", "yl")
N_REP, N_ROWS, N_COLS = 4, 16, 8
HELD = 2 * N_REP
I_BLOCKS = N_COLS * HELD
J_BLOCKS = N_ROWS * HELD

VMEM = pl.BlockSpec(memory_space=pltpu.VMEM)
SMEM = pl.BlockSpec(memory_space=pltpu.SMEM)
F32 = jnp.float32


def exchanged(pieces, axes):
    return lax.all_to_all(pieces, axes, 0, 0, tiled=True)


def called(kernel, outs, scratch, smem, vmem, inputs=VMEM, outputs=VMEM, kind=F32):
    return pl.pallas_call(
        kernel,
        out_shape=[
            jax.ShapeDtypeStruct(*s) if isinstance(s[0], tuple) else jax.ShapeDtypeStruct(s, kind)
            for s in outs
        ],
        in_specs=[SMEM] * len(smem) + [inputs] * len(vmem),
        out_specs=[outputs] * len(outs),
        scratch_shapes=[pltpu.VMEM(*s) if isinstance(s, tuple) else s for s in scratch],
        compiler_params=pltpu.CompilerParams(vmem_limit_bytes=32 * 1024 * 1024),
    )(*smem, *vmem)


def looked_up(table, types, rows):
    found = [jnp.zeros(types.shape, F32) for _ in rows]
    for kind in range(8):
        here = types == float(kind)
        found = [jnp.where(here, table[r, kind], f) for r, f in zip(rows, found)]
    return found


def folded(value):
    parts = [value[s : s + 8] for s in range(0, CHUNK, 8)]
    while len(parts) > 1:
        parts = [a + b for a, b in zip(parts[::2], parts[1::2])]
    return parts[0]


def write_mask(mask_ref):
    down = lax.broadcasted_iota(jnp.int32, (TILE, TILE), 0)
    across = lax.broadcasted_iota(jnp.int32, (TILE, TILE), 1)
    mask_ref[0] = jnp.ones((TILE, TILE), F32)
    mask_ref[1] = jnp.where(down == across, 0.0, 1.0)


def write_spread(spread_ref, rows):
    at = lax.broadcasted_iota(jnp.int32, (32, TILE), 0)
    for c, row in enumerate(rows):
        hit = (at % 8 == row) & (at < 24)
        spread_ref[:, c * TILE : (c + 1) * TILE] = jnp.where(hit, 1.0, 0.0).astype(jnp.bfloat16)


def columns(rows, spread_ref):
    high = rows.astype(jnp.bfloat16).astype(F32)
    rest = rows - high
    middle = rest.astype(jnp.bfloat16).astype(F32)
    parts = jnp.concatenate([high, middle, rest - middle, jnp.zeros_like(rows)], axis=0)
    spread = lax.dot_general(
        parts.astype(jnp.bfloat16),
        spread_ref[...],
        (((0,), (0,)), ((), ())),
        preferred_element_type=F32,
    )
    return lambda s, c: spread[s : s + CHUNK, c * TILE : (c + 1) * TILE]


def offsets(xi, yi, zi, col, s):
    dx = xi - col(s, 0)
    dy = yi - col(s, 1)
    dz = zi - col(s, 2)
    return dx, dy, dz, dx * dx + dy * dy + dz * dz


def decoded(code):
    return code >> 8, (code >> 1) & 127, code & 1


def for_each_tile(meta, first, count, one_tile):
    def steps(begin, number, width):
        def step(k, _):
            at = begin + k * width
            for add in [one_tile(*decoded(meta[at + u])) for u in range(width)]:
                add()
            return 0

        lax.fori_loop(0, number, step, 0)

    half = UNROLL // 2
    whole = (count + half - 1) // UNROLL
    steps(first, whole, UNROLL)
    steps(first + whole * UNROLL, jnp.where(count > whole * UNROLL, 1, 0), half)


def typed_spread(table, spread_ref):
    row = lax.broadcasted_iota(jnp.int32, (48, TILE), 0)
    for c in range(3):
        hit = (row % 4 == c) & (row < 12)
        spread_ref[:, c * TILE : (c + 1) * TILE] = jnp.where(hit, 1.0, 0.0).astype(jnp.bfloat16)
    kind = (row % 8).astype(F32)
    rho, scale, neck = looked_up(table, kind, (0, 1, 2))
    for c, value in enumerate((rho, scale * rho * rho * rho, neck)):
        high = value.astype(jnp.bfloat16).astype(F32)
        rest = value - high
        middle = rest.astype(jnp.bfloat16).astype(F32)
        part = jnp.where(row < 24, high, jnp.where(row < 32, middle, rest - middle))
        part = jnp.where((row >= 16) & (row < 40), part, 0.0)
        spread_ref[:, (3 + c) * TILE : (4 + c) * TILE] = part.astype(jnp.bfloat16)


def typed_columns(atoms, spread):
    high = atoms.astype(jnp.bfloat16).astype(F32)
    rest = atoms - high
    middle = rest.astype(jnp.bfloat16).astype(F32)
    kinds = lax.broadcasted_iota(jnp.int32, (8, TILE), 0).astype(F32)
    hot = jnp.where(atoms[3:4, :] == kinds, 1.0, 0.0)
    parts = jnp.concatenate(
        [high, middle, rest - middle, jnp.ones((4, TILE), F32), hot, hot, hot, jnp.zeros((8, TILE), F32)],
        axis=0,
    )
    given = lax.dot_general(
        parts.astype(jnp.bfloat16),
        spread,
        (((0,), (0,)), ((), ())),
        preferred_element_type=F32,
    )
    return lambda s, c: given[s : s + CHUNK, c * TILE : (c + 1) * TILE]


def j_atoms(side_j, jb):
    return side_j[jb // HELD, jb % HELD]


def first_kernel(table, joined, new_ref, sent_ref, kept_ref):
    pos, vel, old = joined[0:3], joined[3:6], joined[6:9]
    charge, types, lists = joined[9:10], joined[10:11], joined[11:13, 0:TILE]
    [mass] = looked_up(table, types, (6,))
    new = pos + TIMESTEP * vel + TIMESTEP * TIMESTEP / (2.0 * mass) * old
    scale = TIMESTEP / (2.0 * mass)
    new_ref[...] = new
    kept_ref[0:3] = vel + scale * old
    kept_ref[3:4] = scale
    kept_ref[4:5] = charge
    for n in range(N_REP):
        for b in range(2):
            here = slice(b * TILE, (b + 1) * TILE)
            sent_ref[n, b, 0:3, :] = new[:, here]
            sent_ref[n, b, 3:4, :] = types[:, here]
            sent_ref[n, 2, 2 + b : 3 + b, :] = charge[:, here]
        sent_ref[n, 2, 0:2, :] = lists


def row_kernel(places, side_i, sent_ref):
    rows = [
        jnp.concatenate(
            [
                side_i[4 * half + n, places[0], 2, r : r + 1, 0:SLOTS]
                for n in range(4)
            ],
            axis=1,

        )
        for r in range(2)
        for half in range(2)
    ]
    lists = jnp.concatenate(rows, axis=0)
    for n in range(N_ROWS):
        for b in range(HELD):
            sent_ref[n, b] = side_i[places[2], b // 2, b % 2]
        sent_ref[n, HELD] = lists


def pick_kernel(keys_ref, picked):
    keys = keys_ref[...]
    count = jnp.sum(jnp.where(keys < NO_KEY, 1.0, 0.0)).astype(jnp.int32)

    def step(k, keys):
        least = jnp.min(keys)
        place = least.astype(jnp.int32) >> 12
        picked[k] = (place >> 6) * 256 + (place & 63) * 2
        return jnp.where(keys == least, NO_KEY, keys)

    lax.fori_loop(0, count, step, keys)
    for n in range(UNROLL):
        picked[count + n] = 2 * N_ROWS * 256
    picked[PICKED + UNROLL] = count


def packed(table, pack, count, more):
    types = pack[0:count, 3, :]
    found = looked_up(table, types, (0, 1, 2) + more)
    rho = found[0]
    pack[0:count, 3, :] = rho
    pack[0:count, 4, :] = found[1] * rho * rho * rho
    pack[0:count, 5, :] = found[2]
    return rho, found[3:]


def pack_kernel(
    table, side_i, pack_i, charge_i, more_i, mask_ref, typed_ref, plain_ref, pair_ref, near_i
):
    write_mask(mask_ref)
    typed_spread(table, typed_ref)
    write_spread(plain_ref, range(6))
    write_spread(pair_ref, (0, 1, 2, 4, 5, 6))
    for n in range(N_COLS):
        for z in range(N_REP):
            at = n * HELD + 2 * z
            for b in range(2):
                pack_i[at + b, 0:4, :] = side_i[n, z, b]
                pack_i[at + b, 4:8, :] = side_i[n, z, b]
            charge_i[at : at + 2] = side_i[n, z, 2, 2:4, :]
    pack_i[I_BLOCKS] = jnp.ones((8, TILE), F32)
    rho, more = packed(table, pack_i, I_BLOCKS, (3, 4, 5))
    for n, value in enumerate((*more, 1.0 / rho, 1.0 / (rho + OFFSET))):
        more_i[n] = value
    near_i[...] = jnp.zeros_like(near_i)
    for c in range(4):
        here = slice(c * TILE, (c + 1) * TILE)
        value = rho + NECK_GAP
        if c < 3:
            value = -pack_i[0:I_BLOCKS, c, :]
            near_i[0:I_BLOCKS, c, here] = jnp.ones((I_BLOCKS, TILE), F32)
        high = value.astype(jnp.bfloat16).astype(F32)
        rest = value - high
        middle = rest.astype(jnp.bfloat16).astype(F32)
        near_i[0:I_BLOCKS, 4, here] = high
        near_i[0:I_BLOCKS, 5, here] = middle
        near_i[0:I_BLOCKS, 6, here] = rest - middle


def keep_kernel(meta, read, kept):
    def step(k, count):
        code = meta[k]
        kept[count] = code
        return count + read[code >> 8]

    count = lax.fori_loop(0, meta[LISTED], step, 0)
    for n in range(UNROLL):
        kept[count + n] = I_BLOCKS * 256
    kept[LISTED + UNROLL] = count


def born_kernel(meta, pack_i, near_i, side_j, mask_ref, spread_ref, out_ref, acc):
    acc[...] = jnp.zeros_like(acc)
    first_rows = spread_ref[0:16, 0 : 4 * TILE].astype(F32)[0:8]

    def one_tile(ia, jb, same):
        rows = jnp.concatenate([first_rows, near_i[ia]], axis=0).astype(jnp.bfloat16)
        rows = jnp.concatenate([rows, spread_ref[0:16, 4 * TILE :]], axis=1)
        spread = jnp.concatenate([rows, spread_ref[16:, :]], axis=0)
        col = typed_columns(j_atoms(side_j, jb), spread)
        rho = pack_i[ia, 3:4, :]
        rho_sq = rho * rho
        total = jnp.zeros((8, TILE), F32)
        for s in range(0, TILE, CHUNK):
            dx, dy, dz, gap = (col(s, c) for c in range(4))
            q = dx * dx + dy * dy + dz * dz
            base = jnp.maximum(CUT_SQ - q, 0.0)
            weight = base * base * mask_ref[same, s : s + CHUNK, :]
            inv = 1.0 / (q + rho_sq)
            off = q - gap * gap
            bump = jnp.exp2(off * off * (-LOG2E / NECK_WIDTH))
            total += folded(weight * (col(s, 4) * (inv * inv) + col(s, 5) * bump))

        def add():
            acc[ia] += total

        return add

    for_each_tile(meta, 0, meta[LISTED], one_tile)
    born = TAPER * jnp.sum(acc[0:I_BLOCKS], axis=1)
    for n in range(N_COLS):
        out_ref[n] = born


def radius_kernel(places, parts, pack_i, more_i, charge, ready, radius_ref, sent_ref, rate_ref):
    born = parts[0]
    for n in range(1, N_COLS):
        born = born + parts[n]
    rho = pack_i[0:I_BLOCKS, 3, :]
    alpha, beta, gamma, inv_rho, inv_offset = (more_i[n] for n in range(5))
    scaled = rho * born
    poly = alpha * scaled - beta * scaled * scaled + gamma * scaled * scaled * scaled
    squash = jnp.tanh(poly)
    radius = 1.0 / (inv_rho - squash * inv_offset)
    slope = alpha - 2.0 * beta * scaled + 3.0 * gamma * scaled * scaled
    rate_ref[...] = radius * radius * (1.0 - squash * squash) * slope * rho * inv_offset
    radius_ref[0:I_BLOCKS] = radius
    radius_ref[I_BLOCKS : I_BLOCKS + 8] = jnp.ones((8, TILE), F32)
    here = pl.ds(pl.multiple_of(places[2] * HELD, HELD), HELD)
    held, charges = radius_ref[here, :], charge[here, :]
    for n in range(N_ROWS):
        sent_ref[n, 0] = held
        sent_ref[n, 1] = charges


def slope_kernel(meta, places, table, pack_i, side_j, spread_ref, out_ref, own_j, force):
    force[...] = jnp.zeros_like(force)
    for n in range(N_ROWS):
        for b in range(2):
            block = side_j[n, places[0] * 2 + b]
            own_j[2 * n + b, 0:4, :] = block
            own_j[2 * n + b, 4:8, :] = block
    own_j[2 * N_ROWS] = jnp.ones((8, TILE), F32)
    packed(table, own_j, 2 * N_ROWS, ())

    def one_tile(ia, jb, same):
        col = typed_columns(j_atoms(side_j, jb), spread_ref[...])
        xi, yi, zi, rho = (pack_i[ia, c : c + 1, :] for c in range(4))
        rho_sq, rho_gap = rho * rho, rho + NECK_GAP
        sums = [jnp.zeros((8, TILE), F32)] * 3
        for s in range(0, TILE, CHUNK):
            dx, dy, dz, q = offsets(xi, yi, zi, col, s)
            base = jnp.maximum(CUT_SQ - q, 0.0)
            gap = rho_gap + col(s, 3)
            off = q - gap * gap
            bump = jnp.exp2(off * off * (-LOG2E / NECK_WIDTH))
            bump = bump * (2.0 + base * off * (2.0 / NECK_WIDTH))
            inv = 1.0 / (q + rho_sq)
            slope = col(s, 4) * (inv * inv) * (2.0 + (base + base) * inv) + col(s, 5) * bump
            slope = slope * base
            sums = [a + folded(slope * d) for a, d in zip(sums, (dx, dy, dz))]

        def add():
            for c in range(3):
                force[ia, c] += sums[c]

        return add

    for_each_tile(meta, 0, meta[LISTED + 1], one_tile)
    for n in range(N_COLS):
        for b in range(2):
            total = jnp.sum(force[n * HELD + places[0] * 2 + b], axis=1)
            total = -TAPER * total
            out_ref[n, 3 * b : 3 * b + 3, :] = total
        out_ref[n, 6:8, :] = total[0:2]


def direct_kernel(
    picked, places, own_j, pack_i, rad_j, radius_i, charge_i, spread_ref, out_ref, force, sides, own, own_q
):
    force[...] = jnp.zeros_like(force)
    sides[...] = pack_i[0:I_BLOCKS]
    radii = radius_i[0:I_BLOCKS]
    sides[:, 3, :] = radii
    sides[:, 4, :] = 1.0 / radii
    sides[:, 5, :] = charge_i[...]
    own[...] = jnp.ones_like(own)
    for n in range(N_ROWS):
        own[2 * n : 2 * n + 2] = rad_j[n, 0, pl.ds(places[0] * 2, 2), :]
        own_q[2 * n : 2 * n + 2] = rad_j[n, 1, pl.ds(places[0] * 2, 2), :]

    def one_tile(at, jb, same):
        col = columns(sides[jb], spread_ref)
        xi, yi, zi = (own_j[at, c : c + 1, :] for c in range(3))
        radius = own[pl.ds(at, 1), :]
        quarter = 0.25 / radius
        sums = [jnp.zeros((8, TILE), F32)] * 3
        for s in range(0, TILE, CHUNK):
            dx, dy, dz, q = offsets(xi, yi, zi, col, s)
            base = jnp.maximum(CUT_SQ - q, 0.0)
            decay = jnp.exp2(q * (quarter * col(s, 4)) * -LOG2E)
            inv = lax.rsqrt(q + radius * col(s, 3) * decay)
            slope = 2.0 + base * (inv * inv) * (0.5 - 0.125 * decay)
            slope = slope * (base * (inv * col(s, 5)))
            sums = [a + folded(slope * d) for a, d in zip(sums, (dx, dy, dz))]

        def add():
            for c in range(3):
                force[at, c] += sums[c]

        return add

    for_each_tile(picked, 0, picked[PICKED + UNROLL], one_tile)
    scale = (-2.0 * COULOMB * TAPER) * own_q[...]
    for c in range(3):
        out_ref[c] = scale * jnp.sum(force[0 : 2 * N_ROWS, c], axis=1)


def pair_kernel(
    meta, pack_i, side_j, rad_i, rad_j, slopes, ready, mask_ref, spread_ref, out_ref, acc
):
    acc[...] = jnp.zeros_like(acc)

    def one_tile(ia, jb, same):
        n, b = jb // HELD, jb % HELD
        radius_j, charge_j = (rad_j[n, k, pl.ds(b, 1), :] for k in range(2))
        col = columns(
            jnp.concatenate(
                [side_j[n, b], radius_j, 1.0 / radius_j, charge_j, charge_j], axis=0
            ),
            spread_ref,
        )
        xi, yi, zi = (pack_i[ia, c : c + 1, :] for c in range(3))
        radius_i = rad_i[pl.ds(ia, 1), :]
        quarter_i = 0.25 / radius_i
        total = jnp.zeros((8, TILE), F32)
        for s in range(0, TILE, CHUNK):
            _, _, _, q = offsets(xi, yi, zi, col, s)
            base = jnp.maximum(CUT_SQ - q, 0.0)
            weight = base * base * mask_ref[same, s : s + CHUNK, :]
            arg = q * (quarter_i * col(s, 4))
            decay = jnp.exp2(arg * -LOG2E)
            inv = lax.rsqrt(q + radius_i * col(s, 3) * decay)
            weighted = weight * col(s, 5) * (inv * inv * inv)
            total += folded(weighted * col(s, 3) * (decay * (1.0 + arg)))

        def add():
            acc[ia] += total

        return add

    for_each_tile(meta, 0, meta[LISTED + UNROLL], one_tile)
    grads = TAPER * jnp.sum(acc[0:I_BLOCKS], axis=1)
    for n in range(N_COLS):
        out_ref[n, 0:I_BLOCKS] = grads
        out_ref[n, I_BLOCKS : I_BLOCKS + 8] = slopes[n]


def chain_kernel(
    picked, places, pack_i, own_j, parts, charge, radius, rate, direct, spread_ref, out_ref, own_ref, force, chain_ref
):
    force[...] = jnp.zeros_like(force)
    total = parts[0]
    for n in range(1, N_COLS):
        total = total + parts[n]
    charges, radii = charge[...], radius[0:I_BLOCKS]
    grad = -0.5 * charges * total[0:I_BLOCKS]
    chain = (COULOMB * charges * charges / (2.0 * radii * radii) - COULOMB * grad) * rate[...]
    chain_ref[...] = chain
    own_ref[0:8] = total[I_BLOCKS : I_BLOCKS + 8]
    for b in range(2):
        own_ref[8 + b : 9 + b] = chain_ref[pl.ds(places[2] * HELD + places[0] * 2 + b, 1), :]
    fifth = lax.broadcasted_iota(jnp.int32, (8, TILE), 0) == 4

    def one_tile(at, jb, same):
        col = columns(jnp.where(fifth, chain_ref[pl.ds(jb, 1), :], pack_i[jb]), spread_ref)
        xi, yi, zi, rho, vol, neck = (own_j[at, c : c + 1, :] for c in range(6))
        rho_gap = rho + NECK_GAP
        sums = [jnp.zeros((8, TILE), F32)] * 3
        for s in range(0, TILE, CHUNK):
            dx, dy, dz, q = offsets(xi, yi, zi, col, s)
            base = jnp.maximum(CUT_SQ - q, 0.0)
            rho_j = col(s, 3)
            gap = rho_gap + rho_j
            off = q - gap * gap
            bump = jnp.exp2(off * off * (-LOG2E / NECK_WIDTH))
            bump = bump * (2.0 + base * off * (2.0 / NECK_WIDTH))
            inv = 1.0 / (q + rho_j * rho_j)
            slope = vol * (inv * inv) * (2.0 + (base + base) * inv) + neck * bump
            slope = slope * (base * col(s, 4))
            sums = [a + folded(slope * d) for a, d in zip(sums, (dx, dy, dz))]

        def add():
            for c in range(3):
                force[at, c] += sums[c]

        return add

    for_each_tile(picked, 0, picked[PICKED + UNROLL], one_tile)
    for k in range(3):
        value = direct[k] + (2.0 * TAPER) * jnp.sum(force[0 : 2 * N_ROWS, k], axis=1)
        for n in range(N_ROWS):
            out_ref[n, 2 * k : 2 * k + 2, :] = value[2 * n : 2 * n + 2]
            if k == 2:
                out_ref[n, 6:8, :] = value[2 * n : 2 * n + 2]


def last_kernel(parts, own, kept, vel_ref, force_ref):
    total = parts[0]
    for n in range(1, N_ROWS):
        total = total + parts[n]
    for b in range(2):
        here = slice(b * TILE, (b + 1) * TILE)
        for k in range(3):
            row = slice(k, k + 1)
            force = total[2 * k + b : 2 * k + b + 1] - 2.0 * (
                own[8 + b : 9 + b, :] * own[3 * b + k : 3 * b + k + 1, :]
            )
            force_ref[row, here] = force
            vel_ref[row, here] = kept[row, here] + kept[3:4, here] * force


def transposed_keys(lists, places):
    list_a, list_g = lists[:, 0:2].astype(jnp.int32), lists[:, 2:4].astype(jnp.int32)
    source, half, lane = (lax.broadcasted_iota(jnp.int32, list_a.shape, n) for n in range(3))
    j_col, j_row = half * 4 + lane // SLOTS, list_g // 2
    known = (list_a >= 0) & (j_row % N_ROWS == places[1])
    place_j = (j_col * N_REP + j_row // N_ROWS) * 2 + list_g % 2
    key = ((source * 2 + list_a % 2) * I_BLOCKS + place_j) * 4096
    key = key + (source * 2 + half) * TILE + lane
    keys = jnp.where(known & (list_a // 2 == places[2]), key.astype(F32), NO_KEY)
    named = jnp.where(known, place_j, -1).reshape(1, 2 * N_ROWS, TILE)
    blocks = jnp.arange(I_BLOCKS, dtype=jnp.int32)
    read = jnp.any(named == blocks[:, None, None], axis=(1, 2)) | (blocks // 2 % N_REP == places[0])
    return keys.reshape(2 * N_ROWS, TILE), read.astype(jnp.int32)


def tile_codes(lists, rep_at, row_at, col_at):
    list_a, list_g = lists[:, 0].astype(jnp.int32), lists[:, 1].astype(jnp.int32)
    reps = jnp.arange(N_REP, dtype=jnp.int32)[:, None]
    live = list_a >= 0
    counts = jnp.sum(live.astype(jnp.int32), axis=1)
    j_row = list_g // 2
    place_i = (list_a // 2 * N_REP + reps) * 2 + list_a % 2
    place_j = (j_row % N_ROWS * N_REP + j_row // N_ROWS) * 2 + list_g % 2
    same = (j_row == reps * N_ROWS + row_at) & (list_a == col_at * 2 + list_g % 2)
    none = I_BLOCKS * 256
    codes = place_i * 256 + place_j * 2 + same.astype(jnp.int32) - none
    turn = (reps - rep_at) & (N_REP - 1)
    before = jnp.sum(jnp.where(turn < turn.T, counts[:, None], 0), axis=0)
    target = before[:, None] + jnp.arange(SLOTS, dtype=jnp.int32)[None, :]
    target = jnp.where(live, target, -1).reshape(1, LISTED)
    hit = target == jnp.arange(LISTED, dtype=jnp.int32)[:, None]
    placed = none + jnp.sum(jnp.where(hit, codes.reshape(1, LISTED), 0), axis=1)
    own = jnp.sum(jnp.where(turn[:, 0] == 0, counts, 0))
    return jnp.concatenate([placed, jnp.stack([jnp.sum(counts), own])]).astype(jnp.int32)


def body(positions, velocities, old_forces, charges, atom_types, table, tile_pairs):
    rep_at = lax.axis_index(REP)
    row_at = lax.axis_index(ROWS)
    col_at = lax.axis_index(COLS)
    places = jnp.stack([rep_at, row_at, col_at]).astype(jnp.int32)
    row = (1, 2 * TILE)
    joined = jnp.concatenate(
        [
            positions,
            velocities,
            old_forces,
            charges.reshape(row),
            atom_types.reshape(row).astype(F32),
            jnp.pad(tile_pairs.reshape(2, SLOTS).astype(F32), ((0, 0), (0, 2 * TILE - SLOTS))),
        ],
        axis=0,
    )
    new_positions, sent, kept = called(
        first_kernel,
        [(3, 2 * TILE), (N_REP, 3, 4, TILE), (5, 2 * TILE)],
        [],
        [table],
        [joined],
    )
    held = exchanged(sent, REP)
    meta = tile_codes(held[:, 2, 0:2, 0:SLOTS], rep_at, row_at, col_at)
    side_i = exchanged(jnp.broadcast_to(held, (N_COLS, *held.shape)), COLS)
    [sent] = called(row_kernel, [(N_ROWS, 9, 4, TILE)], [], [places], [side_i])
    side_j = exchanged(sent, ROWS)

    sums = ((I_BLOCKS + 1, 8, TILE), F32)
    forces = ((2 * N_ROWS + 1, 3, 8, TILE), F32)
    bf16 = jnp.bfloat16
    pack_i, charge_i, more_i, mask, typed, plain, paired, near_i = called(
        pack_kernel,
        [
            (I_BLOCKS + 1, 8, TILE),
            (I_BLOCKS, TILE),
            (5, I_BLOCKS, TILE),
            (2, TILE, TILE),
            ((48, 6 * TILE), bf16),
            ((32, 6 * TILE), bf16),
            ((32, 6 * TILE), bf16),
            (I_BLOCKS + 1, 8, 4 * TILE),
        ],
        [],
        [table],
        [side_i],
    )
    [born_parts] = called(
        born_kernel,
        [(N_COLS, I_BLOCKS, TILE)],
        [sums],
        [meta],
        [pack_i, near_i, side_j, mask, typed],
    )
    born_parts = exchanged(born_parts, COLS)
    keys, read = transposed_keys(side_j[:, HELD], places)
    [kept_tiles] = called(
        keep_kernel, [(LISTED + UNROLL + 1,)], [], [meta, read], [], outputs=SMEM, kind=jnp.int32
    )
    [picked] = called(
        pick_kernel,
        [(PICKED + UNROLL + 1,)],
        [],
        [],
        [keys],
        outputs=SMEM,
        kind=jnp.int32,
    )
    radius_i, sent, rate_i = called(
        radius_kernel,
        [(I_BLOCKS + 8, TILE), (N_ROWS, 2, HELD, TILE), (I_BLOCKS, TILE)],
        [],
        [places],
        [born_parts, pack_i, more_i, charge_i, kept_tiles],
    )
    rad_j = exchanged(sent, ROWS)
    slopes, own_j = called(
        slope_kernel,
        [(N_COLS, 8, TILE), (2 * N_ROWS + 1, 8, TILE)],
        [((I_BLOCKS + 1, 3, 8, TILE), F32)],
        [meta, places, table],
        [pack_i, side_j, typed],
    )
    [grads] = called(
        pair_kernel,
        [(N_COLS, I_BLOCKS + 8, TILE)],
        [sums],
        [kept_tiles],
        [pack_i, side_j, radius_i, rad_j, slopes, picked, mask, paired],
    )
    grads = exchanged(grads, COLS)
    [direct] = called(
        direct_kernel,
        [(3, 2 * N_ROWS, TILE)],
        [
            forces,
            ((I_BLOCKS, 8, TILE), F32),
            ((2 * N_ROWS + 8, TILE), F32),
            ((2 * N_ROWS, TILE), F32),
        ],
        [picked, places],
        [own_j, pack_i, rad_j, radius_i, charge_i, plain],
    )
    parts, own = called(
        chain_kernel,
        [(N_ROWS, 8, TILE), (10, TILE)],
        [forces, ((I_BLOCKS, TILE), F32)],
        [picked, places],
        [pack_i, own_j, grads, charge_i, radius_i, rate_i, direct, plain],
    )
    parts = exchanged(parts, ROWS)
    new_velocities, new_forces = called(
        last_kernel, [(3, 2 * TILE), (3, 2 * TILE)], [], [], [parts, own, kept]
    )
    return (new_positions, new_velocities, new_forces)


def solution(mesh):
    split = Mesh(mesh.devices.reshape(SIZES), AXES)
    rows, cols = AXES[:4], AXES[4:]
    return jax.shard_map(
        body,
        mesh=split,
        in_specs=(
            P(None, AXES),
            P(None, AXES),
            P(None, AXES),
            P(AXES),
            P(AXES),
            P(),
            P(rows, cols, None, None),
        ),
        out_specs=(P(None, AXES), P(None, AXES), P(None, AXES)),
        check_vma=False,
    )
```

```python
import jax
import jax.numpy as jnp
from jax import lax
from jax.experimental import pallas as pl
from jax.experimental.pallas import tpu as pltpu
from jax.sharding import Mesh
from jax.sharding import PartitionSpec as P

TILE = 128
SLOTS = 32
CHUNK = 32
UNROLL = 8
LISTED = 128
PICKED = 2048

CUTOFF = 12.0
COULOMB = 32.0
TIMESTEP = 0.5
OFFSET = 0.09
NECK_GAP = 0.5
NECK_WIDTH = 16.0
CUT_SQ = CUTOFF * CUTOFF
TAPER = 1.0 / (CUT_SQ * CUT_SQ)
LOG2E = 1.4426950408889634
NO_KEY = 16777216.0

AXES = ("zh", "zl", "yh", "core", "x", "yl")
SIZES = (4, 4, 2, 2, 4, 2)
REP = ("zh",)
ROWS = ("zl", "yh", "core")
COLS = ("x", "yl")
N_REP, N_ROWS, N_COLS = 4, 16, 8
HELD = 2 * N_REP
I_BLOCKS = N_COLS * HELD
J_BLOCKS = N_ROWS * HELD

VMEM = pl.BlockSpec(memory_space=pltpu.VMEM)
SMEM = pl.BlockSpec(memory_space=pltpu.SMEM)
F32 = jnp.float32


def exchanged(pieces, axes):
    return lax.all_to_all(pieces, axes, 0, 0, tiled=True)


def called(kernel, outs, scratch, smem, vmem, inputs=VMEM, outputs=VMEM, kind=F32):
    return pl.pallas_call(
        kernel,
        out_shape=[
            jax.ShapeDtypeStruct(*s) if isinstance(s[0], tuple) else jax.ShapeDtypeStruct(s, kind)
            for s in outs
        ],
        in_specs=[SMEM] * len(smem) + [inputs] * len(vmem),
        out_specs=[outputs] * len(outs),
        scratch_shapes=[pltpu.VMEM(*s) if isinstance(s, tuple) else s for s in scratch],
        compiler_params=pltpu.CompilerParams(vmem_limit_bytes=32 * 1024 * 1024),
    )(*smem, *vmem)


def looked_up(table, types, rows):
    found = [jnp.zeros(types.shape, F32) for _ in rows]
    for kind in range(8):
        here = types == float(kind)
        found = [jnp.where(here, table[r, kind], f) for r, f in zip(rows, found)]
    return found


def folded(value):
    parts = [value[s : s + 8] for s in range(0, CHUNK, 8)]
    while len(parts) > 1:
        parts = [a + b for a, b in zip(parts[::2], parts[1::2])]
    return parts[0]


def write_mask(mask_ref):
    down = lax.broadcasted_iota(jnp.int32, (TILE, TILE), 0)
    across = lax.broadcasted_iota(jnp.int32, (TILE, TILE), 1)
    mask_ref[0] = jnp.ones((TILE, TILE), F32)
    mask_ref[1] = jnp.where(down == across, 0.0, 1.0)


def write_spread(spread_ref, rows):
    at = lax.broadcasted_iota(jnp.int32, (32, TILE), 0)
    for c, row in enumerate(rows):
        hit = (at % 8 == row) & (at < 24)
        spread_ref[:, c * TILE : (c + 1) * TILE] = jnp.where(hit, 1.0, 0.0).astype(jnp.bfloat16)


def columns(rows, spread_ref):
    high = rows.astype(jnp.bfloat16).astype(F32)
    rest = rows - high
    middle = rest.astype(jnp.bfloat16).astype(F32)
    parts = jnp.concatenate([high, middle, rest - middle, jnp.zeros_like(rows)], axis=0)
    spread = lax.dot_general(
        parts.astype(jnp.bfloat16),
        spread_ref[...],
        (((0,), (0,)), ((), ())),
        preferred_element_type=F32,
    )
    return lambda s, c: spread[s : s + CHUNK, c * TILE : (c + 1) * TILE]


def offsets(xi, yi, zi, col, s):
    dx = xi - col(s, 0)
    dy = yi - col(s, 1)
    dz = zi - col(s, 2)
    return dx, dy, dz, dx * dx + dy * dy + dz * dz


def decoded(code):
    return code >> 8, (code >> 1) & 127, code & 1


def for_each_tile(meta, first, count, one_tile):
    def steps(begin, number, width):
        def step(k, _):
            at = begin + k * width
            for add in [one_tile(*decoded(meta[at + u])) for u in range(width)]:
                add()
            return 0

        lax.fori_loop(0, number, step, 0)

    half = UNROLL // 2
    whole = (count + half - 1) // UNROLL
    steps(first, whole, UNROLL)
    steps(first + whole * UNROLL, jnp.where(count > whole * UNROLL, 1, 0), half)


def typed_spread(table, spread_ref):
    row = lax.broadcasted_iota(jnp.int32, (48, TILE), 0)
    for c in range(3):
        hit = (row % 4 == c) & (row < 12)
        spread_ref[:, c * TILE : (c + 1) * TILE] = jnp.where(hit, 1.0, 0.0).astype(jnp.bfloat16)
    kind = (row % 8).astype(F32)
    rho, scale, neck = looked_up(table, kind, (0, 1, 2))
    for c, value in enumerate((rho, scale * rho * rho * rho, neck)):
        high = value.astype(jnp.bfloat16).astype(F32)
        rest = value - high
        middle = rest.astype(jnp.bfloat16).astype(F32)
        part = jnp.where(row < 24, high, jnp.where(row < 32, middle, rest - middle))
        part = jnp.where((row >= 16) & (row < 40), part, 0.0)
        spread_ref[:, (3 + c) * TILE : (4 + c) * TILE] = part.astype(jnp.bfloat16)


def typed_columns(atoms, spread):
    high = atoms.astype(jnp.bfloat16).astype(F32)
    rest = atoms - high
    middle = rest.astype(jnp.bfloat16).astype(F32)
    kinds = lax.broadcasted_iota(jnp.int32, (8, TILE), 0).astype(F32)
    hot = jnp.where(atoms[3:4, :] == kinds, 1.0, 0.0)
    parts = jnp.concatenate(
        [high, middle, rest - middle, jnp.ones((4, TILE), F32), hot, hot, hot, jnp.zeros((8, TILE), F32)],
        axis=0,
    )
    given = lax.dot_general(
        parts.astype(jnp.bfloat16),
        spread,
        (((0,), (0,)), ((), ())),
        preferred_element_type=F32,
    )
    return lambda s, c: given[s : s + CHUNK, c * TILE : (c + 1) * TILE]


def j_atoms(side_j, jb):
    return side_j[jb // HELD, jb % HELD]


def first_kernel(table, joined, new_ref, sent_ref, kept_ref):
    pos, vel, old = joined[0:3], joined[3:6], joined[6:9]
    charge, types, lists = joined[9:10], joined[10:11], joined[11:13, 0:TILE]
    [mass] = looked_up(table, types, (6,))
    new = pos + TIMESTEP * vel + TIMESTEP * TIMESTEP / (2.0 * mass) * old
    scale = TIMESTEP / (2.0 * mass)
    new_ref[...] = new
    kept_ref[0:3] = vel + scale * old
    kept_ref[3:4] = scale
    kept_ref[4:5] = charge
    for n in range(N_REP):
        for b in range(2):
            here = slice(b * TILE, (b + 1) * TILE)
            sent_ref[n, b, 0:3, :] = new[:, here]
            sent_ref[n, b, 3:4, :] = types[:, here]
            sent_ref[n, 2, 2 + b : 3 + b, :] = charge[:, here]
        sent_ref[n, 2, 0:2, :] = lists


def row_kernel(places, side_i, sent_ref):
    rows = [
        jnp.concatenate(
            [
                side_i[4 * half + n, places[0], 2, r : r + 1, 0:SLOTS]
                for n in range(4)
            ],
            axis=1,

        )
        for r in range(2)
        for half in range(2)
    ]
    lists = jnp.concatenate(rows, axis=0)
    for n in range(N_ROWS):
        for b in range(HELD):
            sent_ref[n, b] = side_i[places[2], b // 2, b % 2]
        sent_ref[n, HELD] = lists


def pick_kernel(keys_ref, picked):
    keys = keys_ref[...]
    count = jnp.sum(jnp.where(keys < NO_KEY, 1.0, 0.0)).astype(jnp.int32)

    def step(k, keys):
        least = jnp.min(keys)
        place = least.astype(jnp.int32) >> 12
        picked[k] = (place >> 6) * 256 + (place & 63) * 2
        return jnp.where(keys == least, NO_KEY, keys)

    lax.fori_loop(0, count, step, keys)
    for n in range(UNROLL):
        picked[count + n] = 2 * N_ROWS * 256
    picked[PICKED + UNROLL] = count


def packed(table, pack, count, more):
    types = pack[0:count, 3, :]
    found = looked_up(table, types, (0, 1, 2) + more)
    rho = found[0]
    pack[0:count, 3, :] = rho
    pack[0:count, 4, :] = found[1] * rho * rho * rho
    pack[0:count, 5, :] = found[2]
    return rho, found[3:]


def pack_kernel(
    table, side_i, pack_i, charge_i, more_i, mask_ref, typed_ref, plain_ref, pair_ref, near_i
):
    write_mask(mask_ref)
    typed_spread(table, typed_ref)
    write_spread(plain_ref, range(6))
    write_spread(pair_ref, (0, 1, 2, 4, 5, 6))
    for n in range(N_COLS):
        for z in range(N_REP):
            at = n * HELD + 2 * z
            for b in range(2):
                pack_i[at + b, 0:4, :] = side_i[n, z, b]
                pack_i[at + b, 4:8, :] = side_i[n, z, b]
            charge_i[at : at + 2] = side_i[n, z, 2, 2:4, :]
    pack_i[I_BLOCKS] = jnp.ones((8, TILE), F32)
    rho, more = packed(table, pack_i, I_BLOCKS, (3, 4, 5))
    for n, value in enumerate((*more, 1.0 / rho, 1.0 / (rho + OFFSET))):
        more_i[n] = value
    near_i[...] = jnp.zeros_like(near_i)
    for c in range(4):
        here = slice(c * TILE, (c + 1) * TILE)
        value = rho + NECK_GAP
        if c < 3:
            value = -pack_i[0:I_BLOCKS, c, :]
        high = value.astype(jnp.bfloat16).astype(F32)
        rest = value - high
        middle = rest.astype(jnp.bfloat16).astype(F32)
        near_i[0:I_BLOCKS, 0, here] = high
        near_i[0:I_BLOCKS, 1, here] = middle
        near_i[0:I_BLOCKS, 2, here] = rest - middle


def keep_kernel(meta, read, kept):
    def step(k, count):
        code = meta[k]
        kept[count] = code
        return count + read[code >> 8]

    count = lax.fori_loop(0, meta[LISTED], step, 0)
    for n in range(UNROLL):
        kept[count + n] = I_BLOCKS * 256
    kept[LISTED + UNROLL] = count


def born_kernel(meta, pack_i, near_i, side_j, mask_ref, spread_ref, out_ref, acc):
    acc[...] = jnp.zeros_like(acc)
    first_rows = spread_ref[0:16, 0 : 4 * TILE].astype(F32)[0:12]

    def one_tile(ia, jb, same):
        rows = jnp.concatenate([first_rows, near_i[ia]], axis=0).astype(jnp.bfloat16)
        rows = jnp.concatenate([rows, spread_ref[0:16, 4 * TILE :]], axis=1)
        spread = jnp.concatenate([rows, spread_ref[16:, :]], axis=0)
        col = typed_columns(j_atoms(side_j, jb), spread)
        rho = pack_i[ia, 3:4, :]
        rho_sq = rho * rho
        total = jnp.zeros((8, TILE), F32)
        for s in range(0, TILE, CHUNK):
            dx, dy, dz, gap = (col(s, c) for c in range(4))
            q = dx * dx + dy * dy + dz * dz
            base = jnp.maximum(CUT_SQ - q, 0.0)
            weight = base * base * mask_ref[same, s : s + CHUNK, :]
            inv = 1.0 / (q + rho_sq)
            off = q - gap * gap
            bump = jnp.exp2(off * off * (-LOG2E / NECK_WIDTH))
            total += folded(weight * (col(s, 4) * (inv * inv) + col(s, 5) * bump))

        def add():
            acc[ia] += total

        return add

    for_each_tile(meta, 0, meta[LISTED], one_tile)
    born = TAPER * jnp.sum(acc[0:I_BLOCKS], axis=1)
    for n in range(N_COLS):
        out_ref[n] = born


def radius_kernel(places, parts, pack_i, more_i, charge, ready, radius_ref, sent_ref, rate_ref):
    born = parts[0]
    for n in range(1, N_COLS):
        born = born + parts[n]
    rho = pack_i[0:I_BLOCKS, 3, :]
    alpha, beta, gamma, inv_rho, inv_offset = (more_i[n] for n in range(5))
    scaled = rho * born
    poly = alpha * scaled - beta * scaled * scaled + gamma * scaled * scaled * scaled
    squash = jnp.tanh(poly)
    radius = 1.0 / (inv_rho - squash * inv_offset)
    slope = alpha - 2.0 * beta * scaled + 3.0 * gamma * scaled * scaled
    rate_ref[...] = radius * radius * (1.0 - squash * squash) * slope * rho * inv_offset
    radius_ref[0:I_BLOCKS] = radius
    radius_ref[I_BLOCKS : I_BLOCKS + 8] = jnp.ones((8, TILE), F32)
    here = pl.ds(pl.multiple_of(places[2] * HELD, HELD), HELD)
    held, charges = radius_ref[here, :], charge[here, :]
    for n in range(N_ROWS):
        sent_ref[n, 0] = held
        sent_ref[n, 1] = charges


def slope_kernel(meta, places, table, pack_i, side_j, spread_ref, out_ref, own_j, force):
    force[...] = jnp.zeros_like(force)
    for n in range(N_ROWS):
        for b in range(2):
            block = side_j[n, places[0] * 2 + b]
            own_j[2 * n + b, 0:4, :] = block
            own_j[2 * n + b, 4:8, :] = block
    own_j[2 * N_ROWS] = jnp.ones((8, TILE), F32)
    packed(table, own_j, 2 * N_ROWS, ())

    def one_tile(ia, jb, same):
        col = typed_columns(j_atoms(side_j, jb), spread_ref[...])
        xi, yi, zi, rho = (pack_i[ia, c : c + 1, :] for c in range(4))
        rho_sq, rho_gap = rho * rho, rho + NECK_GAP
        sums = [jnp.zeros((8, TILE), F32)] * 3
        for s in range(0, TILE, CHUNK):
            dx, dy, dz, q = offsets(xi, yi, zi, col, s)
            base = jnp.maximum(CUT_SQ - q, 0.0)
            gap = rho_gap + col(s, 3)
            off = q - gap * gap
            bump = jnp.exp2(off * off * (-LOG2E / NECK_WIDTH))
            bump = bump * (2.0 + base * off * (2.0 / NECK_WIDTH))
            inv = 1.0 / (q + rho_sq)
            slope = col(s, 4) * (inv * inv) * (2.0 + (base + base) * inv) + col(s, 5) * bump
            slope = slope * base
            sums = [a + folded(slope * d) for a, d in zip(sums, (dx, dy, dz))]

        def add():
            for c in range(3):
                force[ia, c] += sums[c]

        return add

    for_each_tile(meta, 0, meta[LISTED + 1], one_tile)
    for n in range(N_COLS):
        for b in range(2):
            total = jnp.sum(force[n * HELD + places[0] * 2 + b], axis=1)
            total = -TAPER * total
            out_ref[n, 3 * b : 3 * b + 3, :] = total
        out_ref[n, 6:8, :] = total[0:2]


def direct_kernel(
    picked, places, own_j, pack_i, rad_j, radius_i, charge_i, spread_ref, out_ref, force, sides, own, own_q
):
    force[...] = jnp.zeros_like(force)
    sides[...] = pack_i[0:I_BLOCKS]
    radii = radius_i[0:I_BLOCKS]
    sides[:, 3, :] = radii
    sides[:, 4, :] = 1.0 / radii
    sides[:, 5, :] = charge_i[...]
    own[...] = jnp.ones_like(own)
    for n in range(N_ROWS):
        own[2 * n : 2 * n + 2] = rad_j[n, 0, pl.ds(places[0] * 2, 2), :]
        own_q[2 * n : 2 * n + 2] = rad_j[n, 1, pl.ds(places[0] * 2, 2), :]

    def one_tile(at, jb, same):
        col = columns(sides[jb], spread_ref)
        xi, yi, zi = (own_j[at, c : c + 1, :] for c in range(3))
        radius = own[pl.ds(at, 1), :]
        quarter = 0.25 / radius
        sums = [jnp.zeros((8, TILE), F32)] * 3
        for s in range(0, TILE, CHUNK):
            dx, dy, dz, q = offsets(xi, yi, zi, col, s)
            base = jnp.maximum(CUT_SQ - q, 0.0)
            decay = jnp.exp2(q * (quarter * col(s, 4)) * -LOG2E)
            inv = lax.rsqrt(q + radius * col(s, 3) * decay)
            slope = 2.0 + base * (inv * inv) * (0.5 - 0.125 * decay)
            slope = slope * (base * (inv * col(s, 5)))
            sums = [a + folded(slope * d) for a, d in zip(sums, (dx, dy, dz))]

        def add():
            for c in range(3):
                force[at, c] += sums[c]

        return add

    for_each_tile(picked, 0, picked[PICKED + UNROLL], one_tile)
    scale = (-2.0 * COULOMB * TAPER) * own_q[...]
    for c in range(3):
        out_ref[c] = scale * jnp.sum(force[0 : 2 * N_ROWS, c], axis=1)


def pair_kernel(
    meta, pack_i, side_j, rad_i, rad_j, slopes, ready, mask_ref, spread_ref, out_ref, acc
):
    acc[...] = jnp.zeros_like(acc)

    def one_tile(ia, jb, same):
        n, b = jb // HELD, jb % HELD
        radius_j, charge_j = (rad_j[n, k, pl.ds(b, 1), :] for k in range(2))
        col = columns(
            jnp.concatenate(
                [side_j[n, b], radius_j, 1.0 / radius_j, charge_j, charge_j], axis=0
            ),
            spread_ref,
        )
        xi, yi, zi = (pack_i[ia, c : c + 1, :] for c in range(3))
        radius_i = rad_i[pl.ds(ia, 1), :]
        quarter_i = 0.25 / radius_i
        total = jnp.zeros((8, TILE), F32)
        for s in range(0, TILE, CHUNK):
            _, _, _, q = offsets(xi, yi, zi, col, s)
            base = jnp.maximum(CUT_SQ - q, 0.0)
            weight = base * base * mask_ref[same, s : s + CHUNK, :]
            arg = q * (quarter_i * col(s, 4))
            decay = jnp.exp2(arg * -LOG2E)
            inv = lax.rsqrt(q + radius_i * col(s, 3) * decay)
            weighted = weight * col(s, 5) * (inv * inv * inv)
            total += folded(weighted * col(s, 3) * (decay * (1.0 + arg)))

        def add():
            acc[ia] += total

        return add

    for_each_tile(meta, 0, meta[LISTED + UNROLL], one_tile)
    grads = TAPER * jnp.sum(acc[0:I_BLOCKS], axis=1)
    for n in range(N_COLS):
        out_ref[n, 0:I_BLOCKS] = grads
        out_ref[n, I_BLOCKS : I_BLOCKS + 8] = slopes[n]


def chain_kernel(
    picked, places, pack_i, own_j, parts, charge, radius, rate, direct, spread_ref, out_ref, own_ref, force, chain_ref
):
    force[...] = jnp.zeros_like(force)
    total = parts[0]
    for n in range(1, N_COLS):
        total = total + parts[n]
    charges, radii = charge[...], radius[0:I_BLOCKS]
    grad = -0.5 * charges * total[0:I_BLOCKS]
    chain = (COULOMB * charges * charges / (2.0 * radii * radii) - COULOMB * grad) * rate[...]
    chain_ref[...] = chain
    own_ref[0:8] = total[I_BLOCKS : I_BLOCKS + 8]
    for b in range(2):
        own_ref[8 + b : 9 + b] = chain_ref[pl.ds(places[2] * HELD + places[0] * 2 + b, 1), :]
    fifth = lax.broadcasted_iota(jnp.int32, (8, TILE), 0) == 4

    def one_tile(at, jb, same):
        col = columns(jnp.where(fifth, chain_ref[pl.ds(jb, 1), :], pack_i[jb]), spread_ref)
        xi, yi, zi, rho, vol, neck = (own_j[at, c : c + 1, :] for c in range(6))
        rho_gap = rho + NECK_GAP
        sums = [jnp.zeros((8, TILE), F32)] * 3
        for s in range(0, TILE, CHUNK):
            dx, dy, dz, q = offsets(xi, yi, zi, col, s)
            base = jnp.maximum(CUT_SQ - q, 0.0)
            rho_j = col(s, 3)
            gap = rho_gap + rho_j
            off = q - gap * gap
            bump = jnp.exp2(off * off * (-LOG2E / NECK_WIDTH))
            bump = bump * (2.0 + base * off * (2.0 / NECK_WIDTH))
            inv = 1.0 / (q + rho_j * rho_j)
            slope = vol * (inv * inv) * (2.0 + (base + base) * inv) + neck * bump
            slope = slope * (base * col(s, 4))
            sums = [a + folded(slope * d) for a, d in zip(sums, (dx, dy, dz))]

        def add():
            for c in range(3):
                force[at, c] += sums[c]

        return add

    for_each_tile(picked, 0, picked[PICKED + UNROLL], one_tile)
    for k in range(3):
        value = direct[k] + (2.0 * TAPER) * jnp.sum(force[0 : 2 * N_ROWS, k], axis=1)
        for n in range(N_ROWS):
            out_ref[n, 2 * k : 2 * k + 2, :] = value[2 * n : 2 * n + 2]
            if k == 2:
                out_ref[n, 6:8, :] = value[2 * n : 2 * n + 2]


def last_kernel(parts, own, kept, vel_ref, force_ref):
    total = parts[0]
    for n in range(1, N_ROWS):
        total = total + parts[n]
    for b in range(2):
        here = slice(b * TILE, (b + 1) * TILE)
        for k in range(3):
            row = slice(k, k + 1)
            force = total[2 * k + b : 2 * k + b + 1] - 2.0 * (
                own[8 + b : 9 + b, :] * own[3 * b + k : 3 * b + k + 1, :]
            )
            force_ref[row, here] = force
            vel_ref[row, here] = kept[row, here] + kept[3:4, here] * force


def transposed_keys(lists, places):
    list_a, list_g = lists[:, 0:2].astype(jnp.int32), lists[:, 2:4].astype(jnp.int32)
    source, half, lane = (lax.broadcasted_iota(jnp.int32, list_a.shape, n) for n in range(3))
    j_col, j_row = half * 4 + lane // SLOTS, list_g // 2
    known = (list_a >= 0) & (j_row % N_ROWS == places[1])
    place_j = (j_col * N_REP + j_row // N_ROWS) * 2 + list_g % 2
    key = ((source * 2 + list_a % 2) * I_BLOCKS + place_j) * 4096
    key = key + (source * 2 + half) * TILE + lane
    keys = jnp.where(known & (list_a // 2 == places[2]), key.astype(F32), NO_KEY)
    named = jnp.where(known, place_j, -1).reshape(1, 2 * N_ROWS, TILE)
    blocks = jnp.arange(I_BLOCKS, dtype=jnp.int32)
    read = jnp.any(named == blocks[:, None, None], axis=(1, 2)) | (blocks // 2 % N_REP == places[0])
    return keys.reshape(2 * N_ROWS, TILE), read.astype(jnp.int32)


def tile_codes(lists, rep_at, row_at, col_at):
    list_a, list_g = lists[:, 0].astype(jnp.int32), lists[:, 1].astype(jnp.int32)
    reps = jnp.arange(N_REP, dtype=jnp.int32)[:, None]
    live = list_a >= 0
    counts = jnp.sum(live.astype(jnp.int32), axis=1)
    j_row = list_g // 2
    place_i = (list_a // 2 * N_REP + reps) * 2 + list_a % 2
    place_j = (j_row % N_ROWS * N_REP + j_row // N_ROWS) * 2 + list_g % 2
    same = (j_row == reps * N_ROWS + row_at) & (list_a == col_at * 2 + list_g % 2)
    none = I_BLOCKS * 256
    codes = place_i * 256 + place_j * 2 + same.astype(jnp.int32) - none
    turn = (reps - rep_at) & (N_REP - 1)
    before = jnp.sum(jnp.where(turn < turn.T, counts[:, None], 0), axis=0)
    target = before[:, None] + jnp.arange(SLOTS, dtype=jnp.int32)[None, :]
    target = jnp.where(live, target, -1).reshape(1, LISTED)
    hit = target == jnp.arange(LISTED, dtype=jnp.int32)[:, None]
    placed = none + jnp.sum(jnp.where(hit, codes.reshape(1, LISTED), 0), axis=1)
    own = jnp.sum(jnp.where(turn[:, 0] == 0, counts, 0))
    return jnp.concatenate([placed, jnp.stack([jnp.sum(counts), own])]).astype(jnp.int32)


def body(positions, velocities, old_forces, charges, atom_types, table, tile_pairs):
    rep_at = lax.axis_index(REP)
    row_at = lax.axis_index(ROWS)
    col_at = lax.axis_index(COLS)
    places = jnp.stack([rep_at, row_at, col_at]).astype(jnp.int32)
    row = (1, 2 * TILE)
    joined = jnp.concatenate(
        [
            positions,
            velocities,
            old_forces,
            charges.reshape(row),
            atom_types.reshape(row).astype(F32),
            jnp.pad(tile_pairs.reshape(2, SLOTS).astype(F32), ((0, 0), (0, 2 * TILE - SLOTS))),
        ],
        axis=0,
    )
    new_positions, sent, kept = called(
        first_kernel,
        [(3, 2 * TILE), (N_REP, 3, 4, TILE), (5, 2 * TILE)],
        [],
        [table],
        [joined],
    )
    held = exchanged(sent, REP)
    meta = tile_codes(held[:, 2, 0:2, 0:SLOTS], rep_at, row_at, col_at)
    side_i = exchanged(jnp.broadcast_to(held, (N_COLS, *held.shape)), COLS)
    [sent] = called(row_kernel, [(N_ROWS, 9, 4, TILE)], [], [places], [side_i])
    side_j = exchanged(sent, ROWS)

    sums = ((I_BLOCKS + 1, 8, TILE), F32)
    forces = ((2 * N_ROWS + 1, 3, 8, TILE), F32)
    bf16 = jnp.bfloat16
    pack_i, charge_i, more_i, mask, typed, plain, paired, near_i = called(
        pack_kernel,
        [
            (I_BLOCKS + 1, 8, TILE),
            (I_BLOCKS, TILE),
            (5, I_BLOCKS, TILE),
            (2, TILE, TILE),
            ((48, 6 * TILE), bf16),
            ((32, 6 * TILE), bf16),
            ((32, 6 * TILE), bf16),
            (I_BLOCKS + 1, 4, 4 * TILE),
        ],
        [],
        [table],
        [side_i],
    )
    [born_parts] = called(
        born_kernel,
        [(N_COLS, I_BLOCKS, TILE)],
        [sums],
        [meta],
        [pack_i, near_i, side_j, mask, typed],
    )
    born_parts = exchanged(born_parts, COLS)
    keys, read = transposed_keys(side_j[:, HELD], places)
    [kept_tiles] = called(
        keep_kernel, [(LISTED + UNROLL + 1,)], [], [meta, read], [], outputs=SMEM, kind=jnp.int32
    )
    [picked] = called(
        pick_kernel,
        [(PICKED + UNROLL + 1,)],
        [],
        [],
        [keys],
        outputs=SMEM,
        kind=jnp.int32,
    )
    radius_i, sent, rate_i = called(
        radius_kernel,
        [(I_BLOCKS + 8, TILE), (N_ROWS, 2, HELD, TILE), (I_BLOCKS, TILE)],
        [],
        [places],
        [born_parts, pack_i, more_i, charge_i, kept_tiles],
    )
    rad_j = exchanged(sent, ROWS)
    slopes, own_j = called(
        slope_kernel,
        [(N_COLS, 8, TILE), (2 * N_ROWS + 1, 8, TILE)],
        [((I_BLOCKS + 1, 3, 8, TILE), F32)],
        [meta, places, table],
        [pack_i, side_j, typed],
    )
    [grads] = called(
        pair_kernel,
        [(N_COLS, I_BLOCKS + 8, TILE)],
        [sums],
        [kept_tiles],
        [pack_i, side_j, radius_i, rad_j, slopes, picked, mask, paired],
    )
    grads = exchanged(grads, COLS)
    [direct] = called(
        direct_kernel,
        [(3, 2 * N_ROWS, TILE)],
        [
            forces,
            ((I_BLOCKS, 8, TILE), F32),
            ((2 * N_ROWS + 8, TILE), F32),
            ((2 * N_ROWS, TILE), F32),
        ],
        [picked, places],
        [own_j, pack_i, rad_j, radius_i, charge_i, plain],
    )
    parts, own = called(
        chain_kernel,
        [(N_ROWS, 8, TILE), (10, TILE)],
        [forces, ((I_BLOCKS, TILE), F32)],
        [picked, places],
        [pack_i, own_j, grads, charge_i, radius_i, rate_i, direct, plain],
    )
    parts = exchanged(parts, ROWS)
    new_velocities, new_forces = called(
        last_kernel, [(3, 2 * TILE), (3, 2 * TILE)], [], [], [parts, own, kept]
    )
    return (new_positions, new_velocities, new_forces)


def solution(mesh):
    split = Mesh(mesh.devices.reshape(SIZES), AXES)
    rows, cols = AXES[:4], AXES[4:]
    return jax.shard_map(
        body,
        mesh=split,
        in_specs=(
            P(None, AXES),
            P(None, AXES),
            P(None, AXES),
            P(AXES),
            P(AXES),
            P(),
            P(rows, cols, None, None),
        ),
        out_specs=(P(None, AXES), P(None, AXES), P(None, AXES)),
        check_vma=False,
    )
```

```python
import jax
import jax.numpy as jnp
from jax import lax
from jax.experimental import pallas as pl
from jax.experimental.pallas import tpu as pltpu
from jax.sharding import Mesh
from jax.sharding import PartitionSpec as P

TILE = 128
SLOTS = 32
CHUNK = 32
UNROLL = 8
LISTED = 128
PICKED = 2048

CUTOFF = 12.0
COULOMB = 32.0
TIMESTEP = 0.5
OFFSET = 0.09
NECK_GAP = 0.5
NECK_WIDTH = 16.0
CUT_SQ = CUTOFF * CUTOFF
TAPER = 1.0 / (CUT_SQ * CUT_SQ)
LOG2E = 1.4426950408889634
NO_KEY = 16777216.0

AXES = ("zh", "zl", "yh", "core", "x", "yl")
SIZES = (4, 4, 2, 2, 4, 2)
REP = ("zh",)
ROWS = ("zl", "yh", "core")
COLS = ("x", "yl")
N_REP, N_ROWS, N_COLS = 4, 16, 8
HELD = 2 * N_REP
I_BLOCKS = N_COLS * HELD
J_BLOCKS = N_ROWS * HELD

VMEM = pl.BlockSpec(memory_space=pltpu.VMEM)
SMEM = pl.BlockSpec(memory_space=pltpu.SMEM)
F32 = jnp.float32


def exchanged(pieces, axes):
    return lax.all_to_all(pieces, axes, 0, 0, tiled=True)


def called(kernel, outs, scratch, smem, vmem, inputs=VMEM, outputs=VMEM, kind=F32):
    return pl.pallas_call(
        kernel,
        out_shape=[
            jax.ShapeDtypeStruct(*s) if isinstance(s[0], tuple) else jax.ShapeDtypeStruct(s, kind)
            for s in outs
        ],
        in_specs=[SMEM] * len(smem) + [inputs] * len(vmem),
        out_specs=[outputs] * len(outs),
        scratch_shapes=[pltpu.VMEM(*s) if isinstance(s, tuple) else s for s in scratch],
        compiler_params=pltpu.CompilerParams(vmem_limit_bytes=32 * 1024 * 1024),
    )(*smem, *vmem)


def looked_up(table, types, rows):
    found = [jnp.zeros(types.shape, F32) for _ in rows]
    for kind in range(8):
        here = types == float(kind)
        found = [jnp.where(here, table[r, kind], f) for r, f in zip(rows, found)]
    return found


def folded(value):
    parts = [value[s : s + 8] for s in range(0, CHUNK, 8)]
    while len(parts) > 1:
        parts = [a + b for a, b in zip(parts[::2], parts[1::2])]
    return parts[0]


def write_mask(mask_ref):
    down = lax.broadcasted_iota(jnp.int32, (TILE, TILE), 0)
    across = lax.broadcasted_iota(jnp.int32, (TILE, TILE), 1)
    mask_ref[0] = jnp.ones((TILE, TILE), F32)
    mask_ref[1] = jnp.where(down == across, 0.0, 1.0)


def write_spread(spread_ref, rows):
    at = lax.broadcasted_iota(jnp.int32, (32, TILE), 0)
    for c, row in enumerate(rows):
        hit = (at % 8 == row) & (at < 24)
        spread_ref[:, c * TILE : (c + 1) * TILE] = jnp.where(hit, 1.0, 0.0).astype(jnp.bfloat16)


def columns(rows, spread):
    high = rows.astype(jnp.bfloat16).astype(F32)
    rest = rows - high
    middle = rest.astype(jnp.bfloat16).astype(F32)
    parts = jnp.concatenate([high, middle, rest - middle, jnp.ones_like(rows)], axis=0)
    given = lax.dot_general(
        parts.astype(jnp.bfloat16),
        spread,
        (((0,), (0,)), ((), ())),
        preferred_element_type=F32,
    )
    return lambda s, c: given[s : s + CHUNK, c * TILE : (c + 1) * TILE]


def offsets(xi, yi, zi, col, s):
    dx = xi - col(s, 0)
    dy = yi - col(s, 1)
    dz = zi - col(s, 2)
    return dx, dy, dz, dx * dx + dy * dy + dz * dz


def decoded(code):
    return code >> 8, (code >> 1) & 127, code & 1


def for_each_tile(meta, first, count, one_tile):
    def steps(begin, number, width):
        def step(k, _):
            at = begin + k * width
            for add in [one_tile(*decoded(meta[at + u])) for u in range(width)]:
                add()
            return 0

        lax.fori_loop(0, number, step, 0)

    half = UNROLL // 2
    whole = (count + half - 1) // UNROLL
    steps(first, whole, UNROLL)
    steps(first + whole * UNROLL, jnp.where(count > whole * UNROLL, 1, 0), half)


def typed_spread(table, spread_ref):
    row = lax.broadcasted_iota(jnp.int32, (48, TILE), 0)
    for c in range(3):
        hit = (row % 4 == c) & (row < 12)
        spread_ref[:, c * TILE : (c + 1) * TILE] = jnp.where(hit, 1.0, 0.0).astype(jnp.bfloat16)
    kind = (row % 8).astype(F32)
    rho, scale, neck = looked_up(table, kind, (0, 1, 2))
    for c, value in enumerate((rho, scale * rho * rho * rho, neck)):
        high = value.astype(jnp.bfloat16).astype(F32)
        rest = value - high
        middle = rest.astype(jnp.bfloat16).astype(F32)
        part = jnp.where(row < 24, high, jnp.where(row < 32, middle, rest - middle))
        part = jnp.where((row >= 16) & (row < 40), part, 0.0)
        spread_ref[:, (3 + c) * TILE : (4 + c) * TILE] = part.astype(jnp.bfloat16)


def typed_columns(atoms, spread):
    high = atoms.astype(jnp.bfloat16).astype(F32)
    rest = atoms - high
    middle = rest.astype(jnp.bfloat16).astype(F32)
    kinds = lax.broadcasted_iota(jnp.int32, (8, TILE), 0).astype(F32)
    hot = jnp.where(atoms[3:4, :] == kinds, 1.0, 0.0)
    parts = jnp.concatenate(
        [high, middle, rest - middle, jnp.ones((4, TILE), F32), hot, hot, hot, jnp.zeros((8, TILE), F32)],
        axis=0,
    )
    given = lax.dot_general(
        parts.astype(jnp.bfloat16),
        spread,
        (((0,), (0,)), ((), ())),
        preferred_element_type=F32,
    )
    return lambda s, c: given[s : s + CHUNK, c * TILE : (c + 1) * TILE]


def j_atoms(side_j, jb):
    return side_j[jb // HELD, jb % HELD]


def first_kernel(table, joined, new_ref, sent_ref, kept_ref):
    pos, vel, old = joined[0:3], joined[3:6], joined[6:9]
    charge, types, lists = joined[9:10], joined[10:11], joined[11:13, 0:TILE]
    [mass] = looked_up(table, types, (6,))
    new = pos + TIMESTEP * vel + TIMESTEP * TIMESTEP / (2.0 * mass) * old
    scale = TIMESTEP / (2.0 * mass)
    new_ref[...] = new
    kept_ref[0:3] = vel + scale * old
    kept_ref[3:4] = scale
    kept_ref[4:5] = charge
    for n in range(N_REP):
        for b in range(2):
            here = slice(b * TILE, (b + 1) * TILE)
            sent_ref[n, b, 0:3, :] = new[:, here]
            sent_ref[n, b, 3:4, :] = types[:, here]
            sent_ref[n, 2, 2 + b : 3 + b, :] = charge[:, here]
        sent_ref[n, 2, 0:2, :] = lists


def row_kernel(places, side_i, sent_ref):
    rows = [
        jnp.concatenate(
            [
                side_i[4 * half + n, places[0], 2, r : r + 1, 0:SLOTS]
                for n in range(4)
            ],
            axis=1,

        )
        for r in range(2)
        for half in range(2)
    ]
    lists = jnp.concatenate(rows, axis=0)
    for n in range(N_ROWS):
        for b in range(HELD):
            sent_ref[n, b] = side_i[places[2], b // 2, b % 2]
        sent_ref[n, HELD] = lists


def pick_kernel(keys_ref, picked):
    keys = keys_ref[...]
    count = jnp.sum(jnp.where(keys < NO_KEY, 1.0, 0.0)).astype(jnp.int32)

    def step(k, keys):
        least = jnp.min(keys)
        place = least.astype(jnp.int32) >> 12
        picked[k] = (place >> 6) * 256 + (place & 63) * 2
        return jnp.where(keys == least, NO_KEY, keys)

    lax.fori_loop(0, count, step, keys)
    for n in range(UNROLL):
        picked[count + n] = 2 * N_ROWS * 256
    picked[PICKED + UNROLL] = count


def packed(table, pack, count, more):
    types = pack[0:count, 3, :]
    found = looked_up(table, types, (0, 1, 2) + more)
    rho = found[0]
    pack[0:count, 3, :] = rho
    pack[0:count, 4, :] = found[1] * rho * rho * rho
    pack[0:count, 5, :] = found[2]
    return rho, found[3:]


def pack_kernel(
    table, side_i, pack_i, charge_i, more_i, mask_ref, typed_ref, plain_ref, pair_ref, near_i
):
    write_mask(mask_ref)
    typed_spread(table, typed_ref)
    write_spread(plain_ref, range(6))
    write_spread(pair_ref, (0, 1, 2, 4, 5, 6))
    for n in range(N_COLS):
        for z in range(N_REP):
            at = n * HELD + 2 * z
            for b in range(2):
                pack_i[at + b, 0:4, :] = side_i[n, z, b]
                pack_i[at + b, 4:8, :] = side_i[n, z, b]
            charge_i[at : at + 2] = side_i[n, z, 2, 2:4, :]
    pack_i[I_BLOCKS] = jnp.ones((8, TILE), F32)
    rho, more = packed(table, pack_i, I_BLOCKS, (3, 4, 5))
    for n, value in enumerate((*more, 1.0 / rho, 1.0 / (rho + OFFSET))):
        more_i[n] = value
    near_i[...] = jnp.zeros_like(near_i)
    for c in range(4):
        here = slice(c * TILE, (c + 1) * TILE)
        value = rho + NECK_GAP
        if c < 3:
            value = -pack_i[0:I_BLOCKS, c, :]
        high = value.astype(jnp.bfloat16).astype(F32)
        rest = value - high
        middle = rest.astype(jnp.bfloat16).astype(F32)
        near_i[0:I_BLOCKS, 0, here] = high
        near_i[0:I_BLOCKS, 1, here] = middle
        near_i[0:I_BLOCKS, 2, here] = rest - middle


def keep_kernel(meta, read, kept):
    def step(k, count):
        code = meta[k]
        kept[count] = code
        return count + read[code >> 8]

    count = lax.fori_loop(0, meta[LISTED], step, 0)
    for n in range(UNROLL):
        kept[count + n] = I_BLOCKS * 256
    kept[LISTED + UNROLL] = count


def born_kernel(meta, pack_i, near_i, side_j, mask_ref, spread_ref, out_ref, acc):
    acc[...] = jnp.zeros_like(acc)
    first_rows = spread_ref[0:16, 0 : 4 * TILE].astype(F32)[0:12]

    def one_tile(ia, jb, same):
        rows = jnp.concatenate([first_rows, near_i[ia]], axis=0).astype(jnp.bfloat16)
        rows = jnp.concatenate([rows, spread_ref[0:16, 4 * TILE :]], axis=1)
        spread = jnp.concatenate([rows, spread_ref[16:, :]], axis=0)
        col = typed_columns(j_atoms(side_j, jb), spread)
        rho = pack_i[ia, 3:4, :]
        rho_sq = rho * rho
        total = jnp.zeros((8, TILE), F32)
        for s in range(0, TILE, CHUNK):
            dx, dy, dz, gap = (col(s, c) for c in range(4))
            q = dx * dx + dy * dy + dz * dz
            base = jnp.maximum(CUT_SQ - q, 0.0)
            weight = base * base * mask_ref[same, s : s + CHUNK, :]
            inv = 1.0 / (q + rho_sq)
            off = q - gap * gap
            bump = jnp.exp2(off * off * (-LOG2E / NECK_WIDTH))
            total += folded(weight * (col(s, 4) * (inv * inv) + col(s, 5) * bump))

        def add():
            acc[ia] += total

        return add

    for_each_tile(meta, 0, meta[LISTED], one_tile)
    born = TAPER * jnp.sum(acc[0:I_BLOCKS], axis=1)
    for n in range(N_COLS):
        out_ref[n] = born


def radius_kernel(places, parts, pack_i, more_i, charge, ready, radius_ref, sent_ref, rate_ref):
    born = parts[0]
    for n in range(1, N_COLS):
        born = born + parts[n]
    rho = pack_i[0:I_BLOCKS, 3, :]
    alpha, beta, gamma, inv_rho, inv_offset = (more_i[n] for n in range(5))
    scaled = rho * born
    poly = alpha * scaled - beta * scaled * scaled + gamma * scaled * scaled * scaled
    squash = jnp.tanh(poly)
    radius = 1.0 / (inv_rho - squash * inv_offset)
    slope = alpha - 2.0 * beta * scaled + 3.0 * gamma * scaled * scaled
    rate_ref[...] = radius * radius * (1.0 - squash * squash) * slope * rho * inv_offset
    radius_ref[0:I_BLOCKS] = radius
    radius_ref[I_BLOCKS : I_BLOCKS + 8] = jnp.ones((8, TILE), F32)
    here = pl.ds(pl.multiple_of(places[2] * HELD, HELD), HELD)
    held, charges = radius_ref[here, :], charge[here, :]
    for n in range(N_ROWS):
        sent_ref[n, 0] = held
        sent_ref[n, 1] = charges


def slope_kernel(meta, places, table, pack_i, side_j, spread_ref, out_ref, own_j, force):
    force[...] = jnp.zeros_like(force)
    for n in range(N_ROWS):
        for b in range(2):
            block = side_j[n, places[0] * 2 + b]
            own_j[2 * n + b, 0:4, :] = block
            own_j[2 * n + b, 4:8, :] = block
    own_j[2 * N_ROWS] = jnp.ones((8, TILE), F32)
    packed(table, own_j, 2 * N_ROWS, ())

    def one_tile(ia, jb, same):
        col = typed_columns(j_atoms(side_j, jb), spread_ref[...])
        xi, yi, zi, rho = (pack_i[ia, c : c + 1, :] for c in range(4))
        rho_sq, rho_gap = rho * rho, rho + NECK_GAP
        sums = [jnp.zeros((8, TILE), F32)] * 3
        for s in range(0, TILE, CHUNK):
            dx, dy, dz, q = offsets(xi, yi, zi, col, s)
            base = jnp.maximum(CUT_SQ - q, 0.0)
            gap = rho_gap + col(s, 3)
            off = q - gap * gap
            bump = jnp.exp2(off * off * (-LOG2E / NECK_WIDTH))
            bump = bump * (2.0 + base * off * (2.0 / NECK_WIDTH))
            inv = 1.0 / (q + rho_sq)
            slope = col(s, 4) * (inv * inv) * (2.0 + (base + base) * inv) + col(s, 5) * bump
            slope = slope * base
            sums = [a + folded(slope * d) for a, d in zip(sums, (dx, dy, dz))]

        def add():
            for c in range(3):
                force[ia, c] += sums[c]

        return add

    for_each_tile(meta, 0, meta[LISTED + 1], one_tile)
    for n in range(N_COLS):
        for b in range(2):
            total = jnp.sum(force[n * HELD + places[0] * 2 + b], axis=1)
            total = -TAPER * total
            out_ref[n, 3 * b : 3 * b + 3, :] = total
        out_ref[n, 6:8, :] = total[0:2]


def direct_kernel(
    picked, places, own_j, pack_i, rad_j, radius_i, charge_i, spread_ref, out_ref, force, sides, own, own_q
):
    force[...] = jnp.zeros_like(force)
    sides[...] = pack_i[0:I_BLOCKS]
    radii = radius_i[0:I_BLOCKS]
    sides[:, 3, :] = radii
    sides[:, 4, :] = 1.0 / radii
    sides[:, 5, :] = charge_i[...]
    own[...] = jnp.ones_like(own)
    for n in range(N_ROWS):
        own[2 * n : 2 * n + 2] = rad_j[n, 0, pl.ds(places[0] * 2, 2), :]
        own_q[2 * n : 2 * n + 2] = rad_j[n, 1, pl.ds(places[0] * 2, 2), :]

    def one_tile(at, jb, same):
        col = columns(sides[jb], spread_ref[...])
        xi, yi, zi = (own_j[at, c : c + 1, :] for c in range(3))
        radius = own[pl.ds(at, 1), :]
        quarter = 0.25 / radius
        sums = [jnp.zeros((8, TILE), F32)] * 3
        for s in range(0, TILE, CHUNK):
            dx, dy, dz, q = offsets(xi, yi, zi, col, s)
            base = jnp.maximum(CUT_SQ - q, 0.0)
            decay = jnp.exp2(q * (quarter * col(s, 4)) * -LOG2E)
            inv = lax.rsqrt(q + radius * col(s, 3) * decay)
            slope = 2.0 + base * (inv * inv) * (0.5 - 0.125 * decay)
            slope = slope * (base * (inv * col(s, 5)))
            sums = [a + folded(slope * d) for a, d in zip(sums, (dx, dy, dz))]

        def add():
            for c in range(3):
                force[at, c] += sums[c]

        return add

    for_each_tile(picked, 0, picked[PICKED + UNROLL], one_tile)
    scale = (-2.0 * COULOMB * TAPER) * own_q[...]
    for c in range(3):
        out_ref[c] = scale * jnp.sum(force[0 : 2 * N_ROWS, c], axis=1)


def pair_kernel(
    meta, near_i, side_j, rad_i, rad_j, slopes, ready, mask_ref, spread_ref, out_ref, acc
):
    acc[...] = jnp.zeros_like(acc)
    xyz = 3 * TILE
    low_rows = spread_ref[16:32, 0:xyz].astype(F32)[0:8]
    no_rows = jnp.zeros((4, xyz), F32)

    def one_tile(ia, jb, same):
        n, b = jb // HELD, jb % HELD
        radius_j, charge_j = (rad_j[n, k, pl.ds(b, 1), :] for k in range(2))
        rows = jnp.concatenate([low_rows, near_i[ia, :, 0:xyz], no_rows], axis=0)
        rows = jnp.concatenate([rows.astype(jnp.bfloat16), spread_ref[16:32, xyz:]], axis=1)
        col = columns(
            jnp.concatenate(
                [side_j[n, b], radius_j, 1.0 / radius_j, charge_j, charge_j], axis=0
            ),
            jnp.concatenate([spread_ref[0:16, :], rows], axis=0),
        )
        radius_i = rad_i[pl.ds(ia, 1), :]
        quarter_i = 0.25 / radius_i
        total = jnp.zeros((8, TILE), F32)
        for s in range(0, TILE, CHUNK):
            dx, dy, dz = (col(s, c) for c in range(3))
            q = dx * dx + dy * dy + dz * dz
            base = jnp.maximum(CUT_SQ - q, 0.0)
            weight = base * base * mask_ref[same, s : s + CHUNK, :]
            arg = q * (quarter_i * col(s, 4))
            decay = jnp.exp2(arg * -LOG2E)
            inv = lax.rsqrt(q + radius_i * col(s, 3) * decay)
            weighted = weight * col(s, 5) * (inv * inv * inv)
            total += folded(weighted * col(s, 3) * (decay * (1.0 + arg)))

        def add():
            acc[ia] += total

        return add

    for_each_tile(meta, 0, meta[LISTED + UNROLL], one_tile)
    grads = TAPER * jnp.sum(acc[0:I_BLOCKS], axis=1)
    for n in range(N_COLS):
        out_ref[n, 0:I_BLOCKS] = grads
        out_ref[n, I_BLOCKS : I_BLOCKS + 8] = slopes[n]


def chain_kernel(
    picked, places, pack_i, own_j, parts, charge, radius, rate, direct, spread_ref, out_ref, own_ref, force, chain_ref
):
    force[...] = jnp.zeros_like(force)
    total = parts[0]
    for n in range(1, N_COLS):
        total = total + parts[n]
    charges, radii = charge[...], radius[0:I_BLOCKS]
    grad = -0.5 * charges * total[0:I_BLOCKS]
    chain = (COULOMB * charges * charges / (2.0 * radii * radii) - COULOMB * grad) * rate[...]
    chain_ref[...] = chain
    own_ref[0:8] = total[I_BLOCKS : I_BLOCKS + 8]
    for b in range(2):
        own_ref[8 + b : 9 + b] = chain_ref[pl.ds(places[2] * HELD + places[0] * 2 + b, 1), :]
    fifth = lax.broadcasted_iota(jnp.int32, (8, TILE), 0) == 4

    def one_tile(at, jb, same):
        col = columns(jnp.where(fifth, chain_ref[pl.ds(jb, 1), :], pack_i[jb]), spread_ref[...])
        xi, yi, zi, rho, vol, neck = (own_j[at, c : c + 1, :] for c in range(6))
        rho_gap = rho + NECK_GAP
        sums = [jnp.zeros((8, TILE), F32)] * 3
        for s in range(0, TILE, CHUNK):
            dx, dy, dz, q = offsets(xi, yi, zi, col, s)
            base = jnp.maximum(CUT_SQ - q, 0.0)
            rho_j = col(s, 3)
            gap = rho_gap + rho_j
            off = q - gap * gap
            bump = jnp.exp2(off * off * (-LOG2E / NECK_WIDTH))
            bump = bump * (2.0 + base * off * (2.0 / NECK_WIDTH))
            inv = 1.0 / (q + rho_j * rho_j)
            slope = vol * (inv * inv) * (2.0 + (base + base) * inv) + neck * bump
            slope = slope * (base * col(s, 4))
            sums = [a + folded(slope * d) for a, d in zip(sums, (dx, dy, dz))]

        def add():
            for c in range(3):
                force[at, c] += sums[c]

        return add

    for_each_tile(picked, 0, picked[PICKED + UNROLL], one_tile)
    for k in range(3):
        value = direct[k] + (2.0 * TAPER) * jnp.sum(force[0 : 2 * N_ROWS, k], axis=1)
        for n in range(N_ROWS):
            out_ref[n, 2 * k : 2 * k + 2, :] = value[2 * n : 2 * n + 2]
            if k == 2:
                out_ref[n, 6:8, :] = value[2 * n : 2 * n + 2]


def last_kernel(parts, own, kept, vel_ref, force_ref):
    total = parts[0]
    for n in range(1, N_ROWS):
        total = total + parts[n]
    for b in range(2):
        here = slice(b * TILE, (b + 1) * TILE)
        for k in range(3):
            row = slice(k, k + 1)
            force = total[2 * k + b : 2 * k + b + 1] - 2.0 * (
                own[8 + b : 9 + b, :] * own[3 * b + k : 3 * b + k + 1, :]
            )
            force_ref[row, here] = force
            vel_ref[row, here] = kept[row, here] + kept[3:4, here] * force


def transposed_keys(lists, places):
    list_a, list_g = lists[:, 0:2].astype(jnp.int32), lists[:, 2:4].astype(jnp.int32)
    source, half, lane = (lax.broadcasted_iota(jnp.int32, list_a.shape, n) for n in range(3))
    j_col, j_row = half * 4 + lane // SLOTS, list_g // 2
    known = (list_a >= 0) & (j_row % N_ROWS == places[1])
    place_j = (j_col * N_REP + j_row // N_ROWS) * 2 + list_g % 2
    key = ((source * 2 + list_a % 2) * I_BLOCKS + place_j) * 4096
    key = key + (source * 2 + half) * TILE + lane
    keys = jnp.where(known & (list_a // 2 == places[2]), key.astype(F32), NO_KEY)
    named = jnp.where(known, place_j, -1).reshape(1, 2 * N_ROWS, TILE)
    blocks = jnp.arange(I_BLOCKS, dtype=jnp.int32)
    read = jnp.any(named == blocks[:, None, None], axis=(1, 2)) | (blocks // 2 % N_REP == places[0])
    return keys.reshape(2 * N_ROWS, TILE), read.astype(jnp.int32)


def tile_codes(lists, rep_at, row_at, col_at):
    list_a, list_g = lists[:, 0].astype(jnp.int32), lists[:, 1].astype(jnp.int32)
    reps = jnp.arange(N_REP, dtype=jnp.int32)[:, None]
    live = list_a >= 0
    counts = jnp.sum(live.astype(jnp.int32), axis=1)
    j_row = list_g // 2
    place_i = (list_a // 2 * N_REP + reps) * 2 + list_a % 2
    place_j = (j_row % N_ROWS * N_REP + j_row // N_ROWS) * 2 + list_g % 2
    same = (j_row == reps * N_ROWS + row_at) & (list_a == col_at * 2 + list_g % 2)
    none = I_BLOCKS * 256
    codes = place_i * 256 + place_j * 2 + same.astype(jnp.int32) - none
    turn = (reps - rep_at) & (N_REP - 1)
    before = jnp.sum(jnp.where(turn < turn.T, counts[:, None], 0), axis=0)
    target = before[:, None] + jnp.arange(SLOTS, dtype=jnp.int32)[None, :]
    target = jnp.where(live, target, -1).reshape(1, LISTED)
    hit = target == jnp.arange(LISTED, dtype=jnp.int32)[:, None]
    placed = none + jnp.sum(jnp.where(hit, codes.reshape(1, LISTED), 0), axis=1)
    own = jnp.sum(jnp.where(turn[:, 0] == 0, counts, 0))
    return jnp.concatenate([placed, jnp.stack([jnp.sum(counts), own])]).astype(jnp.int32)


def body(positions, velocities, old_forces, charges, atom_types, table, tile_pairs):
    rep_at = lax.axis_index(REP)
    row_at = lax.axis_index(ROWS)
    col_at = lax.axis_index(COLS)
    places = jnp.stack([rep_at, row_at, col_at]).astype(jnp.int32)
    row = (1, 2 * TILE)
    joined = jnp.concatenate(
        [
            positions,
            velocities,
            old_forces,
            charges.reshape(row),
            atom_types.reshape(row).astype(F32),
            jnp.pad(tile_pairs.reshape(2, SLOTS).astype(F32), ((0, 0), (0, 2 * TILE - SLOTS))),
        ],
        axis=0,
    )
    new_positions, sent, kept = called(
        first_kernel,
        [(3, 2 * TILE), (N_REP, 3, 4, TILE), (5, 2 * TILE)],
        [],
        [table],
        [joined],
    )
    held = exchanged(sent, REP)
    meta = tile_codes(held[:, 2, 0:2, 0:SLOTS], rep_at, row_at, col_at)
    side_i = exchanged(jnp.broadcast_to(held, (N_COLS, *held.shape)), COLS)
    [sent] = called(row_kernel, [(N_ROWS, 9, 4, TILE)], [], [places], [side_i])
    side_j = exchanged(sent, ROWS)

    sums = ((I_BLOCKS + 1, 8, TILE), F32)
    forces = ((2 * N_ROWS + 1, 3, 8, TILE), F32)
    bf16 = jnp.bfloat16
    pack_i, charge_i, more_i, mask, typed, plain, paired, near_i = called(
        pack_kernel,
        [
            (I_BLOCKS + 1, 8, TILE),
            (I_BLOCKS, TILE),
            (5, I_BLOCKS, TILE),
            (2, TILE, TILE),
            ((48, 6 * TILE), bf16),
            ((32, 6 * TILE), bf16),
            ((32, 6 * TILE), bf16),
            (I_BLOCKS + 1, 4, 4 * TILE),
        ],
        [],
        [table],
        [side_i],
    )
    [born_parts] = called(
        born_kernel,
        [(N_COLS, I_BLOCKS, TILE)],
        [sums],
        [meta],
        [pack_i, near_i, side_j, mask, typed],
    )
    born_parts = exchanged(born_parts, COLS)
    keys, read = transposed_keys(side_j[:, HELD], places)
    [kept_tiles] = called(
        keep_kernel, [(LISTED + UNROLL + 1,)], [], [meta, read], [], outputs=SMEM, kind=jnp.int32
    )
    [picked] = called(
        pick_kernel,
        [(PICKED + UNROLL + 1,)],
        [],
        [],
        [keys],
        outputs=SMEM,
        kind=jnp.int32,
    )
    radius_i, sent, rate_i = called(
        radius_kernel,
        [(I_BLOCKS + 8, TILE), (N_ROWS, 2, HELD, TILE), (I_BLOCKS, TILE)],
        [],
        [places],
        [born_parts, pack_i, more_i, charge_i, kept_tiles],
    )
    rad_j = exchanged(sent, ROWS)
    slopes, own_j = called(
        slope_kernel,
        [(N_COLS, 8, TILE), (2 * N_ROWS + 1, 8, TILE)],
        [((I_BLOCKS + 1, 3, 8, TILE), F32)],
        [meta, places, table],
        [pack_i, side_j, typed],
    )
    [grads] = called(
        pair_kernel,
        [(N_COLS, I_BLOCKS + 8, TILE)],
        [sums],
        [kept_tiles],
        [near_i, side_j, radius_i, rad_j, slopes, picked, mask, paired],
    )
    grads = exchanged(grads, COLS)
    [direct] = called(
        direct_kernel,
        [(3, 2 * N_ROWS, TILE)],
        [
            forces,
            ((I_BLOCKS, 8, TILE), F32),
            ((2 * N_ROWS + 8, TILE), F32),
            ((2 * N_ROWS, TILE), F32),
        ],
        [picked, places],
        [own_j, pack_i, rad_j, radius_i, charge_i, plain],
    )
    parts, own = called(
        chain_kernel,
        [(N_ROWS, 8, TILE), (10, TILE)],
        [forces, ((I_BLOCKS, TILE), F32)],
        [picked, places],
        [pack_i, own_j, grads, charge_i, radius_i, rate_i, direct, plain],
    )
    parts = exchanged(parts, ROWS)
    new_velocities, new_forces = called(
        last_kernel, [(3, 2 * TILE), (3, 2 * TILE)], [], [], [parts, own, kept]
    )
    return (new_positions, new_velocities, new_forces)


def solution(mesh):
    split = Mesh(mesh.devices.reshape(SIZES), AXES)
    rows, cols = AXES[:4], AXES[4:]
    return jax.shard_map(
        body,
        mesh=split,
        in_specs=(
            P(None, AXES),
            P(None, AXES),
            P(None, AXES),
            P(AXES),
            P(AXES),
            P(),
            P(rows, cols, None, None),
        ),
        out_specs=(P(None, AXES), P(None, AXES), P(None, AXES)),
        check_vma=False,
    )
```
